128 devices in a mesh: row: 8 (over x, z_hi), col: 16 (over y, z_lo, core).
Axes of the slice: x: 4, y: 4, z: 4 (z_hi: 2, z_lo: 2; z = z_hi * 2 + z_lo), core: 2. Of those that a mesh axis runs over, the one named last changes fastest.
Arguments:
- tokens: bfloat16 [8, 16, 256, 1536], P('row', 'col'), may hold values from -6 to 6
- layer_norm_gain: float32 [1536], replicated, may hold values from 0.5 to 1.5
- proj_in: bfloat16 [1536, 2304], replicated
- proj_out: bfloat16 [768, 1536], replicated, may hold values from -0.21875 to 0.21875
- tissue: int32 [24, 48], replicated, may hold values from 0 to 1, as said below
- tile_slot: int32 [8, 16], P('row', 'col'), may hold values from 0 to 8, as said below
- cotangent: bfloat16 [8, 16, 256, 1536], P('row', 'col'), may hold values from -12 to 12
Outputs:
- branch_out: bfloat16 [8, 16, 256, 1536], P('row', 'col')
- branch_grad: bfloat16 [8, 16, 256, 1536], P('row', 'col')
- clipped_in: float32 [1536, 2304], P(('row', 'col'))
- clipped_out: float32 [768, 1536], P(('row', 'col'))
- clipped_gain: float32 [1536], P(('row', 'col'))
The draws below stay inside these ranges and needn't reach their ends.
Inputs may be any that keep to these rules, and one draw needn't show every extreme that they name: `tissue`: 0 or 1; each device's 3 x 3 region holds at most one occupied tile, and the first device's region holds one. `tile_slot`: row times 3 plus column of the region's occupied tile; where the region holds none, a tile of the region.
All inputs are finite; a program needn't handle non-finite values.
Results may differ from the reference program's by a relative error of at most 0.007.
The reference program's roundings to bfloat16 on the way count: a program that leaves them out, or rounds other values in their place, can miss the bound.
Values may be sent and summed in bfloat16 or wider, within the bound.
No kernel may reach another device: no remote copies, remote signals or barrier semaphores. Data moves between devices by JAX's collectives and lax.ppermute only.
A program may use at most 128 MiB of HBM per device.

```python
import jax
import jax.numpy as jnp
from jax import lax

D = 1536
HEAD_DIM = 64
REGION = 3
RADIUS = 3
HD = 768
TILE_TOK = 256
COUNT = 4720128
N_ROW = 8
N_COL = 16


def tissue_layout(key):
    spot = jax.random.randint(jax.random.fold_in(key, 11), (N_ROW, N_COL), 0, REGION * REGION)
    centre_rows = jax.random.randint(jax.random.fold_in(key, 12), (2,), 0, N_ROW)
    centre_cols = jax.random.randint(jax.random.fold_in(key, 13), (2,), 0, N_COL)
    reach = max(N_ROW * N_COL // 10, 2)
    jitter = jax.random.randint(jax.random.fold_in(key, 14), (N_ROW, N_COL), 0, reach // 2 + 2)
    rows = jnp.arange(N_ROW, dtype=jnp.int32)[:, None, None]
    cols = jnp.arange(N_COL, dtype=jnp.int32)[None, :, None]
    distance = (rows - centre_rows[None, None, :]) ** 2 + (cols - centre_cols[None, None, :]) ** 2
    nearest = jnp.min(distance, axis=2)
    row_ids = jnp.arange(N_ROW, dtype=jnp.int32)[:, None]
    col_ids = jnp.arange(N_COL, dtype=jnp.int32)[None, :]
    band = (jnp.abs(row_ids - N_ROW // 2) <= 1) | (jnp.abs(col_ids - N_COL // 2) <= 1)
    place = row_ids * N_COL + col_ids
    spot = jnp.where(band, REGION * REGION // 2, spot)
    spot = jnp.where(place == 0, 0, spot)
    spot = jnp.where(place == N_ROW * N_COL - 1, REGION * REGION - 1, spot)
    live = ((nearest <= reach + jitter) | (place == 0) | band).astype(jnp.int32)
    return (spot.astype(jnp.int32), live)


def draw_tissue(key, part):
    spot, live = tissue_layout(key)
    local = jnp.arange(REGION * REGION, dtype=jnp.int32)
    grid = (local[None, None, :] == spot[:, :, None]).astype(jnp.int32) * live[:, :, None]
    grid = grid.reshape(N_ROW, N_COL, REGION, REGION).transpose(0, 2, 1, 3)
    return grid.reshape(REGION * N_ROW, REGION * N_COL)


def draw_tile_slot(key, part):
    spot, live = tissue_layout(key)
    return spot


def draw_proj_in(key, part):
    key = jax.random.fold_in(key, 5)
    spread = D ** (-0.5)
    return (jax.random.normal(key, (D, 3 * HD), jnp.float32) * spread).astype(jnp.bfloat16)


def block_levels(key, shape, cuts, smallest, top_value):
    factor_of = 1.0
    for dim, shards_of in cuts:
        draws = jax.random.uniform(jax.random.fold_in(jax.random.fold_in(key, 6), dim), (shards_of,), jnp.float32, smallest / len(cuts), top_value / len(cuts))
        factor_of = factor_of * jnp.repeat(jnp.exp(draws), shape[dim] // shards_of).reshape((-1,) + (1,) * (len(shape) - 1 - dim))
    return factor_of


def scatter_about(stream_key, shape, scale, limit, pieces=(), kind=jnp.bfloat16):
    values = jax.random.normal(stream_key, shape, jnp.float32) * scale
    if len(pieces) > 0:
        values = block_levels(stream_key, shape, pieces, -0.22, 0.18) * values
    return jnp.clip(values, min=-limit, max=limit).astype(kind)


def setup_inputs(seed: int = 0) -> dict:
    seeds = jax.random.split(jax.random.key(seed), 8)
    tokens = scatter_about(seeds[0], (N_ROW, N_COL, TILE_TOK, D), 1.0, 6.0, ((0, 8), (1, 16)))
    layer_norm_gain = jnp.clip(1.0 + 0.1 * jax.random.normal(seeds[1], (D,), jnp.float32), 0.5, 1.5)
    proj_in = draw_proj_in(jax.random.fold_in(seeds[7], 71), 0)
    proj_out = scatter_about(seeds[3], (HD, D), HD ** -0.5, 0.21875)
    tissue = draw_tissue(jax.random.fold_in(seeds[7], 71), 0)
    tile_slot = draw_tile_slot(jax.random.fold_in(seeds[7], 71), 0)
    cotangent = scatter_about(seeds[6], (N_ROW, N_COL, TILE_TOK, D), 2.0, 12.0, ((0, 8), (1, 16)))
    return dict(tokens=tokens, layer_norm_gain=layer_norm_gain, proj_in=proj_in, proj_out=proj_out, tissue=tissue, tile_slot=tile_slot, cotangent=cotangent)


EPSILON = 1e-05
NEG_BIG = -1e+30

def apply_layer_norm(attention_block):
    values = attention_block.astype(jnp.float32)
    centred = values - lax.optimization_barrier(jnp.mean(values, axis=-1, keepdims=True))
    inverse_deviation = lax.rsqrt(lax.optimization_barrier(jnp.mean(centred * centred, axis=-1, keepdims=True)) + EPSILON)
    return (centred * inverse_deviation, inverse_deviation)

def geometry(tissue, row_at, col_at, slot):
    padded = jnp.pad(tissue, REGION)
    window = lax.dynamic_slice(padded, (row_at * REGION, col_at * REGION), (3 * REGION, 3 * REGION))
    blocks = window.reshape(3, REGION, 3, REGION)
    occupied = lax.optimization_barrier(jnp.sum(blocks, axis=(1, 3)))
    inner = jnp.arange(REGION, dtype=jnp.int32)
    row_in = lax.optimization_barrier(jnp.sum(blocks * inner[None, :, None, None], axis=(1, 3)))
    col_in = lax.optimization_barrier(jnp.sum(blocks * inner[None, None, None, :], axis=(1, 3)))
    three = jnp.arange(3, dtype=jnp.int32)
    key_row = (row_at - 1 + three)[:, None] * REGION + row_in
    key_col = (col_at - 1 + three)[None, :] * REGION + col_in
    query_row = (row_at * REGION + slot // REGION).astype(jnp.int32)
    query_col = (col_at * REGION + slot % REGION).astype(jnp.int32)
    present = lax.dynamic_slice(tissue, (query_row, query_col), (1, 1))[0, 0]
    inside = (jnp.abs(key_row - query_row) <= RADIUS) & (jnp.abs(key_col - query_col) <= RADIUS) & (occupied > 0)
    centre = (three[:, None] == 1) & (three[None, :] == 1)
    return ((inside | centre).reshape(9), present)

def attend(queries, key_rows, val_rows, allowed, dattn):
    tile_len = queries.shape[0]
    heads = queries.shape[1] // HEAD_DIM
    scale = HEAD_DIM ** (-0.5)
    keep = jnp.repeat(allowed, tile_len)

    def split(arr):
        return arr.reshape(arr.shape[0], heads, HEAD_DIM).transpose(1, 0, 2)

    def one_head(parts):
        q_h, k_h, v_h, g_h = parts
        scores = jnp.dot(q_h, k_h.T, preferred_element_type=jnp.float32) * scale
        scores = jnp.where(keep[None, :], scores, NEG_BIG)
        top = lax.optimization_barrier(jnp.max(scores, axis=1, keepdims=True))
        weights = jnp.exp(scores - top)
        probs = weights / lax.optimization_barrier(jnp.sum(weights, axis=1, keepdims=True))
        probs_b = probs.astype(jnp.bfloat16)
        output = jnp.dot(probs_b, v_h, preferred_element_type=jnp.float32)
        dprobs = jnp.dot(g_h, v_h.T, preferred_element_type=jnp.float32)
        centred = dprobs - lax.optimization_barrier(jnp.sum(dprobs * probs, axis=1, keepdims=True))
        dscores = (probs * centred * scale).astype(jnp.bfloat16)
        dquery = jnp.dot(dscores, k_h, preferred_element_type=jnp.float32)
        dkey = jnp.dot(dscores.T, q_h, preferred_element_type=jnp.float32)
        dvalue = jnp.dot(probs_b.T, g_h, preferred_element_type=jnp.float32)
        return (output, dquery, dkey, dvalue)
    results = lax.map(one_head, (split(queries), split(key_rows), split(val_rows), split(dattn)))

    def merge_heads(arr):
        return arr.transpose(1, 0, 2).reshape(arr.shape[1], heads * HEAD_DIM)
    return (merge_heads(results[0]), merge_heads(results[1]), merge_heads(results[2]), merge_heads(results[3]))

def reference(tokens, layer_norm_gain, proj_in, proj_out, tissue, tile_slot, cotangent):
    devices = N_ROW * N_COL
    tile_len = TILE_TOK
    inner_width = HD
    flattened_tokens = tokens.reshape(devices, tile_len, D)
    flat_cot = cotangent.reshape(devices, tile_len, D)

    def project(attention_block):
        centred_scaled_input, inverse_deviation = apply_layer_norm(attention_block)
        normalized_tokens = (centred_scaled_input * layer_norm_gain).astype(jnp.bfloat16)
        return (normalized_tokens, jnp.dot(normalized_tokens, proj_in, preferred_element_type=jnp.float32).astype(jnp.bfloat16))
    normed_all, qkv_all = lax.map(project, flattened_tokens)
    pair_grid = qkv_all[:, :, inner_width:].reshape(N_ROW, N_COL, tile_len, 2 * inner_width)
    pair_grid = jnp.pad(pair_grid, ((1, 1), (1, 1), (0, 0), (0, 0)))
    zero = jnp.int32(0)

    def attention_step(carry, block_index):
        store, grad_out = carry
        row_at = (block_index // N_COL).astype(jnp.int32)
        col_at = (block_index % N_COL).astype(jnp.int32)
        near_kv = lax.dynamic_slice(pair_grid, (row_at, col_at, zero, zero), (3, 3, tile_len, 2 * inner_width))
        near_kv = near_kv.reshape(9 * tile_len, 2 * inner_width)
        allowed, present = geometry(tissue, row_at, col_at, tile_slot[row_at, col_at])
        cot_block = flat_cot[block_index]
        dy_live = jnp.where(present > 0, cot_block, jnp.zeros_like(cot_block))
        dattn = jnp.dot(dy_live, proj_out.T, preferred_element_type=jnp.float32).astype(jnp.bfloat16)
        output, dquery, dkey, dvalue = attend(qkv_all[block_index][:, :inner_width], near_kv[:, :inner_width], near_kv[:, inner_width:], allowed, dattn)
        attn_b = output.astype(jnp.bfloat16)
        branch = jnp.dot(attn_b, proj_out, preferred_element_type=jnp.float32)
        branch = jnp.where(present > 0, branch, jnp.zeros_like(branch)).astype(jnp.bfloat16)
        grad_out = grad_out + jnp.dot(attn_b.T, dy_live, preferred_element_type=jnp.float32)
        rounded = lax.optimization_barrier(jnp.concatenate([dkey, dvalue], axis=1).astype(jnp.bfloat16))
        partial_value = rounded.astype(jnp.float32).reshape(3, 3, tile_len, 2 * inner_width)
        current = lax.dynamic_slice(store, (row_at, col_at, zero, zero), (3, 3, tile_len, 2 * inner_width))
        store = lax.dynamic_update_slice(store, current + partial_value, (row_at, col_at, zero, zero))
        return ((store, grad_out), (branch, dquery))
    store0 = jnp.zeros((N_ROW + 2, N_COL + 2, tile_len, 2 * inner_width), jnp.float32)
    grad_out0 = jnp.zeros((inner_width, D), jnp.float32)
    indices = jnp.arange(devices, dtype=jnp.int32)
    (store, grad_out), (branch_all, dquery_all) = lax.scan(attention_step, (store0, grad_out0), indices)

    def input_step(carry, block_index):
        grad_in, gain_gradient = carry
        row_at = (block_index // N_COL).astype(jnp.int32)
        col_at = (block_index % N_COL).astype(jnp.int32)
        centred_scaled_input, inverse_deviation = apply_layer_norm(flattened_tokens[block_index])
        summed = lax.dynamic_slice(store, (row_at + 1, col_at + 1, zero, zero), (1, 1, tile_len, 2 * inner_width))
        summed = summed.reshape(tile_len, 2 * inner_width)
        dqkv = jnp.concatenate([dquery_all[block_index], summed], axis=1).astype(jnp.bfloat16)
        grad_in = grad_in + jnp.dot(normed_all[block_index].T, dqkv, preferred_element_type=jnp.float32)
        normalized_gradient = jnp.dot(dqkv, proj_in.T, preferred_element_type=jnp.float32)
        gain_gradient = gain_gradient + lax.optimization_barrier(jnp.sum(normalized_gradient * centred_scaled_input, axis=0))
        centred_scaled_gradient = normalized_gradient * layer_norm_gain
        input_gradient = inverse_deviation * (centred_scaled_gradient - lax.optimization_barrier(jnp.mean(centred_scaled_gradient, axis=-1, keepdims=True)) - centred_scaled_input * lax.optimization_barrier(jnp.mean(centred_scaled_gradient * centred_scaled_input, axis=-1, keepdims=True)))
        return ((grad_in, gain_gradient), input_gradient.astype(jnp.bfloat16))
    grad_in0 = jnp.zeros((D, 3 * inner_width), jnp.float32)
    grad_gain0 = jnp.zeros((D,), jnp.float32)
    (grad_in, gain_gradient), grad_all = lax.scan(input_step, (grad_in0, grad_gain0), indices)
    total_sq = jnp.sum(grad_in * grad_in) + jnp.sum(grad_out * grad_out) + jnp.sum(gain_gradient * gain_gradient)
    factor = 1.0 / jnp.maximum(jnp.sqrt(total_sq / COUNT), 1.0)
    branch_out = branch_all.reshape(N_ROW, N_COL, tile_len, D)
    branch_grad = grad_all.reshape(N_ROW, N_COL, tile_len, D)
    return (branch_out, branch_grad, factor * grad_in, factor * grad_out, factor * gain_gradient)
```

```python
import functools

import jax
import jax.numpy as jnp
from jax import lax
from jax.experimental import pallas as pl
from jax.experimental.pallas import tpu as pltpu
from jax.sharding import Mesh
from jax.sharding import PartitionSpec as P

HEAD_DIM = 64
REGION = 3
RADIUS = 3
EPSILON = 1e-05
NEG_BIG = -1e30
GROUPS = 3

AXES = ("x", "zh", "y", "zl", "core")
CHIPS = ("x", "zh", "y", "zl")
SIZES = (4, 2, 4, 2, 2)
ROWS, COLS = 8, 16
N_CHIP = 64

NN = (((1,), (0,)), ((), ()))
NT = (((1,), (1,)), ((), ()))
TN = (((0,), (0,)), ((), ()))
f32 = jnp.float32
bf16 = jnp.bfloat16


def dot(a, b, dims=NN):
    return lax.dot_general(a, b, dims, preferred_element_type=f32)


def shift(value, rows, cols):
    route = [
        (r * COLS + c, (r + rows) * COLS + c + cols)
        for r in range(ROWS)
        for c in range(COLS)
        if 0 <= r + rows < ROWS and 0 <= c + cols < COLS
    ]
    return lax.ppermute(value, AXES, route)


def to_sibling(value):
    return lax.ppermute(value, "core", [(0, 1), (1, 0)])


def apply_layer_norm(block):
    values = block.astype(f32)
    centred = values - jnp.mean(values, axis=-1, keepdims=True)
    inverse_deviation = lax.rsqrt(jnp.mean(centred * centred, axis=-1, keepdims=True) + EPSILON)
    return (centred * inverse_deviation, inverse_deviation)


def geometry(tissue, row_at, col_at, slot):
    padded = jnp.pad(tissue, REGION)
    window = lax.dynamic_slice(padded, (row_at * REGION, col_at * REGION), (3 * REGION, 3 * REGION))
    blocks = window.reshape(3, REGION, 3, REGION)
    occupied = jnp.sum(blocks, axis=(1, 3))
    inner = jnp.arange(REGION, dtype=jnp.int32)
    row_in = jnp.sum(blocks * inner[None, :, None, None], axis=(1, 3))
    col_in = jnp.sum(blocks * inner[None, None, None, :], axis=(1, 3))
    three = jnp.arange(3, dtype=jnp.int32)
    key_row = (row_at - 1 + three)[:, None] * REGION + row_in
    key_col = (col_at - 1 + three)[None, :] * REGION + col_in
    query_row = row_at * REGION + slot // REGION
    query_col = col_at * REGION + slot % REGION
    present = lax.dynamic_slice(tissue, (query_row, query_col), (1, 1))[0, 0]
    inside = (
        (jnp.abs(key_row - query_row) <= RADIUS)
        & (jnp.abs(key_col - query_col) <= RADIUS)
        & (occupied > 0)
    )
    centre = (three[:, None] == 1) & (three[None, :] == 1)
    return ((inside | centre).reshape(9).astype(jnp.int32), present)


def attend_kernel(allow_ref, q_ref, g_ref, left_ref, mid_ref, right_ref,
                  out_ref, dq_ref, dleft_ref, dmid_ref, dright_ref, s_scr, dp_scr):
    tile_len = q_ref.shape[0]
    kv_refs = (left_ref, mid_ref, right_ref)
    dkv_refs = (dleft_ref, dmid_ref, dright_ref)
    places = [(a, b) for b in range(3) for a in range(3)]
    first = lax.broadcasted_iota(jnp.int32, (tile_len, 2 * HEAD_DIM), 1) < HEAD_DIM

    def head_pair(v):
        zero = jnp.zeros_like(v)
        return jnp.concatenate([jnp.where(first, v, zero), jnp.where(first, zero, v)], axis=0)

    qq = head_pair(q_ref[...] * jnp.asarray(HEAD_DIM ** -0.5, bf16))
    gg = head_pair(g_ref[...])
    top = jnp.full((1, 2 * tile_len), NEG_BIG, f32)
    for i, (a, b) in enumerate(places):
        scores = dot(kv_refs[b][a, 0], qq, NT)
        scores = jnp.where(allow_ref[a * 3 + b] > 0, scores, NEG_BIG)
        s_scr[i] = scores
        top = jnp.maximum(top, jnp.max(scores, axis=0, keepdims=True))
    total = jnp.zeros((1, 2 * tile_len), f32)
    mix = jnp.zeros((1, 2 * tile_len), f32)
    for i, (a, b) in enumerate(places):
        weights = jnp.exp(s_scr[i] - top)
        dprobs = dot(kv_refs[b][a, 1], gg, NT)
        total = total + jnp.sum(weights, axis=0, keepdims=True)
        mix = mix + jnp.sum(dprobs * weights, axis=0, keepdims=True)
        s_scr[i] = weights
        dp_scr[i] = dprobs
    inverse = 1.0 / total
    mix = mix * inverse
    outs = [jnp.zeros((HEAD_DIM, tile_len), f32)] * 2
    dqs = [jnp.zeros((HEAD_DIM, tile_len), f32)] * 2
    for i, (a, b) in enumerate(places):
        probs = s_scr[i] * inverse
        probs_b = probs.astype(bf16)
        dscores = (probs * (dp_scr[i] - mix)).astype(bf16)
        dkv_refs[b][a, 1] = dot(probs_b, gg).astype(bf16)
        dkv_refs[b][a, 0] = dot(dscores, qq).astype(bf16)
        keys_t = kv_refs[b][a, 0].T
        vals_t = kv_refs[b][a, 1].T
        for h in range(2):
            part = slice(h * HEAD_DIM, (h + 1) * HEAD_DIM)
            lanes = slice(h * tile_len, (h + 1) * tile_len)
            outs[h] = outs[h] + dot(vals_t[part], probs_b[:, lanes])
            dqs[h] = dqs[h] + dot(keys_t[part], dscores[:, lanes])
    out_ref[...] = jnp.concatenate(outs, axis=0).T.astype(bf16)
    dq_ref[...] = (jnp.concatenate(dqs, axis=0).T * HEAD_DIM ** -0.5).astype(bf16)


def attend(allowed, qkv, dattn, left, mid, right, group):
    tile_len, width = (mid.shape[2], mid.shape[3])
    block = 2 * HEAD_DIM
    steps = width // block
    place = lambda h: (0, h + group * steps)
    near = lambda h: (0, 0, 0, h)
    kv_spec = pl.BlockSpec((3, 2, tile_len, block), near)
    row_spec = pl.BlockSpec((tile_len, block), lambda h: (0, h))
    row_shape = jax.ShapeDtypeStruct((tile_len, width), bf16)
    kv_shape = jax.ShapeDtypeStruct(mid.shape, bf16)
    scratch = pltpu.VMEM((9, tile_len, 2 * tile_len), f32)
    return pl.pallas_call(
        attend_kernel,
        grid=(steps,),
        in_specs=[
            pl.BlockSpec(memory_space=pltpu.SMEM),
            pl.BlockSpec((tile_len, block), place),
            pl.BlockSpec((tile_len, block), place),
            kv_spec, kv_spec, kv_spec,
        ],
        out_specs=[row_spec, row_spec, kv_spec, kv_spec, kv_spec],
        out_shape=[row_shape, row_shape, kv_shape, kv_shape, kv_shape],
        scratch_shapes=[scratch, scratch],
        compiler_params=pltpu.CompilerParams(vmem_limit_bytes=40 * 1024 * 1024),
    )(allowed, qkv, dattn, left, mid, right)


def local(tokens, layer_norm_gain, proj_in, proj_out, tissue, tile_slot, cotangent):
    chip_at = lax.axis_index(CHIPS)
    core = lax.axis_index("core")
    row_at = chip_at // (COLS // 2)
    col_at = (chip_at % (COLS // 2)) * 2 + core
    tile_len, width = tokens.shape[2:]
    inner = proj_out.shape[0]
    half = inner // 2
    own_half = core == 0

    def halves(value):
        size = value.shape[1] // 2
        lower, upper = (value[:, :size], value[:, size:])
        return (jnp.where(own_half, lower, upper), jnp.where(own_half, upper, lower))

    def both_slots(value):
        mine, other = halves(value)
        return jnp.concatenate([mine, to_sibling(other)], axis=0)

    xhat, inverse_deviation = apply_layer_norm(tokens[0, 0])
    normed = (xhat * layer_norm_gain).astype(bf16)
    qkv = dot(normed, proj_in).astype(bf16)
    allowed, present = geometry(tissue, row_at, col_at, tile_slot[0, 0])
    cot_block = cotangent[0, 0]
    dy = jnp.where(present > 0, cot_block, jnp.zeros_like(cot_block))
    dattn = dot(dy, proj_out, NT).astype(bf16)

    size = inner // GROUPS
    near = []
    for g in range(GROUPS):
        lo = g * size
        pair = jnp.stack([
            qkv[:, inner + lo:inner + lo + size],
            qkv[:, 2 * inner + lo:2 * inner + lo + size],
        ])
        mid = jnp.stack([shift(pair, 1, 0), pair, shift(pair, -1, 0)])
        near.append((shift(mid, 0, 1), mid, shift(mid, 0, -1)))

    outs, dqs, dkvs = ([], [], [])
    for g in range(GROUPS):
        out, dq, dleft, dmid, dright = attend(allowed, qkv, dattn, *near[g], g)
        from_right = shift(dleft, 0, -1)
        from_left = shift(dright, 0, 1)
        column = dmid.astype(f32) + from_right.astype(f32) + from_left.astype(f32)
        from_below = shift(column[0].astype(bf16), -1, 0)
        from_above = shift(column[2].astype(bf16), 1, 0)
        total = column[1] + from_below.astype(f32) + from_above.astype(f32)
        outs.append(out)
        dqs.append(dq)
        dkvs.append(total.astype(bf16))
    attn = jnp.concatenate(outs, axis=1)
    dq = jnp.concatenate(dqs, axis=1)
    dkv = jnp.concatenate(dkvs, axis=2)

    branch = dot(attn, proj_out)
    branch = jnp.where(present > 0, branch, jnp.zeros_like(branch)).astype(bf16)

    normed_both = jnp.concatenate([normed, to_sibling(normed)], axis=0)
    attn_both = jnp.concatenate([attn, to_sibling(attn)], axis=0)
    dy_both = both_slots(dy)
    blocks = half // 128

    def packed(grad, rows):
        count = grad.shape[1] // 128
        return grad.reshape(N_CHIP, rows, count, 128).transpose(0, 2, 1, 3).reshape(N_CHIP, count * rows, 128)

    def unpacked(share, rows):
        count = share.shape[0] // rows
        return share.reshape(count, rows, 128).transpose(1, 0, 2).reshape(rows, count * 128)

    def summed(value):
        moved = lax.all_to_all(value, CHIPS, 0, 0, tiled=True)
        return jnp.sum(moved.astype(f32), axis=0)

    rows_in, rows_out = (width // N_CHIP, inner // N_CHIP)
    grad_q = dot(normed_both, both_slots(dq), TN).astype(bf16)
    grad_out = dot(attn_both, dy_both, TN).astype(bf16)
    early = jnp.concatenate([packed(grad_q, rows_in), packed(grad_out, rows_out)], axis=1)
    early = summed(early)
    share_q = unpacked(early[:blocks * rows_in], rows_in)
    share_out = unpacked(early[blocks * rows_in:], rows_out)

    dqkv = jnp.concatenate([dq, dkv[0], dkv[1]], axis=1)
    dnormed = dot(dqkv, proj_in, NT)
    gain_gradient = jnp.sum(dnormed * xhat, axis=0)
    grad_k = dot(normed_both, both_slots(dkv[0]), TN).astype(bf16)
    grad_v = dot(normed_both, both_slots(dkv[1]), TN).astype(bf16)
    gain_part = jnp.pad(gain_gradient.astype(bf16).reshape(N_CHIP, 1, rows_in), ((0, 0), (0, 7), (0, 128 - rows_in)))
    late = summed(jnp.concatenate([packed(grad_k, rows_in), packed(grad_v, rows_in), gain_part], axis=1))
    span = blocks * rows_in
    share_k = unpacked(late[:span], rows_in)
    share_v = unpacked(late[span:2 * span], rows_in)
    share_gain = late[2 * span, :rows_in]
    share_gain = share_gain + to_sibling(share_gain)

    centred = dnormed * layer_norm_gain
    input_gradient = inverse_deviation * (
        centred
        - jnp.mean(centred, axis=-1, keepdims=True)
        - xhat * jnp.mean(centred * xhat, axis=-1, keepdims=True)
    )
    branch_grad = input_gradient.astype(bf16)

    total_sq = (
        jnp.sum(share_q * share_q)
        + jnp.sum(share_k * share_k)
        + jnp.sum(share_v * share_v)
        + jnp.sum(share_out * share_out)
        + 0.5 * jnp.sum(share_gain * share_gain)
    )
    total_sq = jnp.full((8, 128), total_sq, f32)
    for bit in range(7):
        total_sq = total_sq + lax.ppermute(total_sq, AXES, [(i, i ^ (1 << bit)) for i in range(ROWS * COLS)])
    total_sq = total_sq[0, 0]
    count = width * 3 * inner + inner * width + width
    factor = 1.0 / jnp.maximum(jnp.sqrt(total_sq / count), 1.0)

    share = jnp.concatenate([share_q, share_k, share_v], axis=1)

    def own_rows(value):
        size = value.shape[0] // 2
        lower, upper = (value[:size], value[size:])
        mine = jnp.where(own_half, lower, upper)
        other = to_sibling(jnp.where(own_half, upper, lower))
        return (jnp.where(own_half, mine, other), jnp.where(own_half, other, mine))

    low, high = own_rows(share)
    full_in = jnp.concatenate(
        [part[:, s * half:(s + 1) * half] for s in range(3) for part in (low, high)], axis=1
    )
    full_out = jnp.concatenate(own_rows(share_out), axis=1)
    size = rows_in // 2
    gain_own = jnp.where(own_half, share_gain[:size], share_gain[size:])
    return (
        branch[None, None],
        branch_grad[None, None],
        factor * full_in,
        factor * full_out,
        factor * gain_own,
    )


def solution(mesh):
    fine = Mesh(mesh.devices.reshape(SIZES), AXES)
    row, col = (("x", "zh"), ("y", "zl", "core"))
    in_specs = (
        P(row, col, None, None),
        P(),
        P(),
        P(),
        P(),
        P(row, col),
        P(row, col, None, None),
    )
    out_specs = (
        P(row, col, None, None),
        P(row, col, None, None),
        P(AXES, None),
        P(AXES, None),
        P(AXES),
    )
    return jax.shard_map(local, mesh=fine, in_specs=in_specs, out_specs=out_specs, check_vma=False)
```

```python
import jax
import jax.numpy as jnp
from jax import lax
from jax.experimental import pallas as pl
from jax.experimental.pallas import tpu as pltpu
from jax.sharding import Mesh
from jax.sharding import PartitionSpec as P

HEAD_DIM = 64
REGION = 3
RADIUS = 3
EPSILON = 1e-05
NEG_BIG = -1e30
GROUPS = 3

AXES = ("x", "zh", "y", "zl", "core")
CHIPS = ("x", "zh", "y", "zl")
SIZES = (4, 2, 4, 2, 2)
ROWS, COLS = 8, 16
N_CHIP = 64
SPAN = 24

NN = (((1,), (0,)), ((), ()))
NT = (((1,), (1,)), ((), ()))
TN = (((0,), (0,)), ((), ()))
f32 = jnp.float32
bf16 = jnp.bfloat16


def dot(a, b, dims=NN):
    return lax.dot_general(a, b, dims, preferred_element_type=f32)


def routes(move):
    index = lambda p: (((p[0] * 2 + p[1]) * 4 + p[2]) * 2 + p[3]) * 2 + p[4]
    places = [(x, zh, y, zl, c) for x in range(4) for zh in range(2)
              for y in range(4) for zl in range(2) for c in range(2)]
    pairs = [(p, move(*p)) for p in places]
    return [(index(p), index(t)) for p, t in pairs if 0 <= t[0] < 4 and 0 <= t[2] < 4]


def third_column(x, zh, y, zl, c):
    if c == zl:
        return (x, zh, y, zl, 1 - c)
    return (x, zh, y + 1 - 2 * zl, zl, 1 - c)


OTHER_ROW = routes(lambda x, zh, y, zl, c: (x, 1 - zh, y, zl, c))
OTHER_COL = routes(lambda x, zh, y, zl, c: (x, zh, y, 1 - zl, c))
OTHER_BOTH = routes(lambda x, zh, y, zl, c: (x, 1 - zh, y, 1 - zl, c))
BEYOND_ROW = routes(lambda x, zh, y, zl, c: (x + 1 - 2 * zh, zh, y, zl, c))
THIRD_COL = routes(third_column)


def move(value, route, back=False):
    return lax.ppermute(value, AXES, [(t, f) for f, t in route] if back else route)


def to_sibling(value):
    return lax.ppermute(value, "core", [(0, 1), (1, 0)])


def apply_layer_norm(block):
    values = block.astype(f32)
    centred = values - jnp.mean(values, axis=-1, keepdims=True)
    inverse_deviation = lax.rsqrt(jnp.mean(centred * centred, axis=-1, keepdims=True) + EPSILON)
    return (centred * inverse_deviation, inverse_deviation)


def geometry(tissue, row_at, col_at, slot):
    padded = jnp.pad(tissue, REGION)
    window = lax.dynamic_slice(padded, (row_at * REGION, col_at * REGION), (3 * REGION, 3 * REGION))
    blocks = window.reshape(3, REGION, 3, REGION)
    occupied = jnp.sum(blocks, axis=(1, 3))
    inner = jnp.arange(REGION, dtype=jnp.int32)
    row_in = jnp.sum(blocks * inner[None, :, None, None], axis=(1, 3))
    col_in = jnp.sum(blocks * inner[None, None, None, :], axis=(1, 3))
    three = jnp.arange(3, dtype=jnp.int32)
    key_row = (row_at - 1 + three)[:, None] * REGION + row_in
    key_col = (col_at - 1 + three)[None, :] * REGION + col_in
    query_row = row_at * REGION + slot // REGION
    query_col = col_at * REGION + slot % REGION
    present = lax.dynamic_slice(tissue, (query_row, query_col), (1, 1))[0, 0]
    inside = (
        (jnp.abs(key_row - query_row) <= RADIUS)
        & (jnp.abs(key_col - query_col) <= RADIUS)
        & (occupied > 0)
    )
    centre = (three[:, None] == 1) & (three[None, :] == 1)
    return ((inside | centre).astype(jnp.int32), present)


def attend_kernel(allow_ref, q_ref, g_ref, own_ref, side_ref, third_ref,
                  out_ref, dq_ref, down_ref, dside_ref, dthird_ref, s_scr, dp_scr):
    tile_len = q_ref.shape[0]
    kv_refs = (own_ref, side_ref, third_ref)
    dkv_refs = (down_ref, dside_ref, dthird_ref)
    places = [(a, b) for b in range(3) for a in range(3)]
    first = lax.broadcasted_iota(jnp.int32, (tile_len, 2 * HEAD_DIM), 1) < HEAD_DIM

    def head_pair(v):
        zero = jnp.zeros_like(v)
        return jnp.concatenate([jnp.where(first, v, zero), jnp.where(first, zero, v)], axis=0)

    qq = head_pair(q_ref[...] * jnp.asarray(HEAD_DIM ** -0.5, bf16))
    gg = head_pair(g_ref[...])
    top = jnp.full((1, 2 * tile_len), NEG_BIG, f32)
    for i, (a, b) in enumerate(places):
        scores = dot(kv_refs[b][a, 0], qq, NT)
        scores = jnp.where(allow_ref[b * 3 + a] > 0, scores, NEG_BIG)
        s_scr[i] = scores
        top = jnp.maximum(top, jnp.max(scores, axis=0, keepdims=True))
    total = jnp.zeros((1, 2 * tile_len), f32)
    mix = jnp.zeros((1, 2 * tile_len), f32)
    for i, (a, b) in enumerate(places):
        weights = jnp.exp(s_scr[i] - top)
        dprobs = dot(kv_refs[b][a, 1], gg, NT)
        total = total + jnp.sum(weights, axis=0, keepdims=True)
        mix = mix + jnp.sum(dprobs * weights, axis=0, keepdims=True)
        s_scr[i] = weights
        dp_scr[i] = dprobs
    inverse = 1.0 / total
    mix = mix * inverse
    outs = [jnp.zeros((HEAD_DIM, tile_len), f32)] * 2
    dqs = [jnp.zeros((HEAD_DIM, tile_len), f32)] * 2
    for i, (a, b) in enumerate(places):
        probs = s_scr[i] * inverse
        probs_b = probs.astype(bf16)
        dscores = (probs * (dp_scr[i] - mix)).astype(bf16)
        dkv_refs[b][a, 1] = dot(probs_b, gg).astype(bf16)
        dkv_refs[b][a, 0] = dot(dscores, qq).astype(bf16)
        keys_t = kv_refs[b][a, 0].T
        vals_t = kv_refs[b][a, 1].T
        for h in range(2):
            part = slice(h * HEAD_DIM, (h + 1) * HEAD_DIM)
            lanes = slice(h * tile_len, (h + 1) * tile_len)
            outs[h] = outs[h] + dot(vals_t[part], probs_b[:, lanes])
            dqs[h] = dqs[h] + dot(keys_t[part], dscores[:, lanes])
    out_ref[...] = jnp.concatenate(outs, axis=0).T.astype(bf16)
    dq_ref[...] = (jnp.concatenate(dqs, axis=0).T * HEAD_DIM ** -0.5).astype(bf16)


def attend(allowed, qkv, dattn, own, side, third, group):
    tile_len, width = (own.shape[2], own.shape[3])
    block = 2 * HEAD_DIM
    steps = width // block
    place = lambda h: (0, h + group * steps)
    near = lambda h: (0, 0, 0, h)
    kv_spec = pl.BlockSpec((3, 2, tile_len, block), near)
    row_spec = pl.BlockSpec((tile_len, block), lambda h: (0, h))
    row_shape = jax.ShapeDtypeStruct((tile_len, width), bf16)
    kv_shape = jax.ShapeDtypeStruct(own.shape, bf16)
    scratch = pltpu.VMEM((9, tile_len, 2 * tile_len), f32)
    return pl.pallas_call(
        attend_kernel,
        grid=(steps,),
        in_specs=[
            pl.BlockSpec(memory_space=pltpu.SMEM),
            pl.BlockSpec((tile_len, block), place),
            pl.BlockSpec((tile_len, block), place),
            kv_spec, kv_spec, kv_spec,
        ],
        out_specs=[row_spec, row_spec, kv_spec, kv_spec, kv_spec],
        out_shape=[row_shape, row_shape, kv_shape, kv_shape, kv_shape],
        scratch_shapes=[scratch, scratch],
        compiler_params=pltpu.CompilerParams(vmem_limit_bytes=40 * 1024 * 1024),
    )(allowed, qkv, dattn, own, side, third)


def grad_blocks(left_a, left_b, right_a, right_b, first, last):
    lanes = slice(first, last)
    grad = dot(left_a[:, lanes], right_a[...], TN) + dot(left_b[:, lanes], right_b[...], TN)
    return grad.astype(bf16)


def early_kernel(normed_a, normed_b, dq_a, dq_b, attn_a, attn_b, dy_a, dy_b, out_ref):
    step = 16 * SPAN
    blocks = dq_a.shape[1] // 128
    for r in range(normed_a.shape[1] // step):
        grad = grad_blocks(normed_a, normed_b, dq_a, dq_b, r * step, (r + 1) * step)
        for j in range(blocks):
            part = grad[:, j * 128:(j + 1) * 128].reshape(16, SPAN, 128)
            out_ref[r * 16:(r + 1) * 16, j] = part
    for r in range(attn_a.shape[1] // step):
        grad = grad_blocks(attn_a, attn_b, dy_a, dy_b, r * step, (r + 1) * step)
        for i in range(16):
            for q in range(2):
                for j in range(blocks):
                    col = (q * blocks + j) * 128
                    out_ref[2 * (r * 16 + i) + q, blocks + j] = grad[i * SPAN:(i + 1) * SPAN, col:col + 128]


def early_grads(*operands):
    blocks = operands[2].shape[1] // 128
    return pl.pallas_call(
        early_kernel,
        out_shape=jax.ShapeDtypeStruct((N_CHIP, 2 * blocks, SPAN, 128), bf16),
        compiler_params=pltpu.CompilerParams(vmem_limit_bytes=32 * 1024 * 1024),
    )(*operands)


def late_kernel(normed_a, normed_b, dkv_a, dkv_b, out_ref):
    step = 16 * SPAN
    for r in range(normed_a.shape[1] // step):
        grad = grad_blocks(normed_a, normed_b, dkv_a, dkv_b, r * step, (r + 1) * step)
        for j in range(dkv_a.shape[1] // 128):
            part = grad[:, j * 128:(j + 1) * 128].reshape(16, SPAN, 128)
            out_ref[r * 16:(r + 1) * 16, j] = part


def late_grads(*operands):
    return pl.pallas_call(
        late_kernel,
        out_shape=jax.ShapeDtypeStruct((N_CHIP, operands[2].shape[1] // 128, SPAN, 128), bf16),
        compiler_params=pltpu.CompilerParams(vmem_limit_bytes=32 * 1024 * 1024),
    )(*operands)


def summed(value):
    flat = value.reshape(N_CHIP, -1, 128)
    moved = lax.all_to_all(flat, CHIPS, 0, 0, tiled=True)
    return jnp.sum(moved.astype(f32), axis=0)


def unpacked(share):
    count = share.shape[0] // SPAN
    return share.reshape(count, SPAN, 128).transpose(1, 0, 2).reshape(SPAN, count * 128)


def square_sum(value):
    return jnp.sum(value * value)


def local(tokens, layer_norm_gain, proj_in, proj_out, tissue, tile_slot, cotangent):
    chip_at = lax.axis_index(CHIPS)
    core = lax.axis_index("core")
    zh = lax.axis_index("zh")
    row_at = chip_at // (COLS // 2)
    col_at = (chip_at % (COLS // 2)) * 2 + core
    tile_len, width = tokens.shape[2:]
    inner = proj_out.shape[0]
    half = inner // 2
    is_low = core == 0

    def swapped(lower, upper):
        mine, other = (jnp.where(is_low, lower, upper), jnp.where(is_low, upper, lower))
        return (mine, to_sibling(other))

    xhat, inverse_deviation = apply_layer_norm(tokens[0, 0])
    normed = (xhat * layer_norm_gain).astype(bf16)
    qkv = dot(normed, proj_in).astype(bf16)
    size = inner // GROUPS
    near = []
    tied = None
    for g in range(GROUPS):
        lo = inner + g * size
        own = jnp.stack([qkv[:, lo:lo + size], qkv[:, inner + lo:inner + lo + size]])
        if tied is not None:
            own, tied = lax.optimization_barrier((own, tied))
        col = move(own, OTHER_COL)
        both = move(own, OTHER_BOTH)
        row = move(own, OTHER_ROW)
        tied = row
        beyond = move(jnp.stack([row, both]), BEYOND_ROW)
        own_col = jnp.stack([own, row, beyond[0]])
        other_col = jnp.stack([col, both, beyond[1]])
        near.append((own_col, to_sibling(own_col), move(other_col, THIRD_COL)))

    allowed, present = geometry(tissue, row_at, col_at, tile_slot[0, 0])
    first_row = zh == 0
    allowed = jnp.stack([
        allowed[1],
        jnp.where(first_row, allowed[2], allowed[0]),
        jnp.where(first_row, allowed[0], allowed[2]),
    ])
    allowed = jnp.concatenate([
        allowed[:, 1],
        jnp.where(is_low, allowed[:, 2], allowed[:, 0]),
        jnp.where(is_low, allowed[:, 0], allowed[:, 2]),
    ])
    cot_block = cotangent[0, 0]
    dy = jnp.where(present > 0, cot_block, jnp.zeros_like(cot_block))
    dattn = dot(dy, proj_out, NT).astype(bf16)
    normed_side = to_sibling(normed)
    dy_mine, dy_side = swapped(
        jnp.concatenate([dy[:, :half], dy[:, inner:inner + half]], axis=1),
        jnp.concatenate([dy[:, half:inner], dy[:, inner + half:]], axis=1),
    )

    outs, dqs, dkvs, lates = ([], [], [], [])
    for g in range(GROUPS):
        out, dq, down, dside, dthird = attend(allowed, qkv, dattn, *near[g], g)
        side = to_sibling(dside)
        third = move(dthird, THIRD_COL, back=True)
        column = down.astype(f32) + side.astype(f32)
        beyond = move(jnp.stack([column[2].astype(bf16), third[2]]), BEYOND_ROW, back=True)
        beyond = beyond.astype(f32)
        row = move((column[1] + beyond[0]).astype(bf16), OTHER_ROW)
        both = move((third[1].astype(f32) + beyond[1]).astype(bf16), OTHER_BOTH)
        col = move(third[0], OTHER_COL)
        total = column[0] + row.astype(f32) + both.astype(f32) + col.astype(f32)
        total = total.astype(bf16)
        outs.append(out)
        dqs.append(dq)
        dkvs.append(total)
        lates.append(late_grads(normed, normed_side, *swapped(total[0], total[1])))

    attn = jnp.concatenate(outs, axis=1)
    dq = jnp.concatenate(dqs, axis=1)
    branch = dot(attn, proj_out)
    branch = jnp.where(present > 0, branch, jnp.zeros_like(branch)).astype(bf16)
    early = early_grads(
        normed, normed_side, *swapped(dq[:, :half], dq[:, half:]), attn, to_sibling(attn), dy_mine, dy_side
    )
    early = summed(early)
    blocks = half // 128
    share_q = unpacked(early[:blocks * SPAN])
    share_out = unpacked(early[blocks * SPAN:])

    dqkv = jnp.concatenate(
        [dq] + [total[0] for total in dkvs] + [total[1] for total in dkvs], axis=1
    )
    dnormed = dot(dqkv, proj_in, NT)
    gain_gradient = jnp.sum(dnormed * xhat, axis=0)
    gain_part = gain_gradient.astype(bf16).reshape(N_CHIP, 1, SPAN)
    gain_part = jnp.pad(gain_part, ((0, 0), (0, 7), (0, 128 - SPAN)))
    late = jnp.concatenate([part.reshape(N_CHIP, -1, 128) for part in lates] + [gain_part], axis=1)
    late = summed(late)
    share_kv = unpacked(late[:2 * blocks * SPAN])
    share_gain = late[2 * blocks * SPAN, :SPAN]
    share_gain = share_gain + to_sibling(share_gain)

    centred = dnormed * layer_norm_gain
    input_gradient = inverse_deviation * (
        centred
        - jnp.mean(centred, axis=-1, keepdims=True)
        - xhat * jnp.mean(centred * xhat, axis=-1, keepdims=True)
    )
    branch_grad = input_gradient.astype(bf16)

    total_sq = (
        square_sum(share_q) + square_sum(share_out) + square_sum(share_kv) + 0.5 * square_sum(share_gain)
    )
    total_sq = jnp.full((8, 128), total_sq, f32)
    for bit in range(7):
        total_sq = total_sq + lax.ppermute(total_sq, AXES, [(i, i ^ (1 << bit)) for i in range(ROWS * COLS)])
    total_sq = total_sq[0, 0]
    count = width * 3 * inner + inner * width + width
    factor = 1.0 / jnp.maximum(jnp.sqrt(total_sq / count), 1.0)

    def own_rows(value):
        rows = value.shape[0] // 2
        mine, other = swapped(value[:rows], value[rows:])
        return [jnp.where(is_low, mine, other), jnp.where(is_low, other, mine)]

    full_in = jnp.concatenate(own_rows(share_q) + own_rows(share_kv), axis=1)
    rows = share_out.shape[0] // 4
    moved = lax.all_to_all(share_out.reshape(4, rows, half), ("zl", "core"), 0, 0, tiled=True)
    full_out = moved.transpose(1, 0, 2).reshape(rows, 4 * half)
    rows = SPAN // 2
    gain_own = jnp.where(is_low, share_gain[:rows], share_gain[rows:])
    return (
        branch[None, None],
        branch_grad[None, None],
        factor * full_in,
        factor * full_out,
        factor * gain_own,
    )


def solution(mesh):
    fine = Mesh(mesh.devices.reshape(SIZES), AXES)
    row, col = (("x", "zh"), ("y", "zl", "core"))
    in_specs = (
        P(row, col, None, None),
        P(),
        P(),
        P(),
        P(),
        P(row, col),
        P(row, col, None, None),
    )
    out_specs = (
        P(row, col, None, None),
        P(row, col, None, None),
        P(AXES, None),
        P(AXES, None),
        P(AXES),
    )
    return jax.shard_map(local, mesh=fine, in_specs=in_specs, out_specs=out_specs, check_vma=False)
```

```python
import jax
import jax.numpy as jnp
from jax import lax
from jax.experimental import pallas as pl
from jax.experimental.pallas import tpu as pltpu
from jax.sharding import Mesh
from jax.sharding import PartitionSpec as P

HEAD_DIM = 64
REGION = 3
RADIUS = 3
EPSILON = 1e-05
NEG_BIG = -1e30
GROUPS = 3

AXES = ("x", "zh", "y", "zl", "core")
CHIPS = ("x", "zh", "y", "zl")
SIZES = (4, 2, 4, 2, 2)
ROWS, COLS = 8, 16
N_CHIP = 64
SPAN = 24

NN = (((1,), (0,)), ((), ()))
NT = (((1,), (1,)), ((), ()))
TN = (((0,), (0,)), ((), ()))
f32 = jnp.float32
bf16 = jnp.bfloat16


def dot(a, b, dims=NN):
    return lax.dot_general(a, b, dims, preferred_element_type=f32)


def routes(move):
    index = lambda p: (((p[0] * 2 + p[1]) * 4 + p[2]) * 2 + p[3]) * 2 + p[4]
    places = [(x, zh, y, zl, c) for x in range(4) for zh in range(2)
              for y in range(4) for zl in range(2) for c in range(2)]
    pairs = [(p, move(*p)) for p in places]
    return [(index(p), index(t)) for p, t in pairs if 0 <= t[0] < 4 and 0 <= t[2] < 4]


def third_column(x, zh, y, zl, c):
    if c == zl:
        return (x, zh, y, zl, 1 - c)
    return (x, zh, y + 1 - 2 * zl, zl, 1 - c)


OTHER_ROW = routes(lambda x, zh, y, zl, c: (x, 1 - zh, y, zl, c))
OTHER_COL = routes(lambda x, zh, y, zl, c: (x, zh, y, 1 - zl, c))
OTHER_BOTH = routes(lambda x, zh, y, zl, c: (x, 1 - zh, y, 1 - zl, c))
BEYOND_ROW = routes(lambda x, zh, y, zl, c: (x + 1 - 2 * zh, zh, y, zl, c))
THIRD_COL = routes(third_column)


def after(value, *others):
    return lax.optimization_barrier((value,) + others)[0]


def move(value, route, back=False):
    return lax.ppermute(value, AXES, [(t, f) for f, t in route] if back else route)


def to_sibling(value):
    return lax.ppermute(value, "core", [(0, 1), (1, 0)])


def apply_layer_norm(block):
    values = block.astype(f32)
    centred = values - jnp.mean(values, axis=-1, keepdims=True)
    inverse_deviation = lax.rsqrt(jnp.mean(centred * centred, axis=-1, keepdims=True) + EPSILON)
    return (centred * inverse_deviation, inverse_deviation)


def geometry(tissue, row_at, col_at, slot):
    padded = jnp.pad(tissue, REGION)
    window = lax.dynamic_slice(padded, (row_at * REGION, col_at * REGION), (3 * REGION, 3 * REGION))
    blocks = window.reshape(3, REGION, 3, REGION)
    occupied = jnp.sum(blocks, axis=(1, 3))
    inner = jnp.arange(REGION, dtype=jnp.int32)
    row_in = jnp.sum(blocks * inner[None, :, None, None], axis=(1, 3))
    col_in = jnp.sum(blocks * inner[None, None, None, :], axis=(1, 3))
    three = jnp.arange(3, dtype=jnp.int32)
    key_row = (row_at - 1 + three)[:, None] * REGION + row_in
    key_col = (col_at - 1 + three)[None, :] * REGION + col_in
    query_row = row_at * REGION + slot // REGION
    query_col = col_at * REGION + slot % REGION
    present = lax.dynamic_slice(tissue, (query_row, query_col), (1, 1))[0, 0]
    inside = (
        (jnp.abs(key_row - query_row) <= RADIUS)
        & (jnp.abs(key_col - query_col) <= RADIUS)
        & (occupied > 0)
    )
    centre = (three[:, None] == 1) & (three[None, :] == 1)
    return ((inside | centre).astype(jnp.int32), present)


def attend_kernel(allow_ref, q_ref, g_ref, own_ref, side_ref, third_ref,
                  out_ref, dq_ref, down_ref, dside_ref, dthird_ref, s_scr, dp_scr):
    tile_len = q_ref.shape[0]
    kv_refs = (own_ref, side_ref, third_ref)
    dkv_refs = (down_ref, dside_ref, dthird_ref)
    places = [(a, b) for b in range(3) for a in range(3)]
    first = lax.broadcasted_iota(jnp.int32, (tile_len, 2 * HEAD_DIM), 1) < HEAD_DIM

    def head_pair(v):
        zero = jnp.zeros_like(v)
        return jnp.concatenate([jnp.where(first, v, zero), jnp.where(first, zero, v)], axis=0)

    qq = head_pair(q_ref[...] * jnp.asarray(HEAD_DIM ** -0.5, bf16))
    gg = head_pair(g_ref[...])
    top = jnp.full((1, 2 * tile_len), NEG_BIG, f32)
    for i, (a, b) in enumerate(places):
        scores = dot(kv_refs[b][a, 0], qq, NT)
        scores = jnp.where(allow_ref[b * 3 + a] > 0, scores, NEG_BIG)
        s_scr[i] = scores
        top = jnp.maximum(top, jnp.max(scores, axis=0, keepdims=True))
    total = jnp.zeros((1, 2 * tile_len), f32)
    mix = jnp.zeros((1, 2 * tile_len), f32)
    for i, (a, b) in enumerate(places):
        weights = jnp.exp(s_scr[i] - top)
        dprobs = dot(kv_refs[b][a, 1], gg, NT)
        total = total + jnp.sum(weights, axis=0, keepdims=True)
        mix = mix + jnp.sum(dprobs * weights, axis=0, keepdims=True)
        s_scr[i] = weights
        dp_scr[i] = dprobs
    inverse = 1.0 / total
    mix = mix * inverse
    outs = [jnp.zeros((HEAD_DIM, tile_len), f32)] * 2
    dqs = [jnp.zeros((HEAD_DIM, tile_len), f32)] * 2
    for i, (a, b) in enumerate(places):
        probs = s_scr[i] * inverse
        probs_b = probs.astype(bf16)
        dscores = (probs * (dp_scr[i] - mix)).astype(bf16)
        dkv_refs[b][a, 1] = dot(probs_b, gg).astype(bf16)
        dkv_refs[b][a, 0] = dot(dscores, qq).astype(bf16)
        keys_t = kv_refs[b][a, 0].T
        vals_t = kv_refs[b][a, 1].T
        for h in range(2):
            part = slice(h * HEAD_DIM, (h + 1) * HEAD_DIM)
            lanes = slice(h * tile_len, (h + 1) * tile_len)
            outs[h] = outs[h] + dot(vals_t[part], probs_b[:, lanes])
            dqs[h] = dqs[h] + dot(keys_t[part], dscores[:, lanes])
    out_ref[...] = jnp.concatenate(outs, axis=0).T.astype(bf16)
    dq_ref[...] = (jnp.concatenate(dqs, axis=0).T * HEAD_DIM ** -0.5).astype(bf16)


def attend(allowed, queries, dattn, own, side, third, group):
    tile_len, width = (own.shape[2], own.shape[3])
    block = 2 * HEAD_DIM
    steps = width // block
    place = lambda h: (0, h + group * steps)
    near = lambda h: (0, 0, 0, h)
    kv_spec = pl.BlockSpec((3, 2, tile_len, block), near)
    row_spec = pl.BlockSpec((tile_len, block), lambda h: (0, h))
    row_shape = jax.ShapeDtypeStruct((tile_len, width), bf16)
    kv_shape = jax.ShapeDtypeStruct(own.shape, bf16)
    scratch = pltpu.VMEM((9, tile_len, 2 * tile_len), f32)
    return pl.pallas_call(
        attend_kernel,
        grid=(steps,),
        in_specs=[
            pl.BlockSpec(memory_space=pltpu.SMEM),
            pl.BlockSpec((tile_len, block), place),
            pl.BlockSpec((tile_len, block), place),
            kv_spec, kv_spec, kv_spec,
        ],
        out_specs=[row_spec, row_spec, kv_spec, kv_spec, kv_spec],
        out_shape=[row_shape, row_shape, kv_shape, kv_shape, kv_shape],
        scratch_shapes=[scratch, scratch],
        compiler_params=pltpu.CompilerParams(vmem_limit_bytes=40 * 1024 * 1024),
        cost_estimate=pl.CostEstimate(
            flops=width * tile_len * tile_len * 9 * 12 * 4,
            bytes_accessed=width * tile_len * 2 * 40,
            transcendentals=width // HEAD_DIM * tile_len * tile_len * 9,
        ),
    )(allowed, queries, dattn, own, side, third)


def grad_blocks(left_a, left_b, right_a, right_b, first, last):
    lanes = slice(first, last)
    grad = dot(left_a[:, lanes], right_a[...], TN) + dot(left_b[:, lanes], right_b[...], TN)
    return grad.astype(bf16)


def early_kernel(normed_a, normed_b, dq_a, dq_b, attn_a, attn_b, dy_a, dy_b, out_ref):
    step = 16 * SPAN
    blocks = dq_a.shape[1] // 128
    for r in range(normed_a.shape[1] // step):
        grad = grad_blocks(normed_a, normed_b, dq_a, dq_b, r * step, (r + 1) * step)
        for j in range(blocks):
            part = grad[:, j * 128:(j + 1) * 128].reshape(16, SPAN, 128)
            out_ref[r * 16:(r + 1) * 16, j] = part
    for r in range(attn_a.shape[1] // step):
        grad = grad_blocks(attn_a, attn_b, dy_a, dy_b, r * step, (r + 1) * step)
        for i in range(16):
            for q in range(2):
                for j in range(blocks):
                    col = (q * blocks + j) * 128
                    out_ref[2 * (r * 16 + i) + q, blocks + j] = grad[i * SPAN:(i + 1) * SPAN, col:col + 128]


def early_grads(*operands):
    blocks = operands[2].shape[1] // 128
    return pl.pallas_call(
        early_kernel,
        out_shape=jax.ShapeDtypeStruct((N_CHIP, 2 * blocks, SPAN, 128), bf16),
        compiler_params=pltpu.CompilerParams(vmem_limit_bytes=32 * 1024 * 1024),
    )(*operands)


def late_kernel(normed_a, normed_b, dkv_a, dkv_b, out_ref):
    step = 16 * SPAN
    for r in range(normed_a.shape[1] // step):
        grad = grad_blocks(normed_a, normed_b, dkv_a, dkv_b, r * step, (r + 1) * step)
        for j in range(dkv_a.shape[1] // 128):
            part = grad[:, j * 128:(j + 1) * 128].reshape(16, SPAN, 128)
            out_ref[r * 16:(r + 1) * 16, j] = part


def late_grads(*operands):
    return pl.pallas_call(
        late_kernel,
        out_shape=jax.ShapeDtypeStruct((N_CHIP, operands[2].shape[1] // 128, SPAN, 128), bf16),
        compiler_params=pltpu.CompilerParams(vmem_limit_bytes=32 * 1024 * 1024),
    )(*operands)


def summed(value):
    flat = value.reshape(N_CHIP, -1, 128)
    moved = lax.all_to_all(flat, CHIPS, 0, 0, tiled=True)
    return jnp.sum(moved.astype(f32), axis=0)


def unpacked(share):
    count = share.shape[0] // SPAN
    return share.reshape(count, SPAN, 128).transpose(1, 0, 2).reshape(SPAN, count * 128)


def square_sum(value):
    return jnp.sum(value * value)


def local(tokens, layer_norm_gain, proj_in, proj_out, tissue, tile_slot, cotangent):
    chip_at = lax.axis_index(CHIPS)
    core = lax.axis_index("core")
    zh = lax.axis_index("zh")
    row_at = chip_at // (COLS // 2)
    col_at = (chip_at % (COLS // 2)) * 2 + core
    tile_len, width = tokens.shape[2:]
    inner = proj_out.shape[0]
    half = inner // 2
    is_low = core == 0

    def swapped(lower, upper):
        mine, other = (jnp.where(is_low, lower, upper), jnp.where(is_low, upper, lower))
        return (mine, to_sibling(other))

    xhat, inverse_deviation = apply_layer_norm(tokens[0, 0])
    normed = (xhat * layer_norm_gain).astype(bf16)
    size = inner // GROUPS

    def gather_block(g, tied):
        lo = inner + g * size
        weights = jnp.stack([proj_in[:, lo:lo + size], proj_in[:, inner + lo:inner + lo + size]])
        own = jnp.stack([dot(normed, weights[0]), dot(normed, weights[1])]).astype(bf16)
        if tied is not None:
            own = after(own, tied)
        return (own, move(own, OTHER_ROW), move(own, OTHER_COL), move(own, OTHER_BOTH))

    def gather_rows(own, row, col, both):
        beyond = move(jnp.stack([row, both]), BEYOND_ROW)
        return (jnp.stack([own, row, beyond[0]]), jnp.stack([col, both, beyond[1]]))

    blocks_near = []
    for g in range(GROUPS):
        blocks_near.append(gather_block(g, blocks_near[-1][1] if g else None))
    queries = dot(normed, proj_in[:, :inner]).astype(bf16)
    rows_near = [gather_rows(*block) for block in blocks_near]

    allowed, present = geometry(tissue, row_at, col_at, tile_slot[0, 0])
    first_row = zh == 0
    allowed = jnp.stack([
        allowed[1],
        jnp.where(first_row, allowed[2], allowed[0]),
        jnp.where(first_row, allowed[0], allowed[2]),
    ])
    allowed = jnp.concatenate([
        allowed[:, 1],
        jnp.where(is_low, allowed[:, 2], allowed[:, 0]),
        jnp.where(is_low, allowed[:, 0], allowed[:, 2]),
    ])
    cot_block = cotangent[0, 0]
    dy = jnp.where(present > 0, cot_block, jnp.zeros_like(cot_block))
    dattn = dot(dy, proj_out, NT).astype(bf16)
    normed_side = to_sibling(normed)
    dy_mine, dy_side = swapped(
        jnp.concatenate([dy[:, :half], dy[:, inner:inner + half]], axis=1),
        jnp.concatenate([dy[:, half:inner], dy[:, inner + half:]], axis=1),
    )

    outs, dqs, dkvs, lates = ([], [], [], [])
    for g in range(GROUPS):
        own_col, other_col = rows_near[g]
        if g == GROUPS - 1 and g >= 2:
            own_col, other_col, _ = lax.optimization_barrier((own_col, other_col, outs[g - 2]))
        near = (own_col, to_sibling(own_col), move(other_col, THIRD_COL))
        out, dq, down, dside, dthird = attend(allowed, queries, dattn, *near, g)
        side = to_sibling(dside)
        third = move(dthird, THIRD_COL, back=True)
        column = down.astype(f32) + side.astype(f32)
        beyond = move(jnp.stack([column[2].astype(bf16), third[2]]), BEYOND_ROW, back=True)
        beyond = beyond.astype(f32)
        row = move((column[1] + beyond[0]).astype(bf16), OTHER_ROW)
        both = move((third[1].astype(f32) + beyond[1]).astype(bf16), OTHER_BOTH)
        col = move(third[0], OTHER_COL)
        total = column[0] + row.astype(f32) + both.astype(f32) + col.astype(f32)
        total = total.astype(bf16)
        outs.append(out)
        dqs.append(dq)
        dkvs.append(total)
        lates.append(late_grads(normed, normed_side, *swapped(total[0], total[1])))

    attn = jnp.concatenate(outs, axis=1)
    dq = jnp.concatenate(dqs, axis=1)
    branch = dot(attn, proj_out)
    branch = jnp.where(present > 0, branch, jnp.zeros_like(branch)).astype(bf16)
    early = early_grads(
        normed, normed_side, *swapped(dq[:, :half], dq[:, half:]), attn, to_sibling(attn), dy_mine, dy_side
    )
    early = summed(early)
    blocks = half // 128
    share_q = unpacked(early[:blocks * SPAN])
    share_out = unpacked(early[blocks * SPAN:])

    dnormed = dot(dq, proj_in[:, :inner], NT)
    for g, total in enumerate(dkvs):
        lo = inner + g * size
        dnormed = dnormed + (
            dot(total[0], proj_in[:, lo:lo + size], NT)
            + dot(total[1], proj_in[:, inner + lo:inner + lo + size], NT)
        )
    gain_gradient = jnp.sum(dnormed * xhat, axis=0)
    gain_part = gain_gradient.astype(bf16).reshape(N_CHIP, 1, SPAN)
    gain_part = jnp.pad(gain_part, ((0, 0), (0, 7), (0, 128 - SPAN)))
    late = jnp.concatenate([part.reshape(N_CHIP, -1, 128) for part in lates] + [gain_part], axis=1)
    late = lax.all_to_all(late, CHIPS, 0, 0, tiled=True)

    centred = dnormed * layer_norm_gain
    input_gradient = inverse_deviation * (
        centred
        - jnp.mean(centred, axis=-1, keepdims=True)
        - xhat * jnp.mean(centred * xhat, axis=-1, keepdims=True)
    )
    branch_grad = input_gradient.astype(bf16)

    def own_rows(value):
        rows = value.shape[0] // 2
        mine, other = swapped(value[:rows], value[rows:])
        return [jnp.where(is_low, mine, other), jnp.where(is_low, other, mine)]

    rows = share_out.shape[0] // 4
    moved = lax.all_to_all(share_out.reshape(4, rows, half), ("zl", "core"), 0, 0, tiled=True)
    full_out = moved.transpose(1, 0, 2).reshape(rows, 4 * half)
    full_q = own_rows(share_q)
    early_sq = square_sum(share_q) + square_sum(share_out)
    late, branch, branch_grad, full_out, early_sq, *full_q = lax.optimization_barrier(
        (late, branch, branch_grad, full_out, early_sq, *full_q)
    )
    late = jnp.sum(late.astype(f32), axis=0)
    share_kv = unpacked(late[:2 * blocks * SPAN])
    share_gain = late[2 * blocks * SPAN, :SPAN]
    share_gain = share_gain + to_sibling(share_gain)

    total_sq = early_sq + square_sum(share_kv) + 0.5 * square_sum(share_gain)
    total_sq = jnp.full((8, 128), total_sq, f32)
    for bit in range(7):
        total_sq = total_sq + lax.ppermute(total_sq, AXES, [(i, i ^ (1 << bit)) for i in range(ROWS * COLS)])
    total_sq = total_sq[0, 0]
    count = width * 3 * inner + inner * width + width
    factor = 1.0 / jnp.maximum(jnp.sqrt(total_sq / count), 1.0)

    full_in = jnp.concatenate(full_q + own_rows(share_kv), axis=1)
    rows = SPAN // 2
    gain_own = jnp.where(is_low, share_gain[:rows], share_gain[rows:])
    return (
        branch[None, None],
        branch_grad[None, None],
        factor * full_in,
        factor * full_out,
        factor * gain_own,
    )


def solution(mesh):
    fine = Mesh(mesh.devices.reshape(SIZES), AXES)
    row, col = (("x", "zh"), ("y", "zl", "core"))
    in_specs = (
        P(row, col, None, None),
        P(),
        P(),
        P(),
        P(),
        P(row, col),
        P(row, col, None, None),
    )
    out_specs = (
        P(row, col, None, None),
        P(row, col, None, None),
        P(AXES, None),
        P(AXES, None),
        P(AXES),
    )
    return jax.shard_map(local, mesh=fine, in_specs=in_specs, out_specs=out_specs, check_vma=False)
```

```python
import jax
import jax.numpy as jnp
from jax import lax
from jax.experimental import pallas as pl
from jax.experimental.pallas import tpu as pltpu
from jax.sharding import Mesh
from jax.sharding import PartitionSpec as P

HEAD_DIM = 64
REGION = 3
RADIUS = 3
EPSILON = 1e-05
NEG_BIG = -1e30
GROUPS = 3

AXES = ("x", "zh", "y", "zl", "core")
CHIPS = ("x", "zh", "y", "zl")
SIZES = (4, 2, 4, 2, 2)
ROWS, COLS = 8, 16
N_CHIP = 64
SPAN = 24

NN = (((1,), (0,)), ((), ()))
NT = (((1,), (1,)), ((), ()))
TN = (((0,), (0,)), ((), ()))
f32 = jnp.float32
bf16 = jnp.bfloat16


def dot(a, b, dims=NN):
    return lax.dot_general(a, b, dims, preferred_element_type=f32)


def routes(move):
    index = lambda p: (((p[0] * 2 + p[1]) * 4 + p[2]) * 2 + p[3]) * 2 + p[4]
    places = [(x, zh, y, zl, c) for x in range(4) for zh in range(2)
              for y in range(4) for zl in range(2) for c in range(2)]
    pairs = [(p, move(*p)) for p in places]
    return [(index(p), index(t)) for p, t in pairs if 0 <= t[0] < 4 and 0 <= t[2] < 4]


def third_column(x, zh, y, zl, c):
    if c == zl:
        return (x, zh, y, zl, 1 - c)
    return (x, zh, y + 1 - 2 * zl, zl, 1 - c)


OTHER_ROW = routes(lambda x, zh, y, zl, c: (x, 1 - zh, y, zl, c))
OTHER_COL = routes(lambda x, zh, y, zl, c: (x, zh, y, 1 - zl, c))
OTHER_BOTH = routes(lambda x, zh, y, zl, c: (x, 1 - zh, y, 1 - zl, c))
BEYOND_ROW = routes(lambda x, zh, y, zl, c: (x + 1 - 2 * zh, zh, y, zl, c))
THIRD_COL = routes(third_column)


def after(value, *others):
    return lax.optimization_barrier((value,) + others)[0]


def move(value, route, back=False):
    return lax.ppermute(value, AXES, [(t, f) for f, t in route] if back else route)


def to_sibling(value):
    return lax.ppermute(value, "core", [(0, 1), (1, 0)])


def apply_layer_norm(block):
    values = block.astype(f32)
    centred = values - jnp.mean(values, axis=-1, keepdims=True)
    inverse_deviation = lax.rsqrt(jnp.mean(centred * centred, axis=-1, keepdims=True) + EPSILON)
    return (centred * inverse_deviation, inverse_deviation)


def geometry(tissue, row_at, col_at, slot):
    padded = jnp.pad(tissue, REGION)
    window = lax.dynamic_slice(padded, (row_at * REGION, col_at * REGION), (3 * REGION, 3 * REGION))
    blocks = window.reshape(3, REGION, 3, REGION)
    occupied = jnp.sum(blocks, axis=(1, 3))
    inner = jnp.arange(REGION, dtype=jnp.int32)
    row_in = jnp.sum(blocks * inner[None, :, None, None], axis=(1, 3))
    col_in = jnp.sum(blocks * inner[None, None, None, :], axis=(1, 3))
    three = jnp.arange(3, dtype=jnp.int32)
    key_row = (row_at - 1 + three)[:, None] * REGION + row_in
    key_col = (col_at - 1 + three)[None, :] * REGION + col_in
    query_row = row_at * REGION + slot // REGION
    query_col = col_at * REGION + slot % REGION
    present = lax.dynamic_slice(tissue, (query_row, query_col), (1, 1))[0, 0]
    inside = (
        (jnp.abs(key_row - query_row) <= RADIUS)
        & (jnp.abs(key_col - query_col) <= RADIUS)
        & (occupied > 0)
    )
    centre = (three[:, None] == 1) & (three[None, :] == 1)
    return ((inside | centre).astype(jnp.int32), present)


def attend_kernel(allow_ref, q_ref, g_ref, own_ref, side_ref, third_ref,
                  out_ref, dq_ref, down_ref, dside_ref, dthird_ref, s_scr, dp_scr):
    tile_len = q_ref.shape[0]
    kv_refs = (own_ref, side_ref, third_ref)
    dkv_refs = (down_ref, dside_ref, dthird_ref)
    places = [(a, b) for b in range(3) for a in range(3)]
    first = lax.broadcasted_iota(jnp.int32, (tile_len, 2 * HEAD_DIM), 1) < HEAD_DIM

    def head_pair(v):
        zero = jnp.zeros_like(v)
        return jnp.concatenate([jnp.where(first, v, zero), jnp.where(first, zero, v)], axis=0)

    qq = head_pair(q_ref[...] * jnp.asarray(HEAD_DIM ** -0.5, bf16))
    gg = head_pair(g_ref[...])
    top = jnp.full((1, 2 * tile_len), NEG_BIG, f32)
    for i, (a, b) in enumerate(places):
        scores = dot(kv_refs[b][a, 0], qq, NT)
        scores = jnp.where(allow_ref[b * 3 + a] > 0, scores, NEG_BIG)
        s_scr[i] = scores
        top = jnp.maximum(top, jnp.max(scores, axis=0, keepdims=True))
    total = jnp.zeros((1, 2 * tile_len), f32)
    mix = jnp.zeros((1, 2 * tile_len), f32)
    for i, (a, b) in enumerate(places):
        weights = jnp.exp(s_scr[i] - top)
        dprobs = dot(kv_refs[b][a, 1], gg, NT)
        total = total + jnp.sum(weights, axis=0, keepdims=True)
        mix = mix + jnp.sum(dprobs * weights, axis=0, keepdims=True)
        s_scr[i] = weights
        dp_scr[i] = dprobs
    inverse = 1.0 / total
    mix = mix * inverse
    outs = [jnp.zeros((HEAD_DIM, tile_len), f32)] * 2
    dqs = [jnp.zeros((HEAD_DIM, tile_len), f32)] * 2
    for i, (a, b) in enumerate(places):
        probs = s_scr[i] * inverse
        probs_b = probs.astype(bf16)
        dscores = (probs * (dp_scr[i] - mix)).astype(bf16)
        dkv_refs[b][a, 1] = dot(probs_b, gg).astype(bf16)
        dkv_refs[b][a, 0] = dot(dscores, qq).astype(bf16)
        keys_t = kv_refs[b][a, 0].T
        vals_t = kv_refs[b][a, 1].T
        for h in range(2):
            part = slice(h * HEAD_DIM, (h + 1) * HEAD_DIM)
            lanes = slice(h * tile_len, (h + 1) * tile_len)
            outs[h] = outs[h] + dot(vals_t[part], probs_b[:, lanes])
            dqs[h] = dqs[h] + dot(keys_t[part], dscores[:, lanes])
    out_ref[...] = jnp.concatenate(outs, axis=0).T.astype(bf16)
    dq_ref[...] = (jnp.concatenate(dqs, axis=0).T * HEAD_DIM ** -0.5).astype(bf16)


def attend(allowed, qkv, dattn, own, side, third, group):
    tile_len, width = (own.shape[2], own.shape[3])
    block = 2 * HEAD_DIM
    steps = width // block
    place = lambda h: (0, h + group * steps)
    near = lambda h: (0, 0, 0, h)
    kv_spec = pl.BlockSpec((3, 2, tile_len, block), near)
    row_spec = pl.BlockSpec((tile_len, block), lambda h: (0, h))
    row_shape = jax.ShapeDtypeStruct((tile_len, width), bf16)
    kv_shape = jax.ShapeDtypeStruct(own.shape, bf16)
    scratch = pltpu.VMEM((9, tile_len, 2 * tile_len), f32)
    return pl.pallas_call(
        attend_kernel,
        grid=(steps,),
        in_specs=[
            pl.BlockSpec(memory_space=pltpu.SMEM),
            pl.BlockSpec((tile_len, block), place),
            pl.BlockSpec((tile_len, block), place),
            kv_spec, kv_spec, kv_spec,
        ],
        out_specs=[row_spec, row_spec, kv_spec, kv_spec, kv_spec],
        out_shape=[row_shape, row_shape, kv_shape, kv_shape, kv_shape],
        scratch_shapes=[scratch, scratch],
        compiler_params=pltpu.CompilerParams(vmem_limit_bytes=40 * 1024 * 1024),
        cost_estimate=pl.CostEstimate(
            flops=width * tile_len * tile_len * 9 * 12 * 4,
            bytes_accessed=width * tile_len * 2 * 40,
            transcendentals=width // HEAD_DIM * tile_len * tile_len * 9,
        ),
    )(allowed, qkv, dattn, own, side, third)


def grad_blocks(left_a, left_b, right_a, right_b, first, last):
    lanes = slice(first, last)
    grad = dot(left_a[:, lanes], right_a[...], TN) + dot(left_b[:, lanes], right_b[...], TN)
    return grad.astype(bf16)


def early_kernel(normed_a, normed_b, dq_a, dq_b, attn_a, attn_b, dy_a, dy_b, out_ref):
    step = 16 * SPAN
    blocks = dq_a.shape[1] // 128
    for r in range(normed_a.shape[1] // step):
        grad = grad_blocks(normed_a, normed_b, dq_a, dq_b, r * step, (r + 1) * step)
        for j in range(blocks):
            part = grad[:, j * 128:(j + 1) * 128].reshape(16, SPAN, 128)
            out_ref[r * 16:(r + 1) * 16, j] = part
    for r in range(attn_a.shape[1] // step):
        grad = grad_blocks(attn_a, attn_b, dy_a, dy_b, r * step, (r + 1) * step)
        for i in range(16):
            for q in range(2):
                for j in range(blocks):
                    col = (q * blocks + j) * 128
                    out_ref[2 * (r * 16 + i) + q, blocks + j] = grad[i * SPAN:(i + 1) * SPAN, col:col + 128]


def early_grads(*operands):
    blocks = operands[2].shape[1] // 128
    return pl.pallas_call(
        early_kernel,
        out_shape=jax.ShapeDtypeStruct((N_CHIP, 2 * blocks, SPAN, 128), bf16),
        compiler_params=pltpu.CompilerParams(vmem_limit_bytes=32 * 1024 * 1024),
    )(*operands)


def late_kernel(normed_a, normed_b, *refs):
    step = 16 * SPAN
    out_ref = refs[-1]
    for g in range(len(refs) // 2):
        dkv_a, dkv_b = refs[2 * g:2 * g + 2]
        blocks = dkv_a.shape[1] // 128
        for r in range(normed_a.shape[1] // step):
            grad = grad_blocks(normed_a, normed_b, dkv_a, dkv_b, r * step, (r + 1) * step)
            for j in range(blocks):
                part = grad[:, j * 128:(j + 1) * 128].reshape(16, SPAN, 128)
                out_ref[r * 16:(r + 1) * 16, g * blocks + j] = part


def late_grads(*operands):
    blocks = sum(d.shape[1] for d in operands[2::2]) // 128
    return pl.pallas_call(
        late_kernel,
        out_shape=jax.ShapeDtypeStruct((N_CHIP, blocks, SPAN, 128), bf16),
        compiler_params=pltpu.CompilerParams(vmem_limit_bytes=32 * 1024 * 1024),
    )(*operands)


def exchanged(value):
    return lax.all_to_all(value.reshape(N_CHIP, -1, 128), CHIPS, 0, 0, tiled=True)


def butterfly(value):
    for bit in range(7):
        value = value + lax.ppermute(value, AXES, [(i, i ^ (1 << bit)) for i in range(ROWS * COLS)])
    return value


def unpacked(share):
    count = share.shape[0] // SPAN
    return share.reshape(count, SPAN, 128).transpose(1, 0, 2).reshape(SPAN, count * 128)


def square_sum(value):
    return jnp.sum(value * value)


def local(tokens, layer_norm_gain, proj_in, proj_out, tissue, tile_slot, cotangent):
    chip_at = lax.axis_index(CHIPS)
    core = lax.axis_index("core")
    zh = lax.axis_index("zh")
    row_at = chip_at // (COLS // 2)
    col_at = (chip_at % (COLS // 2)) * 2 + core
    tile_len, width = tokens.shape[2:]
    inner = proj_out.shape[0]
    half = inner // 2
    is_low = core == 0

    def swapped(lower, upper):
        mine, other = (jnp.where(is_low, lower, upper), jnp.where(is_low, upper, lower))
        return (mine, to_sibling(other))

    xhat, inverse_deviation = apply_layer_norm(tokens[0, 0])
    normed = (xhat * layer_norm_gain).astype(bf16)
    size = inner // GROUPS
    qkv = dot(normed, proj_in).astype(bf16)

    def gather_block(g, *others):
        lo = inner + g * size
        own = jnp.stack([qkv[:, lo:lo + size], qkv[:, inner + lo:inner + lo + size]])
        if others:
            own = after(own, *others)
        return (own, move(own, OTHER_ROW), move(own, OTHER_COL), move(own, OTHER_BOTH))

    stages = []
    for g in range(GROUPS):
        others = []
        if g >= 1:
            others += stages[g - 1]["block"][1:]
        if g >= 2:
            others.append(stages[g - 2]["beyond"])
        own, row, col, both = gather_block(g, *others)
        outer = jnp.stack([row, both])
        beyond = move(outer, BEYOND_ROW)
        stages.append(dict(block=(own, row, col, both), outer=outer, beyond=beyond,
                           own_col=jnp.stack([own, row, beyond[0]]),
                           other_col=jnp.stack([col, both, beyond[1]])))

    allowed, present = geometry(tissue, row_at, col_at, tile_slot[0, 0])
    first_row = zh == 0
    allowed = jnp.stack([
        allowed[1],
        jnp.where(first_row, allowed[2], allowed[0]),
        jnp.where(first_row, allowed[0], allowed[2]),
    ])
    allowed = jnp.concatenate([
        allowed[:, 1],
        jnp.where(is_low, allowed[:, 2], allowed[:, 0]),
        jnp.where(is_low, allowed[:, 0], allowed[:, 2]),
    ])
    cot_block = cotangent[0, 0]
    dy = jnp.where(present > 0, cot_block, jnp.zeros_like(cot_block))
    dattn = dot(dy, proj_out, NT).astype(bf16)
    outs, dqs, backs, early = ([], [], [], [])
    for g in range(GROUPS):
        own_col, other_col = (stages[g]["own_col"], stages[g]["other_col"])
        side_col, third_col = (to_sibling(own_col), move(other_col, THIRD_COL))
        first = []
        if g + 2 < GROUPS:
            first.append(stages[g + 2]["outer"])
        if g + 1 < GROUPS:
            first += [stages[g + 1]["own_col"], stages[g + 1]["other_col"]]
        if g >= 2:
            first.append(backs[g - 2][3])
        if g == GROUPS - 1:
            first += early
        own_col, side_col, third_col = lax.optimization_barrier((own_col, side_col, third_col, *first))[:3]
        out, dq, down, dside, dthird = attend(allowed, qkv, dattn, own_col, side_col, third_col, g)
        if g == 0:
            normed_side = to_sibling(after(normed, out))
            dy_mine, dy_side = swapped(
                jnp.concatenate([dy[:, :half], dy[:, inner:inner + half]], axis=1),
                after(jnp.concatenate([dy[:, half:inner], dy[:, inner + half:]], axis=1), out),
            )
            early += [normed_side, dy_side]
        side = to_sibling(dside)
        third = move(dthird, THIRD_COL, back=True)
        column = down.astype(f32) + side.astype(f32)
        outer = jnp.stack([column[2].astype(bf16), third[2]])
        outs.append(out)
        dqs.append(dq)
        backs.append((column, third, down, outer))
    dkvs = []
    for column, third, _, outer in backs:
        beyond = move(outer, BEYOND_ROW, back=True).astype(f32)
        row = move((column[1] + beyond[0]).astype(bf16), OTHER_ROW)
        both = move((third[1].astype(f32) + beyond[1]).astype(bf16), OTHER_BOTH)
        col = move(third[0], OTHER_COL)
        total = column[0] + row.astype(f32) + both.astype(f32) + col.astype(f32)
        dkvs.append(total.astype(bf16))

    attn = jnp.concatenate(outs, axis=1)
    dq = jnp.concatenate(dqs, axis=1)
    branch = dot(attn, proj_out)
    branch = jnp.where(present > 0, branch, jnp.zeros_like(branch)).astype(bf16)
    early = early_grads(
        normed, normed_side, *swapped(dq[:, :half], dq[:, half:]), attn, to_sibling(attn), dy_mine, dy_side
    )
    if GROUPS > 1:
        early = after(early, backs[GROUPS - 2][3])
    early = exchanged(early)
    blocks = half // 128
    pairs = [part for total in dkvs for part in swapped(total[0], total[1])]
    late = late_grads(normed, normed_side, *pairs)
    early = after(early, late)
    early = jnp.sum(early.astype(f32), axis=0)
    share_q = unpacked(early[:blocks * SPAN])
    share_out = unpacked(early[blocks * SPAN:])
    dnormed = dot(dq, proj_in[:, :inner], NT)
    for g, total in enumerate(lax.optimization_barrier((*dkvs, late))[:GROUPS]):
        lo = inner + g * size
        dnormed = dnormed + (
            dot(total[0], proj_in[:, lo:lo + size], NT)
            + dot(total[1], proj_in[:, inner + lo:inner + lo + size], NT)
        )
    gain_gradient = jnp.sum(dnormed * xhat, axis=0)
    late = exchanged(late)


    centred = dnormed * layer_norm_gain
    input_gradient = inverse_deviation * (
        centred
        - jnp.mean(centred, axis=-1, keepdims=True)
        - xhat * jnp.mean(centred * xhat, axis=-1, keepdims=True)
    )
    branch_grad = input_gradient.astype(bf16)

    def own_rows(value):
        rows = value.shape[0] // 2
        mine, other = swapped(value[:rows], value[rows:])
        return [jnp.where(is_low, mine, other), jnp.where(is_low, other, mine)]

    rows = share_out.shape[0] // 4
    low_z = lax.axis_index("zl") == 0
    parts = share_out.reshape(2, 2, rows, half)
    mine, other = swapped(parts[:, 0], parts[:, 1])
    parts = jnp.stack([jnp.where(is_low, mine, other), jnp.where(is_low, other, mine)], axis=1)
    mine, other = (jnp.where(low_z, parts[0], parts[1]), jnp.where(low_z, parts[1], parts[0]))
    other = lax.ppermute(other, "zl", [(0, 1), (1, 0)])
    moved = jnp.stack([jnp.where(low_z, mine, other), jnp.where(low_z, other, mine)])
    full_out = moved.transpose(2, 0, 1, 3).reshape(rows, 4 * half)
    full_q = own_rows(share_q)
    early_sq = square_sum(share_q) + square_sum(share_out)
    late, branch, branch_grad, full_out, early_sq, gain_gradient, *full_q = lax.optimization_barrier(
        (late, branch, branch_grad, full_out, early_sq, gain_gradient, *full_q)
    )
    late = jnp.sum(late.astype(f32), axis=0)
    share_kv = unpacked(late)
    rows = width // 128
    summands = jnp.full((16 - rows, 128), early_sq + square_sum(share_kv), f32)
    summands = butterfly(jnp.concatenate([gain_gradient.reshape(rows, 128), summands], axis=0))
    gain = summands[:rows].reshape(-1)
    total_sq = summands[rows, 0] + square_sum(gain)
    count = width * 3 * inner + inner * width + width
    factor = 1.0 / jnp.maximum(jnp.sqrt(total_sq / count), 1.0)

    full_in = jnp.concatenate(full_q + own_rows(share_kv), axis=1)
    rows = SPAN // 2
    gain_own = lax.dynamic_slice(gain, ((chip_at * 2 + core) * rows,), (rows,))
    return (
        branch[None, None],
        branch_grad[None, None],
        factor * full_in,
        factor * full_out,
        factor * gain_own,
    )


def solution(mesh):
    fine = Mesh(mesh.devices.reshape(SIZES), AXES)
    row, col = (("x", "zh"), ("y", "zl", "core"))
    in_specs = (
        P(row, col, None, None),
        P(),
        P(),
        P(),
        P(),
        P(row, col),
        P(row, col, None, None),
    )
    out_specs = (
        P(row, col, None, None),
        P(row, col, None, None),
        P(AXES, None),
        P(AXES, None),
        P(AXES),
    )
    return jax.shard_map(local, mesh=fine, in_specs=in_specs, out_specs=out_specs, check_vma=False)
```

```python
import jax
import jax.numpy as jnp
from jax import lax
from jax.experimental import pallas as pl
from jax.experimental.pallas import tpu as pltpu
from jax.sharding import Mesh
from jax.sharding import PartitionSpec as P

HEAD_DIM = 64
REGION = 3
RADIUS = 3
EPSILON = 1e-05
NEG_BIG = -1e30
GROUPS = 3

AXES = ("x", "zh", "y", "zl", "core")
CHIPS = ("x", "zh", "y", "zl")
SIZES = (4, 2, 4, 2, 2)
ROWS, COLS = 8, 16
GROUP = ("zl", "core")
PAIRS = ("x", "zh", "y")
N_PAIR = 32
SPAN = 24

NN = (((1,), (0,)), ((), ()))
NT = (((1,), (1,)), ((), ()))
TN = (((0,), (0,)), ((), ()))
f32 = jnp.float32
bf16 = jnp.bfloat16


def dot(a, b, dims=NN):
    return lax.dot_general(a, b, dims, preferred_element_type=f32)


def routes(move):
    index = lambda p: (((p[0] * 2 + p[1]) * 4 + p[2]) * 2 + p[3]) * 2 + p[4]
    places = [(x, zh, y, zl, c) for x in range(4) for zh in range(2)
              for y in range(4) for zl in range(2) for c in range(2)]
    pairs = [(p, move(*p)) for p in places]
    return [(index(p), index(t)) for p, t in pairs if 0 <= t[0] < 4 and 0 <= t[2] < 4]


def third_column(x, zh, y, zl, c):
    if c == zl:
        return (x, zh, y, zl, 1 - c)
    return (x, zh, y + 1 - 2 * zl, zl, 1 - c)


OTHER_ROW = routes(lambda x, zh, y, zl, c: (x, 1 - zh, y, zl, c))
OTHER_COL = routes(lambda x, zh, y, zl, c: (x, zh, y, 1 - zl, c))
OTHER_BOTH = routes(lambda x, zh, y, zl, c: (x, 1 - zh, y, 1 - zl, c))
BEYOND_ROW = routes(lambda x, zh, y, zl, c: (x + 1 - 2 * zh, zh, y, zl, c))
THIRD_COL = routes(third_column)


def after(value, *others):
    return lax.optimization_barrier((value,) + others)[0]


def move(value, route, back=False):
    return lax.ppermute(value, AXES, [(t, f) for f, t in route] if back else route)


def to_sibling(value):
    return lax.ppermute(value, "core", [(0, 1), (1, 0)])


def to_pair(value):
    return lax.ppermute(value, "zl", [(0, 1), (1, 0)])


def apply_layer_norm(block):
    values = block.astype(f32)
    centred = values - jnp.mean(values, axis=-1, keepdims=True)
    inverse_deviation = lax.rsqrt(jnp.mean(centred * centred, axis=-1, keepdims=True) + EPSILON)
    return (centred * inverse_deviation, inverse_deviation)


def geometry(tissue, row_at, col_at, slot):
    padded = jnp.pad(tissue, REGION)
    window = lax.dynamic_slice(padded, (row_at * REGION, col_at * REGION), (3 * REGION, 3 * REGION))
    blocks = window.reshape(3, REGION, 3, REGION)
    occupied = jnp.sum(blocks, axis=(1, 3))
    inner = jnp.arange(REGION, dtype=jnp.int32)
    row_in = jnp.sum(blocks * inner[None, :, None, None], axis=(1, 3))
    col_in = jnp.sum(blocks * inner[None, None, None, :], axis=(1, 3))
    three = jnp.arange(3, dtype=jnp.int32)
    key_row = (row_at - 1 + three)[:, None] * REGION + row_in
    key_col = (col_at - 1 + three)[None, :] * REGION + col_in
    query_row = row_at * REGION + slot // REGION
    query_col = col_at * REGION + slot % REGION
    present = lax.dynamic_slice(tissue, (query_row, query_col), (1, 1))[0, 0]
    inside = (
        (jnp.abs(key_row - query_row) <= RADIUS)
        & (jnp.abs(key_col - query_col) <= RADIUS)
        & (occupied > 0)
    )
    centre = (three[:, None] == 1) & (three[None, :] == 1)
    return ((inside | centre).astype(jnp.int32), present)


def attend_kernel(allow_ref, q_ref, g_ref, own_ref, side_ref, third_ref,
                  out_ref, dq_ref, down_ref, dside_ref, dthird_ref, s_scr, dp_scr):
    tile_len = q_ref.shape[0]
    kv_refs = (own_ref, side_ref, third_ref)
    dkv_refs = (down_ref, dside_ref, dthird_ref)
    places = [(a, b) for b in range(3) for a in range(3)]
    first = lax.broadcasted_iota(jnp.int32, (tile_len, 2 * HEAD_DIM), 1) < HEAD_DIM

    def head_pair(v):
        zero = jnp.zeros_like(v)
        return jnp.concatenate([jnp.where(first, v, zero), jnp.where(first, zero, v)], axis=0)

    qq = head_pair(q_ref[...] * jnp.asarray(HEAD_DIM ** -0.5, bf16))
    gg = head_pair(g_ref[...])
    top = jnp.full((1, 2 * tile_len), NEG_BIG, f32)
    for i, (a, b) in enumerate(places):
        scores = dot(kv_refs[b][a, 0], qq, NT)
        scores = jnp.where(allow_ref[b * 3 + a] > 0, scores, NEG_BIG)
        s_scr[i] = scores
        top = jnp.maximum(top, jnp.max(scores, axis=0, keepdims=True))
    total = jnp.zeros((1, 2 * tile_len), f32)
    mix = jnp.zeros((1, 2 * tile_len), f32)
    for i, (a, b) in enumerate(places):
        weights = jnp.exp(s_scr[i] - top)
        dprobs = dot(kv_refs[b][a, 1], gg, NT)
        total = total + jnp.sum(weights, axis=0, keepdims=True)
        mix = mix + jnp.sum(dprobs * weights, axis=0, keepdims=True)
        s_scr[i] = weights
        dp_scr[i] = dprobs
    inverse = 1.0 / total
    mix = mix * inverse
    outs = [jnp.zeros((HEAD_DIM, tile_len), f32)] * 2
    dqs = [jnp.zeros((HEAD_DIM, tile_len), f32)] * 2
    for i, (a, b) in enumerate(places):
        probs = s_scr[i] * inverse
        probs_b = probs.astype(bf16)
        dscores = (probs * (dp_scr[i] - mix)).astype(bf16)
        dkv_refs[b][a, 1] = dot(probs_b, gg).astype(bf16)
        dkv_refs[b][a, 0] = dot(dscores, qq).astype(bf16)
        keys_t = kv_refs[b][a, 0].T
        vals_t = kv_refs[b][a, 1].T
        for h in range(2):
            part = slice(h * HEAD_DIM, (h + 1) * HEAD_DIM)
            lanes = slice(h * tile_len, (h + 1) * tile_len)
            outs[h] = outs[h] + dot(vals_t[part], probs_b[:, lanes])
            dqs[h] = dqs[h] + dot(keys_t[part], dscores[:, lanes])
    out_ref[...] = jnp.concatenate(outs, axis=0).T.astype(bf16)
    dq_ref[...] = (jnp.concatenate(dqs, axis=0).T * HEAD_DIM ** -0.5).astype(bf16)


def attend(allowed, qkv, dattn, own, side, third, group):
    tile_len, width = (own.shape[2], own.shape[3])
    block = 2 * HEAD_DIM
    steps = width // block
    place = lambda h: (0, h + group * steps)
    near = lambda h: (0, 0, 0, h)
    kv_spec = pl.BlockSpec((3, 2, tile_len, block), near)
    row_spec = pl.BlockSpec((tile_len, block), lambda h: (0, h))
    row_shape = jax.ShapeDtypeStruct((tile_len, width), bf16)
    kv_shape = jax.ShapeDtypeStruct(own.shape, bf16)
    scratch = pltpu.VMEM((9, tile_len, 2 * tile_len), f32)
    return pl.pallas_call(
        attend_kernel,
        grid=(steps,),
        in_specs=[
            pl.BlockSpec(memory_space=pltpu.SMEM),
            pl.BlockSpec((tile_len, block), place),
            pl.BlockSpec((tile_len, block), place),
            kv_spec, kv_spec, kv_spec,
        ],
        out_specs=[row_spec, row_spec, kv_spec, kv_spec, kv_spec],
        out_shape=[row_shape, row_shape, kv_shape, kv_shape, kv_shape],
        scratch_shapes=[scratch, scratch],
        compiler_params=pltpu.CompilerParams(vmem_limit_bytes=40 * 1024 * 1024),
        cost_estimate=pl.CostEstimate(
            flops=width * tile_len * tile_len * 9 * 12 * 4,
            bytes_accessed=width * tile_len * 2 * 40,
            transcendentals=width // HEAD_DIM * tile_len * tile_len * 9,
        ),
    )(allowed, qkv, dattn, own, side, third)


def grad_blocks(left, right, places, first, last):
    lanes = slice(first, last)
    grad = dot(left[places[0], :, lanes], right[0], TN)
    for slot in range(1, 4):
        grad = grad + dot(left[places[slot], :, lanes], right[slot], TN)
    return grad.astype(bf16)


def early_kernel(place_ref, normed, dq, attn, dy, out_ref):
    step = 16 * SPAN
    blocks = dq.shape[2] // 128
    upper = place_ref[4] > 0
    places = [place_ref[slot] for slot in range(4)]
    for r in range(normed.shape[2] // step):
        grad = grad_blocks(normed, dq, range(4), r * step, (r + 1) * step)
        grad = grad.reshape(8, 2, SPAN, step)
        grad = jnp.where(upper, grad[:, 1], grad[:, 0])
        for j in range(blocks):
            out_ref[r * 8:(r + 1) * 8, j] = grad[:, :, j * 128:(j + 1) * 128]
    for r in range(attn.shape[2] // step):
        grad = grad_blocks(attn, dy, places, r * step, (r + 1) * step)
        grad = grad.reshape(16, SPAN, step)
        for j in range(blocks):
            out_ref[r * 16:(r + 1) * 16, blocks + j] = grad[:, :, j * 128:(j + 1) * 128]


def late_kernel(place_ref, normed, dkv, early, out_ref):
    step = 16 * SPAN
    blocks = dkv.shape[2] // 128
    places = [place_ref[slot] for slot in range(4)]
    out_ref[:, :2 * blocks] = early[...]
    for r in range(normed.shape[2] // step):
        grad = grad_blocks(normed, dkv, places, r * step, (r + 1) * step)
        grad = grad.reshape(8, 2, SPAN, step)
        for half in range(2):
            for j in range(blocks):
                out_ref[r * 8:(r + 1) * 8, (2 + half) * blocks + j] = grad[:, half, :, j * 128:(j + 1) * 128]


def grads(kernel, blocks, places, *operands):
    vmem = pl.BlockSpec(memory_space=pltpu.VMEM)
    return pl.pallas_call(
        kernel,
        in_specs=[pl.BlockSpec(memory_space=pltpu.SMEM)] + [vmem] * len(operands),
        out_specs=vmem,
        out_shape=jax.ShapeDtypeStruct((N_PAIR, blocks, SPAN, 128), bf16),
        compiler_params=pltpu.CompilerParams(vmem_limit_bytes=32 * 1024 * 1024),
        cost_estimate=pl.CostEstimate(flops=1000000, bytes_accessed=1000000, transcendentals=0),
    )(places, *operands)


def butterfly(value):
    for bit in range(7):
        value = value + lax.ppermute(value, AXES, [(i, i ^ (1 << bit)) for i in range(ROWS * COLS)])
    return value


def unpacked(share):
    count = share.shape[0] // SPAN
    return share.reshape(count, SPAN, 128).transpose(1, 0, 2).reshape(SPAN, count * 128)


def square_sum(value):
    return jnp.sum(value * value)


def local(tokens, layer_norm_gain, proj_in, proj_out, tissue, tile_slot, cotangent):
    chip_at = lax.axis_index(CHIPS)
    core = lax.axis_index("core")
    zh = lax.axis_index("zh")
    row_at = chip_at // (COLS // 2)
    col_at = (chip_at % (COLS // 2)) * 2 + core
    tile_len, width = tokens.shape[2:]
    inner = proj_out.shape[0]
    half = inner // 2
    is_low = core == 0

    def swapped(lower, upper):
        mine, other = (jnp.where(is_low, lower, upper), jnp.where(is_low, upper, lower))
        return (mine, to_sibling(other))

    xhat, inverse_deviation = apply_layer_norm(tokens[0, 0])
    normed = (xhat * layer_norm_gain).astype(bf16)
    size = inner // GROUPS
    qkv = dot(normed, proj_in).astype(bf16)

    def gather_block(g, *others):
        lo = inner + g * size
        own = jnp.stack([qkv[:, lo:lo + size], qkv[:, inner + lo:inner + lo + size]])
        if others:
            own = after(own, *others)
        return (own, move(own, OTHER_ROW), move(own, OTHER_COL), move(own, OTHER_BOTH))

    stages = []
    for g in range(GROUPS):
        others = []
        if g >= 1:
            others += stages[g - 1]["block"][1:]
        if g >= 2:
            others.append(stages[g - 2]["beyond"])
        own, row, col, both = gather_block(g, *others)
        outer = jnp.stack([row, both])
        if g >= 1:
            outer = after(outer, stages[g - 1]["own_col"], stages[g - 1]["other_col"])
        beyond = move(outer, BEYOND_ROW)
        stages.append(dict(block=(own, row, col, both), outer=outer, beyond=beyond,
                           own_col=jnp.stack([own, row, beyond[0]]),
                           other_col=jnp.stack([col, both, beyond[1]])))

    allowed, present = geometry(tissue, row_at, col_at, tile_slot[0, 0])
    first_row = zh == 0
    allowed = jnp.stack([
        allowed[1],
        jnp.where(first_row, allowed[2], allowed[0]),
        jnp.where(first_row, allowed[0], allowed[2]),
    ])
    allowed = jnp.concatenate([
        allowed[:, 1],
        jnp.where(is_low, allowed[:, 2], allowed[:, 0]),
        jnp.where(is_low, allowed[:, 0], allowed[:, 2]),
    ])
    cot_block = cotangent[0, 0]
    dy = jnp.where(present > 0, cot_block, jnp.zeros_like(cot_block))
    dattn = dot(dy, proj_out, NT).astype(bf16)
    outs, dqs, backs, early = ([], [], [], [])
    for g in range(GROUPS):
        own_col, other_col = (stages[g]["own_col"], stages[g]["other_col"])
        side_col, third_col = (to_sibling(own_col), move(other_col, THIRD_COL))
        first = []
        if g + 2 < GROUPS:
            first.append(stages[g + 2]["outer"])
        if g + 1 < GROUPS:
            first += [stages[g + 1]["own_col"], stages[g + 1]["other_col"]]
        if g >= 2:
            first.append(backs[g - 2][3])
        if g == GROUPS - 1:
            first += early
        own_col, side_col, third_col = lax.optimization_barrier((own_col, side_col, third_col, *first))[:3]
        out, dq, down, dside, dthird = attend(allowed, qkv, dattn, own_col, side_col, third_col, g)
        if g == 0:
            two = after(normed, out)
            two = jnp.stack([two, to_pair(two)])
            normed_all = jnp.concatenate([two, to_sibling(two)], axis=0)
            dy_slices = after(jnp.stack([dy[:, i * half:(i + 1) * half] for i in range(4)]), out)
            dy_all = lax.all_to_all(dy_slices, GROUP, 0, 0, tiled=True)
            early += [normed_all, dy_all]
        side = to_sibling(dside)
        third = move(dthird, THIRD_COL, back=True)
        column = down.astype(f32) + side.astype(f32)
        outer = jnp.stack([column[2].astype(bf16), third[2]])
        outs.append(out)
        dqs.append(dq)
        backs.append((column, third, down, outer))
    attn = jnp.concatenate(outs, axis=1)
    dq = jnp.concatenate(dqs, axis=1)
    last = backs[-1][3]
    zl = lax.axis_index("zl")
    me = 2 * zl + core
    places = [(me ^ slot) for slot in range(4)]
    places = jnp.stack([(p % 2) * 2 + p // 2 for p in places] + [zl]).astype(jnp.int32)
    two = jnp.concatenate([attn, dq], axis=1)
    two = jnp.stack([two, to_pair(two)])
    low, high = (two[:, :, inner:inner + half], two[:, :, inner + half:])
    mine = jnp.concatenate([two[:, :, :inner], jnp.where(is_low, low, high)], axis=2)
    other = jnp.concatenate([two[:, :, :inner], jnp.where(is_low, high, low)], axis=2)
    four = jnp.concatenate([mine, to_sibling(other)], axis=0)
    early = grads(
        early_kernel, 2 * (half // 128), places, normed_all, four[:, :, inner:], four[:, :, :inner], dy_all
    )
    dkvs = []
    for g, (column, third, _, outer) in enumerate(backs):
        beyond = move(outer, BEYOND_ROW, back=True).astype(f32)
        row = (column[1] + beyond[0]).astype(bf16)
        both = (third[1].astype(f32) + beyond[1]).astype(bf16)
        col = third[0]
        if g == GROUPS - 2:
            row, both, col = lax.optimization_barrier((row, both, col, last))[:3]
        row = move(row, OTHER_ROW)
        both = move(both, OTHER_BOTH)
        col = move(col, OTHER_COL)
        total = column[0] + row.astype(f32) + both.astype(f32) + col.astype(f32)
        dkvs.append(total.astype(bf16))

    branch = dot(attn, proj_out)
    branch = jnp.where(present > 0, branch, jnp.zeros_like(branch)).astype(bf16)
    blocks = half // 128
    joined = jnp.concatenate([total[0] for total in dkvs] + [total[1] for total in dkvs], axis=1)
    slices = jnp.stack([joined[:, i * half:(i + 1) * half] for i in range(4)])
    slices = lax.all_to_all(slices, GROUP, 0, 0, tiled=True)
    late = grads(late_kernel, 4 * blocks, places, normed_all, slices, early)

    dnormed = dot(dq, proj_in[:, :inner], NT)
    for g, total in enumerate(lax.optimization_barrier((*dkvs, late))[:GROUPS]):
        lo = inner + g * size
        dnormed = dnormed + (
            dot(total[0], proj_in[:, lo:lo + size], NT)
            + dot(total[1], proj_in[:, inner + lo:inner + lo + size], NT)
        )
    gain_gradient = jnp.sum(dnormed * xhat, axis=0)
    late = lax.all_to_all(late.reshape(N_PAIR, -1, 128), PAIRS, 0, 0, tiled=True)


    centred = dnormed * layer_norm_gain
    input_gradient = inverse_deviation * (
        centred
        - jnp.mean(centred, axis=-1, keepdims=True)
        - xhat * jnp.mean(centred * xhat, axis=-1, keepdims=True)
    )
    branch_grad = input_gradient.astype(bf16)

    late, branch, branch_grad, gain_gradient = lax.optimization_barrier(
        (late, branch, branch_grad, gain_gradient)
    )
    share = jnp.sum(late.astype(f32), axis=0)
    rows = width // 128
    summands = jnp.full((16 - rows, 128), square_sum(share), f32)
    summands = butterfly(jnp.concatenate([gain_gradient.reshape(rows, 128), summands], axis=0))
    gain = summands[:rows].reshape(-1)
    total_sq = summands[rows, 0] + square_sum(gain)
    count = width * 3 * inner + inner * width + width
    factor = 1.0 / jnp.maximum(jnp.sqrt(total_sq / count), 1.0)

    span = blocks * SPAN
    share_q = unpacked(share[:span])
    rows = SPAN // 2
    mine, other = swapped(share_q[:rows], share_q[rows:])
    full_q = [jnp.where(is_low, mine, other), jnp.where(is_low, other, mine)]
    share_out = unpacked(share[span:2 * span]).reshape(4, SPAN // 4, half)
    share_kv = jnp.concatenate([unpacked(share[2 * span:3 * span]), unpacked(share[3 * span:])], axis=0)
    parts = jnp.concatenate([share_kv.reshape(4, rows, half), share_out], axis=1)
    parts = parts.reshape(2, 2, rows + SPAN // 4, half)
    mine, other = swapped(parts[:, 0], parts[:, 1])
    parts = jnp.stack([jnp.where(is_low, mine, other), jnp.where(is_low, other, mine)], axis=1)
    low_z = zl == 0
    mine, other = (jnp.where(low_z, parts[0], parts[1]), jnp.where(low_z, parts[1], parts[0]))
    other = to_pair(other)
    parts = jnp.stack([jnp.where(low_z, mine, other), jnp.where(low_z, other, mine)])
    parts = [parts[i // 2, i % 2] for i in range(4)]
    full_in = jnp.concatenate(full_q + [part[:rows] for part in parts], axis=1)
    full_out = jnp.concatenate([part[rows:] for part in parts], axis=1)
    rows = SPAN // 2
    gain_own = lax.dynamic_slice(gain, ((chip_at * 2 + core) * rows,), (rows,))
    return (
        branch[None, None],
        branch_grad[None, None],
        factor * full_in,
        factor * full_out,
        factor * gain_own,
    )


def solution(mesh):
    fine = Mesh(mesh.devices.reshape(SIZES), AXES)
    row, col = (("x", "zh"), ("y", "zl", "core"))
    in_specs = (
        P(row, col, None, None),
        P(),
        P(),
        P(),
        P(),
        P(row, col),
        P(row, col, None, None),
    )
    out_specs = (
        P(row, col, None, None),
        P(row, col, None, None),
        P(AXES, None),
        P(AXES, None),
        P(AXES),
    )
    return jax.shard_map(local, mesh=fine, in_specs=in_specs, out_specs=out_specs, check_vma=False)
```

```python
import jax
import jax.numpy as jnp
from jax import lax
from jax.experimental import pallas as pl
from jax.experimental.pallas import tpu as pltpu
from jax.sharding import Mesh
from jax.sharding import PartitionSpec as P

HEAD_DIM = 64
REGION = 3
RADIUS = 3
EPSILON = 1e-05
NEG_BIG = -1e30
GROUPS = 2

AXES = ("x", "zh", "y", "zl", "core")
CHIPS = ("x", "zh", "y", "zl")
SIZES = (4, 2, 4, 2, 2)
ROWS, COLS = 8, 16
GROUP = ("zl", "core")
PAIRS = ("x", "zh", "y")
N_PAIR = 32
SPAN = 24

NN = (((1,), (0,)), ((), ()))
NT = (((1,), (1,)), ((), ()))
TN = (((0,), (0,)), ((), ()))
f32 = jnp.float32
bf16 = jnp.bfloat16


def dot(a, b, dims=NN):
    return lax.dot_general(a, b, dims, preferred_element_type=f32)


def routes(move):
    index = lambda p: (((p[0] * 2 + p[1]) * 4 + p[2]) * 2 + p[3]) * 2 + p[4]
    places = [(x, zh, y, zl, c) for x in range(4) for zh in range(2)
              for y in range(4) for zl in range(2) for c in range(2)]
    pairs = [(p, move(*p)) for p in places]
    return [(index(p), index(t)) for p, t in pairs if 0 <= t[0] < 4 and 0 <= t[2] < 4]


def third_column(x, zh, y, zl, c):
    if c == zl:
        return (x, zh, y, zl, 1 - c)
    return (x, zh, y + 1 - 2 * zl, zl, 1 - c)


OTHER_ROW = routes(lambda x, zh, y, zl, c: (x, 1 - zh, y, zl, c))
OTHER_COL = routes(lambda x, zh, y, zl, c: (x, zh, y, 1 - zl, c))
OTHER_BOTH = routes(lambda x, zh, y, zl, c: (x, 1 - zh, y, 1 - zl, c))
BEYOND_ROW = routes(lambda x, zh, y, zl, c: (x + 1 - 2 * zh, zh, y, zl, c))
THIRD_COL = routes(third_column)


def after(value, *others):
    return lax.optimization_barrier((value,) + others)[0]


def move(value, route, back=False):
    return lax.ppermute(value, AXES, [(t, f) for f, t in route] if back else route)


def to_sibling(value):
    return lax.ppermute(value, "core", [(0, 1), (1, 0)])


def to_pair(value):
    return lax.ppermute(value, "zl", [(0, 1), (1, 0)])


def apply_layer_norm(block):
    values = block.astype(f32)
    centred = values - jnp.mean(values, axis=-1, keepdims=True)
    inverse_deviation = lax.rsqrt(jnp.mean(centred * centred, axis=-1, keepdims=True) + EPSILON)
    return (centred * inverse_deviation, inverse_deviation)


def geometry(tissue, row_at, col_at, slot):
    padded = jnp.pad(tissue, REGION)
    window = lax.dynamic_slice(padded, (row_at * REGION, col_at * REGION), (3 * REGION, 3 * REGION))
    blocks = window.reshape(3, REGION, 3, REGION)
    occupied = jnp.sum(blocks, axis=(1, 3))
    inner = jnp.arange(REGION, dtype=jnp.int32)
    row_in = jnp.sum(blocks * inner[None, :, None, None], axis=(1, 3))
    col_in = jnp.sum(blocks * inner[None, None, None, :], axis=(1, 3))
    three = jnp.arange(3, dtype=jnp.int32)
    key_row = (row_at - 1 + three)[:, None] * REGION + row_in
    key_col = (col_at - 1 + three)[None, :] * REGION + col_in
    query_row = row_at * REGION + slot // REGION
    query_col = col_at * REGION + slot % REGION
    present = lax.dynamic_slice(tissue, (query_row, query_col), (1, 1))[0, 0]
    inside = (
        (jnp.abs(key_row - query_row) <= RADIUS)
        & (jnp.abs(key_col - query_col) <= RADIUS)
        & (occupied > 0)
    )
    centre = (three[:, None] == 1) & (three[None, :] == 1)
    return ((inside | centre).astype(jnp.int32), present)


def attend_kernel(allow_ref, q_ref, g_ref, own_ref, side_ref, third_ref,
                  out_ref, dq_ref, down_ref, dside_ref, dthird_ref, s_scr, dp_scr):
    tile_len = q_ref.shape[0]
    kv_refs = (own_ref, side_ref, third_ref)
    dkv_refs = (down_ref, dside_ref, dthird_ref)
    places = [(a, b) for b in range(3) for a in range(3)]
    first = lax.broadcasted_iota(jnp.int32, (tile_len, 2 * HEAD_DIM), 1) < HEAD_DIM

    def head_pair(v):
        zero = jnp.zeros_like(v)
        return jnp.concatenate([jnp.where(first, v, zero), jnp.where(first, zero, v)], axis=0)

    qq = head_pair(q_ref[...] * jnp.asarray(HEAD_DIM ** -0.5, bf16))
    gg = head_pair(g_ref[...])
    top = jnp.full((1, 2 * tile_len), NEG_BIG, f32)
    for i, (a, b) in enumerate(places):
        scores = dot(kv_refs[b][a, 0], qq, NT)
        scores = jnp.where(allow_ref[b * 3 + a] > 0, scores, NEG_BIG)
        s_scr[i] = scores
        top = jnp.maximum(top, jnp.max(scores, axis=0, keepdims=True))
    total = jnp.zeros((1, 2 * tile_len), f32)
    mix = jnp.zeros((1, 2 * tile_len), f32)
    for i, (a, b) in enumerate(places):
        weights = jnp.exp(s_scr[i] - top)
        dprobs = dot(kv_refs[b][a, 1], gg, NT)
        total = total + jnp.sum(weights, axis=0, keepdims=True)
        mix = mix + jnp.sum(dprobs * weights, axis=0, keepdims=True)
        s_scr[i] = weights
        dp_scr[i] = dprobs
    inverse = 1.0 / total
    mix = mix * inverse
    outs = [jnp.zeros((HEAD_DIM, tile_len), f32)] * 2
    dqs = [jnp.zeros((HEAD_DIM, tile_len), f32)] * 2
    for i, (a, b) in enumerate(places):
        probs = s_scr[i] * inverse
        probs_b = probs.astype(bf16)
        dscores = (probs * (dp_scr[i] - mix)).astype(bf16)
        dkv_refs[b][a, 1] = dot(probs_b, gg).astype(bf16)
        dkv_refs[b][a, 0] = dot(dscores, qq).astype(bf16)
        keys_t = kv_refs[b][a, 0].T
        vals_t = kv_refs[b][a, 1].T
        for h in range(2):
            part = slice(h * HEAD_DIM, (h + 1) * HEAD_DIM)
            lanes = slice(h * tile_len, (h + 1) * tile_len)
            outs[h] = outs[h] + dot(vals_t[part], probs_b[:, lanes])
            dqs[h] = dqs[h] + dot(keys_t[part], dscores[:, lanes])
    out_ref[...] = jnp.concatenate(outs, axis=0).T.astype(bf16)
    dq_ref[...] = (jnp.concatenate(dqs, axis=0).T * HEAD_DIM ** -0.5).astype(bf16)


def attend(allowed, qkv, dattn, own, side, third, group):
    tile_len, width = (own.shape[2], own.shape[3])
    block = 2 * HEAD_DIM
    steps = width // block
    place = lambda h: (0, h + group * steps)
    near = lambda h: (0, 0, 0, h)
    kv_spec = pl.BlockSpec((3, 2, tile_len, block), near)
    row_spec = pl.BlockSpec((tile_len, block), lambda h: (0, h))
    row_shape = jax.ShapeDtypeStruct((tile_len, width), bf16)
    kv_shape = jax.ShapeDtypeStruct(own.shape, bf16)
    scratch = pltpu.VMEM((9, tile_len, 2 * tile_len), f32)
    return pl.pallas_call(
        attend_kernel,
        grid=(steps,),
        in_specs=[
            pl.BlockSpec(memory_space=pltpu.SMEM),
            pl.BlockSpec((tile_len, block), place),
            pl.BlockSpec((tile_len, block), place),
            kv_spec, kv_spec, kv_spec,
        ],
        out_specs=[row_spec, row_spec, kv_spec, kv_spec, kv_spec],
        out_shape=[row_shape, row_shape, kv_shape, kv_shape, kv_shape],
        scratch_shapes=[scratch, scratch],
        compiler_params=pltpu.CompilerParams(vmem_limit_bytes=40 * 1024 * 1024),
        cost_estimate=pl.CostEstimate(
            flops=width * tile_len * tile_len * 9 * 12 * 4,
            bytes_accessed=width * tile_len * 2 * 40,
            transcendentals=width // HEAD_DIM * tile_len * tile_len * 9,
        ),
    )(allowed, qkv, dattn, own, side, third)


def grad_blocks(left, right, places, first, last):
    lanes = slice(first, last)
    grad = dot(left[places[0], :, lanes], right[0], TN)
    for slot in range(1, 4):
        grad = grad + dot(left[places[slot], :, lanes], right[slot], TN)
    return grad.astype(bf16)


def early_kernel(place_ref, normed, dq, attn, dy, out_ref):
    step = 16 * SPAN
    blocks = dq.shape[2] // 128
    upper = place_ref[4] > 0
    places = [place_ref[slot] for slot in range(4)]
    for r in range(normed.shape[2] // step):
        grad = grad_blocks(normed, dq, range(4), r * step, (r + 1) * step)
        grad = grad.reshape(8, 2, SPAN, step)
        grad = jnp.where(upper, grad[:, 1], grad[:, 0])
        for j in range(blocks):
            out_ref[r * 8:(r + 1) * 8, j] = grad[:, :, j * 128:(j + 1) * 128]
    for r in range(attn.shape[2] // step):
        grad = grad_blocks(attn, dy, places, r * step, (r + 1) * step)
        grad = grad.reshape(16, SPAN, step)
        for j in range(blocks):
            out_ref[r * 16:(r + 1) * 16, blocks + j] = grad[:, :, j * 128:(j + 1) * 128]


def late_kernel(place_ref, normed, dkv, early, out_ref):
    step = 16 * SPAN
    blocks = dkv.shape[2] // 128
    places = [place_ref[slot] for slot in range(4)]
    out_ref[:, :2 * blocks] = early[...]
    for r in range(normed.shape[2] // step):
        grad = grad_blocks(normed, dkv, places, r * step, (r + 1) * step)
        grad = grad.reshape(8, 2, SPAN, step)
        for half in range(2):
            for j in range(blocks):
                out_ref[r * 8:(r + 1) * 8, (2 + half) * blocks + j] = grad[:, half, :, j * 128:(j + 1) * 128]


def grads(kernel, blocks, places, *operands):
    vmem = pl.BlockSpec(memory_space=pltpu.VMEM)
    return pl.pallas_call(
        kernel,
        in_specs=[pl.BlockSpec(memory_space=pltpu.SMEM)] + [vmem] * len(operands),
        out_specs=vmem,
        out_shape=jax.ShapeDtypeStruct((N_PAIR, blocks, SPAN, 128), bf16),
        compiler_params=pltpu.CompilerParams(vmem_limit_bytes=32 * 1024 * 1024),
        cost_estimate=pl.CostEstimate(flops=1000000, bytes_accessed=1000000, transcendentals=0),
    )(places, *operands)


def butterfly(value):
    for bit in range(7):
        value = value + lax.ppermute(value, AXES, [(i, i ^ (1 << bit)) for i in range(ROWS * COLS)])
    return value


def unpacked(share):
    count = share.shape[0] // SPAN
    return share.reshape(count, SPAN, 128).transpose(1, 0, 2).reshape(SPAN, count * 128)


def square_sum(value):
    return jnp.sum(value * value)


def local(tokens, layer_norm_gain, proj_in, proj_out, tissue, tile_slot, cotangent):
    chip_at = lax.axis_index(CHIPS)
    core = lax.axis_index("core")
    zh = lax.axis_index("zh")
    row_at = chip_at // (COLS // 2)
    col_at = (chip_at % (COLS // 2)) * 2 + core
    tile_len, width = tokens.shape[2:]
    inner = proj_out.shape[0]
    half = inner // 2
    is_low = core == 0

    def swapped(lower, upper):
        mine, other = (jnp.where(is_low, lower, upper), jnp.where(is_low, upper, lower))
        return (mine, to_sibling(other))

    xhat, inverse_deviation = apply_layer_norm(tokens[0, 0])
    normed = (xhat * layer_norm_gain).astype(bf16)
    size = inner // GROUPS
    qkv = dot(normed, proj_in).astype(bf16)

    def gather_block(g, *others):
        lo = inner + g * size
        own = jnp.stack([qkv[:, lo:lo + size], qkv[:, inner + lo:inner + lo + size]])
        if others:
            own = after(own, *others)
        return (own, move(own, OTHER_ROW), move(own, OTHER_COL), move(own, OTHER_BOTH))

    stages = []
    for g in range(GROUPS):
        others = []
        if g >= 1:
            others += stages[g - 1]["block"][1:]
        if g >= 2:
            others.append(stages[g - 2]["beyond"])
        own, row, col, both = gather_block(g, *others)
        outer = jnp.stack([row, both])
        if g >= 1:
            outer = after(outer, stages[g - 1]["own_col"], stages[g - 1]["other_col"])
        beyond = move(outer, BEYOND_ROW)
        stages.append(dict(block=(own, row, col, both), outer=outer, beyond=beyond,
                           own_col=jnp.stack([own, row, beyond[0]]),
                           other_col=jnp.stack([col, both, beyond[1]])))

    allowed, present = geometry(tissue, row_at, col_at, tile_slot[0, 0])
    first_row = zh == 0
    allowed = jnp.stack([
        allowed[1],
        jnp.where(first_row, allowed[2], allowed[0]),
        jnp.where(first_row, allowed[0], allowed[2]),
    ])
    allowed = jnp.concatenate([
        allowed[:, 1],
        jnp.where(is_low, allowed[:, 2], allowed[:, 0]),
        jnp.where(is_low, allowed[:, 0], allowed[:, 2]),
    ])
    cot_block = cotangent[0, 0]
    dy = jnp.where(present > 0, cot_block, jnp.zeros_like(cot_block))
    dattn = dot(dy, proj_out, NT).astype(bf16)
    outs, dqs, backs, early = ([], [], [], [])
    for g in range(GROUPS):
        own_col, other_col = (stages[g]["own_col"], stages[g]["other_col"])
        side_col, third_col = (to_sibling(own_col), move(other_col, THIRD_COL))
        first = []
        if g + 2 < GROUPS:
            first.append(stages[g + 2]["outer"])
        if g + 1 < GROUPS:
            first += [stages[g + 1]["own_col"], stages[g + 1]["other_col"]]
        if g >= 2:
            first.append(backs[g - 2][3])
        own_col, side_col, third_col = lax.optimization_barrier((own_col, side_col, third_col, *first))[:3]
        out, dq, down, dside, dthird = attend(allowed, qkv, dattn, own_col, side_col, third_col, g)
        if g == 0:
            two = after(normed, out)
            two = jnp.stack([two, to_pair(two)])
            normed_all = jnp.concatenate([two, to_sibling(two)], axis=0)
            dy_slices = after(jnp.stack([dy[:, i * half:(i + 1) * half] for i in range(4)]), out)
            dy_all = lax.all_to_all(dy_slices, GROUP, 0, 0, tiled=True)
            early += [normed_all, dy_all]
        side = to_sibling(dside)
        third = move(dthird, THIRD_COL, back=True)
        column = down.astype(f32) + side.astype(f32)
        outer = jnp.stack([column[2].astype(bf16), third[2]])
        if g == GROUPS - 1:
            outer, *early = lax.optimization_barrier((outer, *early))
            normed_all, dy_all = early
        outs.append(out)
        dqs.append(dq)
        backs.append((column, third, down, outer))
    attn = jnp.concatenate(outs, axis=1)
    dq = jnp.concatenate(dqs, axis=1)
    last = backs[-1][3]
    zl = lax.axis_index("zl")
    me = 2 * zl + core
    places = [(me ^ slot) for slot in range(4)]
    places = jnp.stack([(p % 2) * 2 + p // 2 for p in places] + [zl]).astype(jnp.int32)
    two = jnp.concatenate([attn, dq], axis=1)
    two = jnp.stack([two, to_pair(two)])
    low, high = (two[:, :, inner:inner + half], two[:, :, inner + half:])
    mine = jnp.concatenate([two[:, :, :inner], jnp.where(is_low, low, high)], axis=2)
    other = jnp.concatenate([two[:, :, :inner], jnp.where(is_low, high, low)], axis=2)
    four = jnp.concatenate([mine, to_sibling(other)], axis=0)
    early = grads(
        early_kernel, 2 * (half // 128), places, normed_all, four[:, :, inner:], four[:, :, :inner], dy_all
    )
    dkvs = []
    for g, (column, third, _, outer) in enumerate(backs):
        beyond = move(outer, BEYOND_ROW, back=True).astype(f32)
        row = (column[1] + beyond[0]).astype(bf16)
        both = (third[1].astype(f32) + beyond[1]).astype(bf16)
        col = third[0]
        if g == GROUPS - 2:
            row, both, col = lax.optimization_barrier((row, both, col, last))[:3]
        row = move(row, OTHER_ROW)
        both = move(both, OTHER_BOTH)
        col = move(col, OTHER_COL)
        total = column[0] + row.astype(f32) + both.astype(f32) + col.astype(f32)
        dkvs.append(total.astype(bf16))

    branch = dot(attn, proj_out)
    branch = jnp.where(present > 0, branch, jnp.zeros_like(branch)).astype(bf16)
    blocks = half // 128
    *dkvs, branch, early = lax.optimization_barrier((*dkvs, branch, early))
    slices = jnp.stack([total[part] for part in range(2) for total in dkvs])
    slices = lax.all_to_all(slices, GROUP, 0, 0, tiled=True)
    late = grads(late_kernel, 4 * blocks, places, normed_all, slices, early)

    dnormed = dot(dq, proj_in[:, :inner], NT)
    for g, total in enumerate(lax.optimization_barrier((*dkvs, late))[:GROUPS]):
        lo = inner + g * size
        dnormed = dnormed + (
            dot(total[0], proj_in[:, lo:lo + size], NT)
            + dot(total[1], proj_in[:, inner + lo:inner + lo + size], NT)
        )
    gain_gradient = jnp.sum(dnormed * xhat, axis=0)
    late = lax.all_to_all(late.reshape(N_PAIR, -1, 128), PAIRS, 0, 0, tiled=True)


    centred = dnormed * layer_norm_gain
    input_gradient = inverse_deviation * (
        centred
        - jnp.mean(centred, axis=-1, keepdims=True)
        - xhat * jnp.mean(centred * xhat, axis=-1, keepdims=True)
    )
    branch_grad = input_gradient.astype(bf16)

    late, branch, branch_grad, gain_gradient = lax.optimization_barrier(
        (late, branch, branch_grad, gain_gradient)
    )
    share = jnp.sum(late.astype(f32), axis=0)
    rows = width // 128
    summands = jnp.full((16 - rows, 128), square_sum(share), f32)
    summands = butterfly(jnp.concatenate([gain_gradient.reshape(rows, 128), summands], axis=0))
    gain = summands[:rows].reshape(-1)
    total_sq = summands[rows, 0] + square_sum(gain)
    count = width * 3 * inner + inner * width + width
    factor = 1.0 / jnp.maximum(jnp.sqrt(total_sq / count), 1.0)

    span = blocks * SPAN
    share_q = unpacked(share[:span])
    rows = SPAN // 2
    mine, other = swapped(share_q[:rows], share_q[rows:])
    full_q = [jnp.where(is_low, mine, other), jnp.where(is_low, other, mine)]
    share_out = unpacked(share[span:2 * span]).reshape(4, SPAN // 4, half)
    share_kv = jnp.concatenate([unpacked(share[2 * span:3 * span]), unpacked(share[3 * span:])], axis=0)
    parts = jnp.concatenate([share_kv.reshape(4, rows, half), share_out], axis=1)
    parts = parts.reshape(2, 2, rows + SPAN // 4, half)
    mine, other = swapped(parts[:, 0], parts[:, 1])
    parts = jnp.stack([jnp.where(is_low, mine, other), jnp.where(is_low, other, mine)], axis=1)
    low_z = zl == 0
    mine, other = (jnp.where(low_z, parts[0], parts[1]), jnp.where(low_z, parts[1], parts[0]))
    other = to_pair(other)
    parts = jnp.stack([jnp.where(low_z, mine, other), jnp.where(low_z, other, mine)])
    parts = [parts[i // 2, i % 2] for i in range(4)]
    full_in = jnp.concatenate(full_q + [part[:rows] for part in parts], axis=1)
    full_out = jnp.concatenate([part[rows:] for part in parts], axis=1)
    rows = SPAN // 2
    gain_own = lax.dynamic_slice(gain, ((chip_at * 2 + core) * rows,), (rows,))
    return (
        branch[None, None],
        branch_grad[None, None],
        factor * full_in,
        factor * full_out,
        factor * gain_own,
    )


def solution(mesh):
    fine = Mesh(mesh.devices.reshape(SIZES), AXES)
    row, col = (("x", "zh"), ("y", "zl", "core"))
    in_specs = (
        P(row, col, None, None),
        P(),
        P(),
        P(),
        P(),
        P(row, col),
        P(row, col, None, None),
    )
    out_specs = (
        P(row, col, None, None),
        P(row, col, None, None),
        P(AXES, None),
        P(AXES, None),
        P(AXES),
    )
    return jax.shard_map(local, mesh=fine, in_specs=in_specs, out_specs=out_specs, check_vma=False)
```

```python
import jax
import jax.numpy as jnp
from jax import lax
from jax.experimental import pallas as pl
from jax.experimental.pallas import tpu as pltpu
from jax.sharding import Mesh
from jax.sharding import PartitionSpec as P

HEAD_DIM = 64
REGION = 3
RADIUS = 3
EPSILON = 1e-05
NEG_BIG = -1e30
GROUP_LANES = (384, 256, 128)
GROUPS = len(GROUP_LANES)

AXES = ("x", "zh", "y", "zl", "core")
CHIPS = ("x", "zh", "y", "zl")
SIZES = (4, 2, 4, 2, 2)
ROWS, COLS = 8, 16
GROUP = ("zl", "core")
PAIRS = ("x", "zh", "y")
N_PAIR = 32
SPAN = 24

NN = (((1,), (0,)), ((), ()))
NT = (((1,), (1,)), ((), ()))
TN = (((0,), (0,)), ((), ()))
f32 = jnp.float32
bf16 = jnp.bfloat16


def dot(a, b, dims=NN):
    return lax.dot_general(a, b, dims, preferred_element_type=f32)


def routes(move):
    index = lambda p: (((p[0] * 2 + p[1]) * 4 + p[2]) * 2 + p[3]) * 2 + p[4]
    places = [(x, zh, y, zl, c) for x in range(4) for zh in range(2)
              for y in range(4) for zl in range(2) for c in range(2)]
    pairs = [(p, move(*p)) for p in places]
    return [(index(p), index(t)) for p, t in pairs if 0 <= t[0] < 4 and 0 <= t[2] < 4]


def third_column(x, zh, y, zl, c):
    if c == zl:
        return (x, zh, y, zl, 1 - c)
    return (x, zh, y + 1 - 2 * zl, zl, 1 - c)


OTHER_ROW = routes(lambda x, zh, y, zl, c: (x, 1 - zh, y, zl, c))
OTHER_COL = routes(lambda x, zh, y, zl, c: (x, zh, y, 1 - zl, c))
OTHER_BOTH = routes(lambda x, zh, y, zl, c: (x, 1 - zh, y, 1 - zl, c))
BEYOND_ROW = routes(lambda x, zh, y, zl, c: (x + 1 - 2 * zh, zh, y, zl, c))
THIRD_COL = routes(third_column)


def after(value, *others):
    return lax.optimization_barrier((value,) + others)[0]


def move(value, route, back=False):
    return lax.ppermute(value, AXES, [(t, f) for f, t in route] if back else route)


def to_sibling(value):
    return lax.ppermute(value, "core", [(0, 1), (1, 0)])


def to_pair(value):
    return lax.ppermute(value, "zl", [(0, 1), (1, 0)])


def apply_layer_norm(block):
    values = block.astype(f32)
    centred = values - jnp.mean(values, axis=-1, keepdims=True)
    inverse_deviation = lax.rsqrt(jnp.mean(centred * centred, axis=-1, keepdims=True) + EPSILON)
    return (centred * inverse_deviation, inverse_deviation)


def geometry(tissue, row_at, col_at, slot):
    padded = jnp.pad(tissue, REGION)
    window = lax.dynamic_slice(padded, (row_at * REGION, col_at * REGION), (3 * REGION, 3 * REGION))
    blocks = window.reshape(3, REGION, 3, REGION)
    occupied = jnp.sum(blocks, axis=(1, 3))
    inner = jnp.arange(REGION, dtype=jnp.int32)
    row_in = jnp.sum(blocks * inner[None, :, None, None], axis=(1, 3))
    col_in = jnp.sum(blocks * inner[None, None, None, :], axis=(1, 3))
    three = jnp.arange(3, dtype=jnp.int32)
    key_row = (row_at - 1 + three)[:, None] * REGION + row_in
    key_col = (col_at - 1 + three)[None, :] * REGION + col_in
    query_row = row_at * REGION + slot // REGION
    query_col = col_at * REGION + slot % REGION
    present = lax.dynamic_slice(tissue, (query_row, query_col), (1, 1))[0, 0]
    inside = (
        (jnp.abs(key_row - query_row) <= RADIUS)
        & (jnp.abs(key_col - query_col) <= RADIUS)
        & (occupied > 0)
    )
    centre = (three[:, None] == 1) & (three[None, :] == 1)
    return ((inside | centre).astype(jnp.int32), present)


def attend_kernel(allow_ref, q_ref, g_ref, own_ref, side_ref, third_ref,
                  out_ref, dq_ref, down_ref, dside_ref, dthird_ref, s_scr, dp_scr):
    tile_len = q_ref.shape[0]
    kv_refs = (own_ref, side_ref, third_ref)
    dkv_refs = (down_ref, dside_ref, dthird_ref)
    places = [(a, b) for b in range(3) for a in range(3)]
    first = lax.broadcasted_iota(jnp.int32, (tile_len, 2 * HEAD_DIM), 1) < HEAD_DIM

    def head_pair(v):
        zero = jnp.zeros_like(v)
        return jnp.concatenate([jnp.where(first, v, zero), jnp.where(first, zero, v)], axis=0)

    qq = head_pair(q_ref[...] * jnp.asarray(HEAD_DIM ** -0.5, bf16))
    gg = head_pair(g_ref[...])
    top = jnp.full((1, 2 * tile_len), NEG_BIG, f32)
    for i, (a, b) in enumerate(places):
        scores = dot(kv_refs[b][a, 0], qq, NT)
        scores = jnp.where(allow_ref[b * 3 + a] > 0, scores, NEG_BIG)
        s_scr[i] = scores
        top = jnp.maximum(top, jnp.max(scores, axis=0, keepdims=True))
    total = jnp.zeros((1, 2 * tile_len), f32)
    mix = jnp.zeros((1, 2 * tile_len), f32)
    for i, (a, b) in enumerate(places):
        weights = jnp.exp(s_scr[i] - top)
        dprobs = dot(kv_refs[b][a, 1], gg, NT)
        total = total + jnp.sum(weights, axis=0, keepdims=True)
        mix = mix + jnp.sum(dprobs * weights, axis=0, keepdims=True)
        s_scr[i] = weights
        dp_scr[i] = dprobs
    inverse = 1.0 / total
    mix = mix * inverse
    outs = [jnp.zeros((HEAD_DIM, tile_len), f32)] * 2
    dqs = [jnp.zeros((HEAD_DIM, tile_len), f32)] * 2
    for i, (a, b) in enumerate(places):
        probs = s_scr[i] * inverse
        probs_b = probs.astype(bf16)
        dscores = (probs * (dp_scr[i] - mix)).astype(bf16)
        dkv_refs[b][a, 1] = dot(probs_b, gg).astype(bf16)
        dkv_refs[b][a, 0] = dot(dscores, qq).astype(bf16)
        keys_t = kv_refs[b][a, 0].T
        vals_t = kv_refs[b][a, 1].T
        for h in range(2):
            part = slice(h * HEAD_DIM, (h + 1) * HEAD_DIM)
            lanes = slice(h * tile_len, (h + 1) * tile_len)
            outs[h] = outs[h] + dot(vals_t[part], probs_b[:, lanes])
            dqs[h] = dqs[h] + dot(keys_t[part], dscores[:, lanes])
    out_ref[...] = jnp.concatenate(outs, axis=0).T.astype(bf16)
    dq_ref[...] = (jnp.concatenate(dqs, axis=0).T * HEAD_DIM ** -0.5).astype(bf16)


def attend(allowed, qkv, dattn, own, side, third, first):
    tile_len, width = (own.shape[2], own.shape[3])
    block = 2 * HEAD_DIM
    steps = width // block
    place = lambda h: (0, h + first // block)
    near = lambda h: (0, 0, 0, h)
    kv_spec = pl.BlockSpec((3, 2, tile_len, block), near)
    row_spec = pl.BlockSpec((tile_len, block), lambda h: (0, h))
    row_shape = jax.ShapeDtypeStruct((tile_len, width), bf16)
    kv_shape = jax.ShapeDtypeStruct(own.shape, bf16)
    scratch = pltpu.VMEM((9, tile_len, 2 * tile_len), f32)
    return pl.pallas_call(
        attend_kernel,
        grid=(steps,),
        in_specs=[
            pl.BlockSpec(memory_space=pltpu.SMEM),
            pl.BlockSpec((tile_len, block), place),
            pl.BlockSpec((tile_len, block), place),
            kv_spec, kv_spec, kv_spec,
        ],
        out_specs=[row_spec, row_spec, kv_spec, kv_spec, kv_spec],
        out_shape=[row_shape, row_shape, kv_shape, kv_shape, kv_shape],
        scratch_shapes=[scratch, scratch],
        compiler_params=pltpu.CompilerParams(vmem_limit_bytes=40 * 1024 * 1024),
        cost_estimate=pl.CostEstimate(
            flops=width * tile_len * tile_len * 9 * 12 * 4,
            bytes_accessed=width * tile_len * 2 * 40,
            transcendentals=width // HEAD_DIM * tile_len * tile_len * 9,
        ),
    )(allowed, qkv, dattn, own, side, third)


def grad_blocks(lefts, rights):
    grad = dot(lefts[0], rights[0], TN)
    for left, right in zip(lefts[1:], rights[1:]):
        grad = grad + dot(left, right, TN)
    return grad.astype(bf16)


def early_kernel(place_ref, *refs):
    normed, both, (dy, out_ref) = (refs[:4], refs[4:8], refs[8:])
    step = 16 * SPAN
    inner, half = (both[0].shape[1] // 2, dy.shape[2])
    blocks = half // 128
    upper_chip, upper_core = (place_ref[4] > 0, place_ref[5] > 0)
    dq = [jnp.where(upper_core, ref[:, inner + half:], ref[:, inner:inner + half]) for ref in both]
    dys = [dy[place_ref[slot]] for slot in range(4)]
    for r in range(normed[0].shape[1] // step):
        lanes = slice(r * step, (r + 1) * step)
        grad = grad_blocks([ref[:, lanes] for ref in normed], dq).reshape(8, 2, SPAN, half)
        grad = jnp.where(upper_chip, grad[:, 1], grad[:, 0])
        for j in range(blocks):
            out_ref[r * 8:(r + 1) * 8, j] = grad[:, :, j * 128:(j + 1) * 128]
    for r in range(inner // step):
        lanes = slice(r * step, (r + 1) * step)
        grad = grad_blocks([ref[:, lanes] for ref in both], dys).reshape(16, SPAN, half)
        for j in range(blocks):
            out_ref[r * 16:(r + 1) * 16, blocks + j] = grad[:, :, j * 128:(j + 1) * 128]


def early_grads(places, *operands):
    vmem = pl.BlockSpec(memory_space=pltpu.VMEM)
    blocks = operands[-1].shape[2] // 128
    return pl.pallas_call(
        early_kernel,
        in_specs=[pl.BlockSpec(memory_space=pltpu.SMEM)] + [vmem] * len(operands),
        out_specs=vmem,
        out_shape=jax.ShapeDtypeStruct((N_PAIR, 2 * blocks, SPAN, 128), bf16),
        compiler_params=pltpu.CompilerParams(vmem_limit_bytes=32 * 1024 * 1024),
        cost_estimate=pl.CostEstimate(flops=1000000, bytes_accessed=1000000, transcendentals=0),
    )(places, *operands)


def late_kernel(place_ref, *refs):
    normed, (dkv, early, out_ref) = (refs[:4], refs[4:])
    blocks = dkv.shape[2] // 128
    out_ref[:, :2 * blocks] = early[...]
    grad = grad_blocks([ref[...] for ref in normed], [dkv[place_ref[slot]] for slot in range(4)])
    grad = grad.reshape(8, 2, SPAN, dkv.shape[2])
    for half in range(2):
        for j in range(blocks):
            out_ref[:, (2 + half) * blocks + j] = grad[:, half, :, j * 128:(j + 1) * 128]


def late_grads(places, *operands):
    step = 16 * SPAN
    tile_len, width = operands[0].shape
    dkv, early = operands[4:]
    blocks = 2 * early.shape[1]
    row = lambda r: (r, 0, 0, 0)
    return pl.pallas_call(
        late_kernel,
        grid=(width // step,),
        in_specs=[pl.BlockSpec(memory_space=pltpu.SMEM)]
        + [pl.BlockSpec((tile_len, step), lambda r: (0, r))] * 4
        + [pl.BlockSpec(dkv.shape, lambda r: (0, 0, 0)), pl.BlockSpec((8, blocks // 2, SPAN, 128), row)],
        out_specs=pl.BlockSpec((8, blocks, SPAN, 128), row),
        out_shape=jax.ShapeDtypeStruct((N_PAIR, blocks, SPAN, 128), bf16),
        compiler_params=pltpu.CompilerParams(vmem_limit_bytes=32 * 1024 * 1024),
        cost_estimate=pl.CostEstimate(flops=1000000, bytes_accessed=1000000, transcendentals=0),
    )(places, *operands)


def butterfly(value):
    for bit in range(7):
        value = value + lax.ppermute(value, AXES, [(i, i ^ (1 << bit)) for i in range(ROWS * COLS)])
    return value


def unpacked(share):
    count = share.shape[0] // SPAN
    return share.reshape(count, SPAN, 128).transpose(1, 0, 2).reshape(SPAN, count * 128)


def square_sum(value):
    return jnp.sum(value * value)


def local(tokens, layer_norm_gain, proj_in, proj_out, tissue, tile_slot, cotangent):
    chip_at = lax.axis_index(CHIPS)
    core = lax.axis_index("core")
    zh = lax.axis_index("zh")
    row_at = chip_at // (COLS // 2)
    col_at = (chip_at % (COLS // 2)) * 2 + core
    tile_len, width = tokens.shape[2:]
    inner = proj_out.shape[0]
    half = inner // 2
    is_low = core == 0

    def swapped(lower, upper):
        mine, other = (jnp.where(is_low, lower, upper), jnp.where(is_low, upper, lower))
        return (mine, to_sibling(other))

    xhat, inverse_deviation = apply_layer_norm(tokens[0, 0])
    normed = (xhat * layer_norm_gain).astype(bf16)
    starts = [sum(GROUP_LANES[:g]) for g in range(GROUPS)]
    qkv = dot(normed, proj_in).astype(bf16)

    def gather_block(g, *others):
        lo, size = (inner + starts[g], GROUP_LANES[g])
        own = jnp.stack([qkv[:, lo:lo + size], qkv[:, inner + lo:inner + lo + size]])
        if others:
            own = after(own, *others)
        return (own, move(own, OTHER_ROW), move(own, OTHER_COL), move(own, OTHER_BOTH))

    def column_operands(block, beyond):
        own, row, col, both = block
        return (jnp.stack([own, row, beyond[0]]), jnp.stack([col, both, beyond[1]]))

    stages, columns = ([], [])
    for g in range(GROUPS):
        own, row, col, both = gather_block(g, *(stages[-1]["block"][2:3] if g else []))
        outer = jnp.stack([row, both])
        if g >= 1:
            outer = after(outer, *columns[g - 1])
        beyond = move(outer, BEYOND_ROW)
        stages.append(dict(block=(own, row, col, both), outer=outer, beyond=beyond))
        if g < 2:
            columns.append(column_operands(stages[g]["block"], beyond))

    allowed, present = geometry(tissue, row_at, col_at, tile_slot[0, 0])
    first_row = zh == 0
    allowed = jnp.stack([
        allowed[1],
        jnp.where(first_row, allowed[2], allowed[0]),
        jnp.where(first_row, allowed[0], allowed[2]),
    ])
    allowed = jnp.concatenate([
        allowed[:, 1],
        jnp.where(is_low, allowed[:, 2], allowed[:, 0]),
        jnp.where(is_low, allowed[:, 0], allowed[:, 2]),
    ])
    cot_block = cotangent[0, 0]
    dy = jnp.where(present > 0, cot_block, jnp.zeros_like(cot_block))
    dattn = dot(dy, proj_out, NT).astype(bf16)
    def block_sends(column, third, down, outer, beyond):
        return ((column[1] + beyond[0]).astype(bf16), (third[1].astype(f32) + beyond[1]).astype(bf16))

    outs, dqs, backs, early, sides = ([], [], [], [], {})
    for g in range(GROUPS):
        own_col, other_col = columns[g]
        side_col, third_col = (sides[g] if g in sides else to_sibling(own_col), move(other_col, THIRD_COL))
        first = []
        if g == 0:
            sides[1] = to_sibling(columns[1][0])
            first += [*columns[1], sides[1], stages[2]["outer"]]
        else:
            first.append(outs[g - 1])
            first.append(last_side)
        if g == 1:
            sides[2] = to_sibling(columns[2][0])
            first += [*columns[2], sides[2]]
        if g == 2:
            first.append(backs[0][3])
        own_col, side_col, third_col = lax.optimization_barrier((own_col, side_col, third_col, *first))[:3]
        out, dq, down, dside, dthird = attend(allowed, qkv, dattn, own_col, side_col, third_col, starts[g])
        if g == 0:
            columns.append(column_operands(stages[2]["block"], after(stages[2]["beyond"], out)))
            mine = after(normed, out)
            pair = to_pair(mine)
            early = [pair, to_sibling(mine), to_sibling(pair)]
            dy_slices = after(jnp.stack([dy[:, i * half:(i + 1) * half] for i in range(4)]), out)
            early.append(lax.all_to_all(dy_slices, GROUP, 0, 0, tiled=True))
        side = to_sibling(dside)
        last_side = side
        third = move(dthird, THIRD_COL, back=True)
        column = down.astype(f32) + side.astype(f32)
        outer = jnp.stack([column[2].astype(bf16), third[2]])
        if g == 1:
            outer = after(outer, *block_sends(*backs[0]))
        if g == GROUPS - 1:
            outer, *early, _, _ = lax.optimization_barrier((outer, *early, *block_sends(*backs[0])))
            *normed_others, dy_all = early
        outs.append(out)
        dqs.append(dq)
        backs.append((column, third, down, outer, move(outer, BEYOND_ROW, back=True).astype(f32)))
    attn = jnp.concatenate(outs, axis=1)
    dq = jnp.concatenate(dqs, axis=1)
    last = backs[-1][3]
    zl = lax.axis_index("zl")
    me = 2 * zl + core
    places = jnp.stack([me, me ^ 2, me ^ 1, me ^ 3, zl, core]).astype(jnp.int32)
    mine = jnp.concatenate([attn, dq], axis=1)
    pair = to_pair(mine)
    early = early_grads(
        places, normed, *normed_others, mine, pair, to_sibling(mine), to_sibling(pair), dy_all
    )
    dkvs = []
    for g, (column, third, down, outer, beyond) in enumerate(backs):
        row, both = block_sends(column, third, down, outer, beyond)
        col = third[0]
        if g == 1:
            row, both, col = lax.optimization_barrier((row, both, col, last, previous[2]))[:3]
        if g == 2:
            row, both, col = lax.optimization_barrier((row, both, col, *previous[:2]))[:3]
        sends = (row, both)
        row = move(row, OTHER_ROW)
        both = move(both, OTHER_BOTH)
        col = move(col, OTHER_COL)
        previous = (*sends, col)
        total = column[0] + row.astype(f32) + both.astype(f32) + col.astype(f32)
        dkvs.append(total.astype(bf16))

    branch = dot(attn, proj_out)
    branch = jnp.where(present > 0, branch, jnp.zeros_like(branch)).astype(bf16)
    blocks = half // 128
    *dkvs, branch, early = lax.optimization_barrier((*dkvs, branch, early))
    joined = jnp.concatenate([total[part] for part in range(2) for total in dkvs], axis=1)
    slices = jnp.stack([joined[:, i * half:(i + 1) * half] for i in range(4)])
    slices = lax.all_to_all(slices, GROUP, 0, 0, tiled=True)
    late = late_grads(places, normed, *normed_others, slices, early)

    dnormed = dot(dq, proj_in[:, :inner], NT)
    for g, total in enumerate(lax.optimization_barrier((*dkvs, late))[:GROUPS]):
        lo, size = (inner + starts[g], GROUP_LANES[g])
        dnormed = dnormed + (
            dot(total[0], proj_in[:, lo:lo + size], NT)
            + dot(total[1], proj_in[:, inner + lo:inner + lo + size], NT)
        )
    gain_gradient = jnp.sum(dnormed * xhat, axis=0)
    late = lax.all_to_all(late.reshape(N_PAIR, -1, 128), PAIRS, 0, 0, tiled=True)


    centred = dnormed * layer_norm_gain
    input_gradient = inverse_deviation * (
        centred
        - jnp.mean(centred, axis=-1, keepdims=True)
        - xhat * jnp.mean(centred * xhat, axis=-1, keepdims=True)
    )
    branch_grad = input_gradient.astype(bf16)

    late, branch, branch_grad, gain_gradient = lax.optimization_barrier(
        (late, branch, branch_grad, gain_gradient)
    )
    share = jnp.sum(late.astype(f32), axis=0)
    rows = width // 128
    summands = jnp.full((16 - rows, 128), square_sum(share), f32)
    summands = butterfly(jnp.concatenate([gain_gradient.reshape(rows, 128), summands], axis=0))
    gain = summands[:rows].reshape(-1)
    total_sq = summands[rows, 0] + square_sum(gain)
    count = width * 3 * inner + inner * width + width
    factor = 1.0 / jnp.maximum(jnp.sqrt(total_sq / count), 1.0)

    span = blocks * SPAN
    share_q = unpacked(share[:span])
    rows = SPAN // 2
    mine, other = swapped(share_q[:rows], share_q[rows:])
    full_q = [jnp.where(is_low, mine, other), jnp.where(is_low, other, mine)]
    share_out = unpacked(share[span:2 * span]).reshape(4, SPAN // 4, half)
    share_kv = jnp.concatenate([unpacked(share[2 * span:3 * span]), unpacked(share[3 * span:])], axis=0)
    parts = jnp.concatenate([share_kv.reshape(4, rows, half), share_out], axis=1)
    parts = parts.reshape(2, 2, rows + SPAN // 4, half)
    mine, other = swapped(parts[:, 0], parts[:, 1])
    parts = jnp.stack([jnp.where(is_low, mine, other), jnp.where(is_low, other, mine)], axis=1)
    low_z = zl == 0
    mine, other = (jnp.where(low_z, parts[0], parts[1]), jnp.where(low_z, parts[1], parts[0]))
    other = to_pair(other)
    parts = jnp.stack([jnp.where(low_z, mine, other), jnp.where(low_z, other, mine)])
    parts = [parts[i // 2, i % 2] for i in range(4)]
    full_in = jnp.concatenate(full_q + [part[:rows] for part in parts], axis=1)
    full_out = jnp.concatenate([part[rows:] for part in parts], axis=1)
    rows = SPAN // 2
    gain_own = lax.dynamic_slice(gain, ((chip_at * 2 + core) * rows,), (rows,))
    return (
        branch[None, None],
        branch_grad[None, None],
        factor * full_in,
        factor * full_out,
        factor * gain_own,
    )


def solution(mesh):
    fine = Mesh(mesh.devices.reshape(SIZES), AXES)
    row, col = (("x", "zh"), ("y", "zl", "core"))
    in_specs = (
        P(row, col, None, None),
        P(),
        P(),
        P(),
        P(),
        P(row, col),
        P(row, col, None, None),
    )
    out_specs = (
        P(row, col, None, None),
        P(row, col, None, None),
        P(AXES, None),
        P(AXES, None),
        P(AXES),
    )
    return jax.shard_map(local, mesh=fine, in_specs=in_specs, out_specs=out_specs, check_vma=False)
```

```python
import jax
import jax.numpy as jnp
from jax import lax
from jax.experimental import pallas as pl
from jax.experimental.pallas import tpu as pltpu
from jax.sharding import Mesh
from jax.sharding import PartitionSpec as P

HEAD_DIM = 64
REGION = 3
RADIUS = 3
EPSILON = 1e-05
NEG_BIG = -1e30
GROUPS = 3

AXES = ("x", "zh", "y", "zl", "core")
CHIPS = ("x", "zh", "y", "zl")
SIZES = (4, 2, 4, 2, 2)
ROWS, COLS = 8, 16
N_CHIP = 64
SPAN = 24

NN = (((1,), (0,)), ((), ()))
NT = (((1,), (1,)), ((), ()))
TN = (((0,), (0,)), ((), ()))
f32 = jnp.float32
bf16 = jnp.bfloat16


def dot(a, b, dims=NN):
    return lax.dot_general(a, b, dims, preferred_element_type=f32)


def routes(move):
    index = lambda p: (((p[0] * 2 + p[1]) * 4 + p[2]) * 2 + p[3]) * 2 + p[4]
    places = [(x, zh, y, zl, c) for x in range(4) for zh in range(2)
              for y in range(4) for zl in range(2) for c in range(2)]
    pairs = [(p, move(*p)) for p in places]
    return [(index(p), index(t)) for p, t in pairs if 0 <= t[0] < 4 and 0 <= t[2] < 4]


def third_column(x, zh, y, zl, c):
    if c == zl:
        return (x, zh, y, zl, 1 - c)
    return (x, zh, y + 1 - 2 * zl, zl, 1 - c)


OTHER_ROW = routes(lambda x, zh, y, zl, c: (x, 1 - zh, y, zl, c))
OTHER_COL = routes(lambda x, zh, y, zl, c: (x, zh, y, 1 - zl, c))
OTHER_BOTH = routes(lambda x, zh, y, zl, c: (x, 1 - zh, y, 1 - zl, c))
BEYOND_ROW = routes(lambda x, zh, y, zl, c: (x + 1 - 2 * zh, zh, y, zl, c))
THIRD_COL = routes(third_column)


def after(value, *others):
    return lax.optimization_barrier((value,) + others)[0]


def move(value, route, back=False):
    return lax.ppermute(value, AXES, [(t, f) for f, t in route] if back else route)


def to_sibling(value):
    return lax.ppermute(value, "core", [(0, 1), (1, 0)])


def apply_layer_norm(block):
    values = block.astype(f32)
    centred = values - jnp.mean(values, axis=-1, keepdims=True)
    inverse_deviation = lax.rsqrt(jnp.mean(centred * centred, axis=-1, keepdims=True) + EPSILON)
    return (centred * inverse_deviation, inverse_deviation)


def geometry(tissue, row_at, col_at, slot):
    padded = jnp.pad(tissue, REGION)
    window = lax.dynamic_slice(padded, (row_at * REGION, col_at * REGION), (3 * REGION, 3 * REGION))
    blocks = window.reshape(3, REGION, 3, REGION)
    occupied = jnp.sum(blocks, axis=(1, 3))
    inner = jnp.arange(REGION, dtype=jnp.int32)
    row_in = jnp.sum(blocks * inner[None, :, None, None], axis=(1, 3))
    col_in = jnp.sum(blocks * inner[None, None, None, :], axis=(1, 3))
    three = jnp.arange(3, dtype=jnp.int32)
    key_row = (row_at - 1 + three)[:, None] * REGION + row_in
    key_col = (col_at - 1 + three)[None, :] * REGION + col_in
    query_row = row_at * REGION + slot // REGION
    query_col = col_at * REGION + slot % REGION
    present = lax.dynamic_slice(tissue, (query_row, query_col), (1, 1))[0, 0]
    inside = (
        (jnp.abs(key_row - query_row) <= RADIUS)
        & (jnp.abs(key_col - query_col) <= RADIUS)
        & (occupied > 0)
    )
    centre = (three[:, None] == 1) & (three[None, :] == 1)
    return ((inside | centre).astype(jnp.int32), present)


def attend_kernel(allow_ref, q_ref, g_ref, own_ref, side_ref, third_ref,
                  out_ref, dq_ref, down_ref, dside_ref, dthird_ref, s_scr, dp_scr):
    tile_len = q_ref.shape[0]
    kv_refs = (own_ref, side_ref, third_ref)
    dkv_refs = (down_ref, dside_ref, dthird_ref)
    places = [(a, b) for b in range(3) for a in range(3)]
    first = lax.broadcasted_iota(jnp.int32, (tile_len, 2 * HEAD_DIM), 1) < HEAD_DIM

    def head_pair(v):
        zero = jnp.zeros_like(v)
        return jnp.concatenate([jnp.where(first, v, zero), jnp.where(first, zero, v)], axis=0)

    qq = head_pair(q_ref[...] * jnp.asarray(HEAD_DIM ** -0.5, bf16))
    gg = head_pair(g_ref[...])
    top = jnp.full((1, 2 * tile_len), NEG_BIG, f32)
    for i, (a, b) in enumerate(places):
        scores = dot(kv_refs[b][a, 0], qq, NT)
        scores = jnp.where(allow_ref[b * 3 + a] > 0, scores, NEG_BIG)
        s_scr[i] = scores
        top = jnp.maximum(top, jnp.max(scores, axis=0, keepdims=True))
    total = jnp.zeros((1, 2 * tile_len), f32)
    mix = jnp.zeros((1, 2 * tile_len), f32)
    for i, (a, b) in enumerate(places):
        weights = jnp.exp(s_scr[i] - top)
        dprobs = dot(kv_refs[b][a, 1], gg, NT)
        total = total + jnp.sum(weights, axis=0, keepdims=True)
        mix = mix + jnp.sum(dprobs * weights, axis=0, keepdims=True)
        s_scr[i] = weights
        dp_scr[i] = dprobs
    inverse = 1.0 / total
    mix = mix * inverse
    outs = [jnp.zeros((HEAD_DIM, tile_len), f32)] * 2
    dqs = [jnp.zeros((HEAD_DIM, tile_len), f32)] * 2
    for i, (a, b) in enumerate(places):
        probs = s_scr[i] * inverse
        probs_b = probs.astype(bf16)
        dscores = (probs * (dp_scr[i] - mix)).astype(bf16)
        dkv_refs[b][a, 1] = dot(probs_b, gg).astype(bf16)
        dkv_refs[b][a, 0] = dot(dscores, qq).astype(bf16)
        keys_t = kv_refs[b][a, 0].T
        vals_t = kv_refs[b][a, 1].T
        for h in range(2):
            part = slice(h * HEAD_DIM, (h + 1) * HEAD_DIM)
            lanes = slice(h * tile_len, (h + 1) * tile_len)
            outs[h] = outs[h] + dot(vals_t[part], probs_b[:, lanes])
            dqs[h] = dqs[h] + dot(keys_t[part], dscores[:, lanes])
    out_ref[...] = jnp.concatenate(outs, axis=0).T.astype(bf16)
    dq_ref[...] = (jnp.concatenate(dqs, axis=0).T * HEAD_DIM ** -0.5).astype(bf16)


def attend(allowed, qkv, dattn, own, side, third, group):
    tile_len, width = (own.shape[2], own.shape[3])
    block = 2 * HEAD_DIM
    steps = width // block
    place = lambda h: (0, h + group * steps)
    near = lambda h: (0, 0, 0, h)
    kv_spec = pl.BlockSpec((3, 2, tile_len, block), near)
    row_spec = pl.BlockSpec((tile_len, block), lambda h: (0, h))
    row_shape = jax.ShapeDtypeStruct((tile_len, width), bf16)
    kv_shape = jax.ShapeDtypeStruct(own.shape, bf16)
    scratch = pltpu.VMEM((9, tile_len, 2 * tile_len), f32)
    return pl.pallas_call(
        attend_kernel,
        grid=(steps,),
        in_specs=[
            pl.BlockSpec(memory_space=pltpu.SMEM),
            pl.BlockSpec((tile_len, block), place),
            pl.BlockSpec((tile_len, block), place),
            kv_spec, kv_spec, kv_spec,
        ],
        out_specs=[row_spec, row_spec, kv_spec, kv_spec, kv_spec],
        out_shape=[row_shape, row_shape, kv_shape, kv_shape, kv_shape],
        scratch_shapes=[scratch, scratch],
        compiler_params=pltpu.CompilerParams(vmem_limit_bytes=40 * 1024 * 1024),
        cost_estimate=pl.CostEstimate(
            flops=width * tile_len * tile_len * 9 * 12 * 4,
            bytes_accessed=width * tile_len * 2 * 40,
            transcendentals=width // HEAD_DIM * tile_len * tile_len * 9,
        ),
    )(allowed, qkv, dattn, own, side, third)


def grad_blocks(left_a, left_b, right_a, right_b, first, last):
    lanes = slice(first, last)
    grad = dot(left_a[:, lanes], right_a[...], TN) + dot(left_b[:, lanes], right_b[...], TN)
    return grad.astype(bf16)


def early_kernel(normed_a, normed_b, dq_a, dq_b, attn_a, attn_b, dy_a, dy_b, out_ref):
    step = 16 * SPAN
    blocks = dq_a.shape[1] // 128
    for r in range(normed_a.shape[1] // step):
        grad = grad_blocks(normed_a, normed_b, dq_a, dq_b, r * step, (r + 1) * step)
        for j in range(blocks):
            part = grad[:, j * 128:(j + 1) * 128].reshape(16, SPAN, 128)
            out_ref[r * 16:(r + 1) * 16, j] = part
    for r in range(attn_a.shape[1] // step):
        grad = grad_blocks(attn_a, attn_b, dy_a, dy_b, r * step, (r + 1) * step)
        for i in range(16):
            for q in range(2):
                for j in range(blocks):
                    col = (q * blocks + j) * 128
                    out_ref[2 * (r * 16 + i) + q, blocks + j] = grad[i * SPAN:(i + 1) * SPAN, col:col + 128]


def early_grads(*operands):
    blocks = operands[2].shape[1] // 128
    return pl.pallas_call(
        early_kernel,
        out_shape=jax.ShapeDtypeStruct((N_CHIP, 2 * blocks, SPAN, 128), bf16),
        compiler_params=pltpu.CompilerParams(vmem_limit_bytes=32 * 1024 * 1024),
        cost_estimate=pl.CostEstimate(flops=1000000, bytes_accessed=1000000, transcendentals=0),
    )(*operands)


def late_kernel(normed_a, normed_b, *refs):
    step = 16 * SPAN
    out_ref = refs[-1]
    for g in range(len(refs) // 2):
        dkv_a, dkv_b = refs[2 * g:2 * g + 2]
        blocks = dkv_a.shape[1] // 128
        for r in range(normed_a.shape[1] // step):
            grad = grad_blocks(normed_a, normed_b, dkv_a, dkv_b, r * step, (r + 1) * step)
            for j in range(blocks):
                part = grad[:, j * 128:(j + 1) * 128].reshape(16, SPAN, 128)
                out_ref[r * 16:(r + 1) * 16, g * blocks + j] = part


def late_grads(*operands):
    blocks = sum(d.shape[1] for d in operands[2::2]) // 128
    return pl.pallas_call(
        late_kernel,
        out_shape=jax.ShapeDtypeStruct((N_CHIP, blocks, SPAN, 128), bf16),
        compiler_params=pltpu.CompilerParams(vmem_limit_bytes=32 * 1024 * 1024),
        cost_estimate=pl.CostEstimate(flops=1000000, bytes_accessed=1000000, transcendentals=0),
    )(*operands)


def exchanged(value):
    return lax.all_to_all(value.reshape(N_CHIP, -1, 128), CHIPS, 0, 0, tiled=True)


def butterfly(value):
    for bit in range(7):
        value = value + lax.ppermute(value, AXES, [(i, i ^ (1 << bit)) for i in range(ROWS * COLS)])
    return value


def unpacked(share):
    count = share.shape[0] // SPAN
    return share.reshape(count, SPAN, 128).transpose(1, 0, 2).reshape(SPAN, count * 128)


def square_sum(value):
    return jnp.sum(value * value)


def local(tokens, layer_norm_gain, proj_in, proj_out, tissue, tile_slot, cotangent):
    chip_at = lax.axis_index(CHIPS)
    core = lax.axis_index("core")
    zh = lax.axis_index("zh")
    row_at = chip_at // (COLS // 2)
    col_at = (chip_at % (COLS // 2)) * 2 + core
    tile_len, width = tokens.shape[2:]
    inner = proj_out.shape[0]
    half = inner // 2
    is_low = core == 0

    def swapped(lower, upper):
        mine, other = (jnp.where(is_low, lower, upper), jnp.where(is_low, upper, lower))
        return (mine, to_sibling(other))

    xhat, inverse_deviation = apply_layer_norm(tokens[0, 0])
    normed = (xhat * layer_norm_gain).astype(bf16)
    size = inner // GROUPS
    qkv = dot(normed, proj_in).astype(bf16)

    def gather_block(g, *others):
        lo = inner + g * size
        own = jnp.stack([qkv[:, lo:lo + size], qkv[:, inner + lo:inner + lo + size]])
        if others:
            own = after(own, *others)
        return (own, move(own, OTHER_ROW), move(own, OTHER_COL), move(own, OTHER_BOTH))

    stages = []
    for g in range(GROUPS):
        others = []
        if g >= 1:
            others += stages[g - 1]["block"][1:]
        if g >= 2:
            others.append(stages[g - 2]["beyond"])
        own, row, col, both = gather_block(g, *others)
        outer = jnp.stack([row, both])
        if g >= 1:
            outer = after(outer, stages[g - 1]["own_col"], stages[g - 1]["other_col"])
        beyond = move(outer, BEYOND_ROW)
        stages.append(dict(block=(own, row, col, both), outer=outer, beyond=beyond,
                           own_col=jnp.stack([own, row, beyond[0]]),
                           other_col=jnp.stack([col, both, beyond[1]])))

    allowed, present = geometry(tissue, row_at, col_at, tile_slot[0, 0])
    first_row = zh == 0
    allowed = jnp.stack([
        allowed[1],
        jnp.where(first_row, allowed[2], allowed[0]),
        jnp.where(first_row, allowed[0], allowed[2]),
    ])
    allowed = jnp.concatenate([
        allowed[:, 1],
        jnp.where(is_low, allowed[:, 2], allowed[:, 0]),
        jnp.where(is_low, allowed[:, 0], allowed[:, 2]),
    ])
    cot_block = cotangent[0, 0]
    dy = jnp.where(present > 0, cot_block, jnp.zeros_like(cot_block))
    dattn = dot(dy, proj_out, NT).astype(bf16)
    outs, dqs, backs, early = ([], [], [], [])
    for g in range(GROUPS):
        own_col, other_col = (stages[g]["own_col"], stages[g]["other_col"])
        side_col, third_col = (to_sibling(own_col), move(other_col, THIRD_COL))
        first = []
        if g + 2 < GROUPS:
            first.append(stages[g + 2]["outer"])
        if g + 1 < GROUPS:
            first += [stages[g + 1]["own_col"], stages[g + 1]["other_col"]]
        if g >= 2:
            first.append(backs[g - 2][3])
        if g == GROUPS - 1:
            first += early
        own_col, side_col, third_col = lax.optimization_barrier((own_col, side_col, third_col, *first))[:3]
        out, dq, down, dside, dthird = attend(allowed, qkv, dattn, own_col, side_col, third_col, g)
        if g == 0:
            normed_side = to_sibling(after(normed, out))
            dy_mine, dy_side = swapped(
                jnp.concatenate([dy[:, :half], dy[:, inner:inner + half]], axis=1),
                after(jnp.concatenate([dy[:, half:inner], dy[:, inner + half:]], axis=1), out),
            )
            early += [normed_side, dy_side]
        side = to_sibling(dside)
        third = move(dthird, THIRD_COL, back=True)
        column = down.astype(f32) + side.astype(f32)
        outer = jnp.stack([column[2].astype(bf16), third[2]])
        outs.append(out)
        dqs.append(dq)
        backs.append((column, third, down, outer))
    attn = jnp.concatenate(outs, axis=1)
    dq = jnp.concatenate(dqs, axis=1)
    last = backs[-1][3]
    early = early_grads(
        normed, normed_side, *swapped(dq[:, :half], dq[:, half:]), attn, to_sibling(attn), dy_mine,
        after(dy_side, last),
    )
    dkvs = []
    for g, (column, third, _, outer) in enumerate(backs):
        beyond = move(outer, BEYOND_ROW, back=True).astype(f32)
        row = (column[1] + beyond[0]).astype(bf16)
        both = (third[1].astype(f32) + beyond[1]).astype(bf16)
        col = third[0]
        if g == GROUPS - 1:
            row, both, col = lax.optimization_barrier((row, both, col, early))[:3]
        elif g == GROUPS - 2:
            row, both, col = lax.optimization_barrier((row, both, col, last))[:3]
        row = move(row, OTHER_ROW)
        both = move(both, OTHER_BOTH)
        col = move(col, OTHER_COL)
        total = column[0] + row.astype(f32) + both.astype(f32) + col.astype(f32)
        dkvs.append(total.astype(bf16))

    branch = dot(attn, proj_out)
    branch = jnp.where(present > 0, branch, jnp.zeros_like(branch)).astype(bf16)
    early = exchanged(early)
    blocks = half // 128
    *dkvs, early = lax.optimization_barrier((*dkvs, early))
    pairs = [part for total in dkvs for part in swapped(total[0], total[1])]
    late = late_grads(normed, normed_side, *pairs)
    early = after(early, late)
    early = jnp.sum(early.astype(f32), axis=0)
    share_q = unpacked(early[:blocks * SPAN])
    share_out = unpacked(early[blocks * SPAN:])
    dnormed = dot(dq, proj_in[:, :inner], NT)
    for g, total in enumerate(lax.optimization_barrier((*dkvs, late))[:GROUPS]):
        lo = inner + g * size
        dnormed = dnormed + (
            dot(total[0], proj_in[:, lo:lo + size], NT)
            + dot(total[1], proj_in[:, inner + lo:inner + lo + size], NT)
        )
    gain_gradient = jnp.sum(dnormed * xhat, axis=0)
    late = exchanged(late)


    centred = dnormed * layer_norm_gain
    input_gradient = inverse_deviation * (
        centred
        - jnp.mean(centred, axis=-1, keepdims=True)
        - xhat * jnp.mean(centred * xhat, axis=-1, keepdims=True)
    )
    branch_grad = input_gradient.astype(bf16)

    def own_rows(value):
        rows = value.shape[0] // 2
        mine, other = swapped(value[:rows], value[rows:])
        return [jnp.where(is_low, mine, other), jnp.where(is_low, other, mine)]

    rows = share_out.shape[0] // 4
    low_z = lax.axis_index("zl") == 0
    parts = share_out.reshape(2, 2, rows, half)
    mine, other = swapped(parts[:, 0], parts[:, 1])
    parts = jnp.stack([jnp.where(is_low, mine, other), jnp.where(is_low, other, mine)], axis=1)
    mine, other = (jnp.where(low_z, parts[0], parts[1]), jnp.where(low_z, parts[1], parts[0]))
    other = lax.ppermute(other, "zl", [(0, 1), (1, 0)])
    moved = jnp.stack([jnp.where(low_z, mine, other), jnp.where(low_z, other, mine)])
    full_out = moved.transpose(2, 0, 1, 3).reshape(rows, 4 * half)
    full_q = own_rows(share_q)
    early_sq = square_sum(share_q) + square_sum(share_out)
    late, branch, branch_grad, full_out, early_sq, gain_gradient, *full_q = lax.optimization_barrier(
        (late, branch, branch_grad, full_out, early_sq, gain_gradient, *full_q)
    )
    late = jnp.sum(late.astype(f32), axis=0)
    share_kv = unpacked(late)
    rows = width // 128
    summands = jnp.full((16 - rows, 128), early_sq + square_sum(share_kv), f32)
    summands = butterfly(jnp.concatenate([gain_gradient.reshape(rows, 128), summands], axis=0))
    gain = summands[:rows].reshape(-1)
    total_sq = summands[rows, 0] + square_sum(gain)
    count = width * 3 * inner + inner * width + width
    factor = 1.0 / jnp.maximum(jnp.sqrt(total_sq / count), 1.0)

    full_in = jnp.concatenate(full_q + own_rows(share_kv), axis=1)
    rows = SPAN // 2
    gain_own = lax.dynamic_slice(gain, ((chip_at * 2 + core) * rows,), (rows,))
    return (
        branch[None, None],
        branch_grad[None, None],
        factor * full_in,
        factor * full_out,
        factor * gain_own,
    )


def solution(mesh):
    fine = Mesh(mesh.devices.reshape(SIZES), AXES)
    row, col = (("x", "zh"), ("y", "zl", "core"))
    in_specs = (
        P(row, col, None, None),
        P(),
        P(),
        P(),
        P(),
        P(row, col),
        P(row, col, None, None),
    )
    out_specs = (
        P(row, col, None, None),
        P(row, col, None, None),
        P(AXES, None),
        P(AXES, None),
        P(AXES),
    )
    return jax.shard_map(local, mesh=fine, in_specs=in_specs, out_specs=out_specs, check_vma=False)
```

```python
import jax
import jax.numpy as jnp
from jax import lax
from jax.experimental import pallas as pl
from jax.experimental.pallas import tpu as pltpu
from jax.sharding import Mesh
from jax.sharding import PartitionSpec as P

HEAD_DIM = 64
REGION = 3
RADIUS = 3
EPSILON = 1e-05
NEG_BIG = -1e30
GROUPS = 3

AXES = ("x", "zh", "y", "zl", "core")
CHIPS = ("x", "zh", "y", "zl")
SIZES = (4, 2, 4, 2, 2)
ROWS, COLS = 8, 16
N_CHIP = 64
SPAN = 24

NN = (((1,), (0,)), ((), ()))
NT = (((1,), (1,)), ((), ()))
TN = (((0,), (0,)), ((), ()))
f32 = jnp.float32
bf16 = jnp.bfloat16


def dot(a, b, dims=NN):
    return lax.dot_general(a, b, dims, preferred_element_type=f32)


def routes(move):
    index = lambda p: (((p[0] * 2 + p[1]) * 4 + p[2]) * 2 + p[3]) * 2 + p[4]
    places = [(x, zh, y, zl, c) for x in range(4) for zh in range(2)
              for y in range(4) for zl in range(2) for c in range(2)]
    pairs = [(p, move(*p)) for p in places]
    return [(index(p), index(t)) for p, t in pairs if 0 <= t[0] < 4 and 0 <= t[2] < 4]


def third_column(x, zh, y, zl, c):
    if c == zl:
        return (x, zh, y, zl, 1 - c)
    return (x, zh, y + 1 - 2 * zl, zl, 1 - c)


OTHER_ROW = routes(lambda x, zh, y, zl, c: (x, 1 - zh, y, zl, c))
OTHER_COL = routes(lambda x, zh, y, zl, c: (x, zh, y, 1 - zl, c))
OTHER_BOTH = routes(lambda x, zh, y, zl, c: (x, 1 - zh, y, 1 - zl, c))
BEYOND_ROW = routes(lambda x, zh, y, zl, c: (x + 1 - 2 * zh, zh, y, zl, c))
THIRD_COL = routes(third_column)


def after(value, *others):
    return lax.optimization_barrier((value,) + others)[0]


def move(value, route, back=False):
    return lax.ppermute(value, AXES, [(t, f) for f, t in route] if back else route)


def to_sibling(value):
    return lax.ppermute(value, "core", [(0, 1), (1, 0)])


def apply_layer_norm(block):
    values = block.astype(f32)
    centred = values - jnp.mean(values, axis=-1, keepdims=True)
    inverse_deviation = lax.rsqrt(jnp.mean(centred * centred, axis=-1, keepdims=True) + EPSILON)
    return (centred * inverse_deviation, inverse_deviation)


def geometry(tissue, row_at, col_at, slot):
    padded = jnp.pad(tissue, REGION)
    window = lax.dynamic_slice(padded, (row_at * REGION, col_at * REGION), (3 * REGION, 3 * REGION))
    blocks = window.reshape(3, REGION, 3, REGION)
    occupied = jnp.sum(blocks, axis=(1, 3))
    inner = jnp.arange(REGION, dtype=jnp.int32)
    row_in = jnp.sum(blocks * inner[None, :, None, None], axis=(1, 3))
    col_in = jnp.sum(blocks * inner[None, None, None, :], axis=(1, 3))
    three = jnp.arange(3, dtype=jnp.int32)
    key_row = (row_at - 1 + three)[:, None] * REGION + row_in
    key_col = (col_at - 1 + three)[None, :] * REGION + col_in
    query_row = row_at * REGION + slot // REGION
    query_col = col_at * REGION + slot % REGION
    present = lax.dynamic_slice(tissue, (query_row, query_col), (1, 1))[0, 0]
    inside = (
        (jnp.abs(key_row - query_row) <= RADIUS)
        & (jnp.abs(key_col - query_col) <= RADIUS)
        & (occupied > 0)
    )
    centre = (three[:, None] == 1) & (three[None, :] == 1)
    return ((inside | centre).astype(jnp.int32), present)


def attend_kernel(allow_ref, q_ref, g_ref, own_ref, side_ref, third_ref,
                  out_ref, dq_ref, down_ref, dside_ref, dthird_ref, s_scr, dp_scr):
    tile_len = q_ref.shape[0]
    kv_refs = (own_ref, side_ref, third_ref)
    dkv_refs = (down_ref, dside_ref, dthird_ref)
    places = [(a, b) for b in range(3) for a in range(3)]
    first = lax.broadcasted_iota(jnp.int32, (tile_len, 2 * HEAD_DIM), 1) < HEAD_DIM

    def head_pair(v):
        zero = jnp.zeros_like(v)
        return jnp.concatenate([jnp.where(first, v, zero), jnp.where(first, zero, v)], axis=0)

    qq = head_pair(q_ref[...] * jnp.asarray(HEAD_DIM ** -0.5, bf16))
    gg = head_pair(g_ref[...])
    top = jnp.full((1, 2 * tile_len), NEG_BIG, f32)
    for i, (a, b) in enumerate(places):
        scores = dot(kv_refs[b][a, 0], qq, NT)
        scores = jnp.where(allow_ref[b * 3 + a] > 0, scores, NEG_BIG)
        s_scr[i] = scores
        top = jnp.maximum(top, jnp.max(scores, axis=0, keepdims=True))
    total = jnp.zeros((1, 2 * tile_len), f32)
    mix = jnp.zeros((1, 2 * tile_len), f32)
    for i, (a, b) in enumerate(places):
        weights = jnp.exp(s_scr[i] - top)
        dprobs = dot(kv_refs[b][a, 1], gg, NT)
        total = total + jnp.sum(weights, axis=0, keepdims=True)
        mix = mix + jnp.sum(dprobs * weights, axis=0, keepdims=True)
        s_scr[i] = weights
        dp_scr[i] = dprobs
    inverse = 1.0 / total
    mix = mix * inverse
    outs = [jnp.zeros((HEAD_DIM, tile_len), f32)] * 2
    dqs = [jnp.zeros((HEAD_DIM, tile_len), f32)] * 2
    for i, (a, b) in enumerate(places):
        probs = s_scr[i] * inverse
        probs_b = probs.astype(bf16)
        dscores = (probs * (dp_scr[i] - mix)).astype(bf16)
        dkv_refs[b][a, 1] = dot(probs_b, gg).astype(bf16)
        dkv_refs[b][a, 0] = dot(dscores, qq).astype(bf16)
        keys_t = kv_refs[b][a, 0].T
        vals_t = kv_refs[b][a, 1].T
        for h in range(2):
            part = slice(h * HEAD_DIM, (h + 1) * HEAD_DIM)
            lanes = slice(h * tile_len, (h + 1) * tile_len)
            outs[h] = outs[h] + dot(vals_t[part], probs_b[:, lanes])
            dqs[h] = dqs[h] + dot(keys_t[part], dscores[:, lanes])
    out_ref[...] = jnp.concatenate(outs, axis=0).T.astype(bf16)
    dq_ref[...] = (jnp.concatenate(dqs, axis=0).T * HEAD_DIM ** -0.5).astype(bf16)


def attend(allowed, qkv, dattn, own, side, third, group):
    tile_len, width = (own.shape[2], own.shape[3])
    block = 2 * HEAD_DIM
    steps = width // block
    place = lambda h: (0, h + group * steps)
    near = lambda h: (0, 0, 0, h)
    kv_spec = pl.BlockSpec((3, 2, tile_len, block), near)
    row_spec = pl.BlockSpec((tile_len, block), lambda h: (0, h))
    row_shape = jax.ShapeDtypeStruct((tile_len, width), bf16)
    kv_shape = jax.ShapeDtypeStruct(own.shape, bf16)
    scratch = pltpu.VMEM((9, tile_len, 2 * tile_len), f32)
    return pl.pallas_call(
        attend_kernel,
        grid=(steps,),
        in_specs=[
            pl.BlockSpec(memory_space=pltpu.SMEM),
            pl.BlockSpec((tile_len, block), place),
            pl.BlockSpec((tile_len, block), place),
            kv_spec, kv_spec, kv_spec,
        ],
        out_specs=[row_spec, row_spec, kv_spec, kv_spec, kv_spec],
        out_shape=[row_shape, row_shape, kv_shape, kv_shape, kv_shape],
        scratch_shapes=[scratch, scratch],
        compiler_params=pltpu.CompilerParams(vmem_limit_bytes=40 * 1024 * 1024),
        cost_estimate=pl.CostEstimate(
            flops=width * tile_len * tile_len * 9 * 12 * 4,
            bytes_accessed=width * tile_len * 2 * 40,
            transcendentals=width // HEAD_DIM * tile_len * tile_len * 9,
        ),
    )(allowed, qkv, dattn, own, side, third)


def grad_blocks(left_a, left_b, right_a, right_b, first, last):
    lanes = slice(first, last)
    grad = dot(left_a[:, lanes], right_a[...], TN) + dot(left_b[:, lanes], right_b[...], TN)
    return grad.astype(bf16)


def early_kernel(normed_a, normed_b, dq_a, dq_b, attn_a, attn_b, dy_a, dy_b, out_ref):
    step = 16 * SPAN
    blocks = dq_a.shape[1] // 128
    for r in range(normed_a.shape[1] // step):
        grad = grad_blocks(normed_a, normed_b, dq_a, dq_b, r * step, (r + 1) * step)
        for j in range(blocks):
            part = grad[:, j * 128:(j + 1) * 128].reshape(16, SPAN, 128)
            out_ref[r * 16:(r + 1) * 16, j] = part
    for r in range(attn_a.shape[1] // step):
        grad = grad_blocks(attn_a, attn_b, dy_a, dy_b, r * step, (r + 1) * step)
        for i in range(16):
            for q in range(2):
                for j in range(blocks):
                    col = (q * blocks + j) * 128
                    out_ref[2 * (r * 16 + i) + q, blocks + j] = grad[i * SPAN:(i + 1) * SPAN, col:col + 128]


def early_grads(*operands):
    blocks = operands[2].shape[1] // 128
    return pl.pallas_call(
        early_kernel,
        out_shape=jax.ShapeDtypeStruct((N_CHIP, 2 * blocks, SPAN, 128), bf16),
        compiler_params=pltpu.CompilerParams(vmem_limit_bytes=32 * 1024 * 1024),
    )(*operands)


def late_kernel(early_ref, normed_a, normed_b, *refs):
    step = 16 * SPAN
    out_ref = refs[-1]
    done = early_ref.shape[1]
    out_ref[:, :done] = early_ref[...]
    for g in range(len(refs) // 2):
        dkv_a, dkv_b = refs[2 * g:2 * g + 2]
        blocks = dkv_a.shape[1] // 128
        for r in range(normed_a.shape[1] // step):
            grad = grad_blocks(normed_a, normed_b, dkv_a, dkv_b, r * step, (r + 1) * step)
            for j in range(blocks):
                part = grad[:, j * 128:(j + 1) * 128].reshape(16, SPAN, 128)
                out_ref[r * 16:(r + 1) * 16, done + g * blocks + j] = part


def late_grads(*operands):
    blocks = operands[0].shape[1] + sum(d.shape[1] for d in operands[3::2]) // 128
    return pl.pallas_call(
        late_kernel,
        out_shape=jax.ShapeDtypeStruct((N_CHIP, blocks, SPAN, 128), bf16),
        compiler_params=pltpu.CompilerParams(vmem_limit_bytes=32 * 1024 * 1024),
    )(*operands)


def exchanged(value):
    return lax.all_to_all(value.reshape(N_CHIP, -1, 128), CHIPS, 0, 0, tiled=True)


def butterfly(value):
    for bit in range(7):
        value = value + lax.ppermute(value, AXES, [(i, i ^ (1 << bit)) for i in range(ROWS * COLS)])
    return value


def unpacked(share):
    count = share.shape[0] // SPAN
    return share.reshape(count, SPAN, 128).transpose(1, 0, 2).reshape(SPAN, count * 128)


def square_sum(value):
    return jnp.sum(value * value)


def local(tokens, layer_norm_gain, proj_in, proj_out, tissue, tile_slot, cotangent):
    chip_at = lax.axis_index(CHIPS)
    core = lax.axis_index("core")
    zh = lax.axis_index("zh")
    row_at = chip_at // (COLS // 2)
    col_at = (chip_at % (COLS // 2)) * 2 + core
    tile_len, width = tokens.shape[2:]
    inner = proj_out.shape[0]
    half = inner // 2
    is_low = core == 0

    def swapped(lower, upper):
        mine, other = (jnp.where(is_low, lower, upper), jnp.where(is_low, upper, lower))
        return (mine, to_sibling(other))

    xhat, inverse_deviation = apply_layer_norm(tokens[0, 0])
    normed = (xhat * layer_norm_gain).astype(bf16)
    size = inner // GROUPS
    qkv = dot(normed, proj_in).astype(bf16)

    def gather_block(g, *others):
        lo = inner + g * size
        own = jnp.stack([qkv[:, lo:lo + size], qkv[:, inner + lo:inner + lo + size]])
        if others:
            own = after(own, *others)
        return (own, move(own, OTHER_ROW), move(own, OTHER_COL), move(own, OTHER_BOTH))

    stages = []
    for g in range(GROUPS):
        others = []
        if g >= 1:
            others += stages[g - 1]["block"][1:]
        if g >= 2:
            others.append(stages[g - 2]["beyond"])
        own, row, col, both = gather_block(g, *others)
        outer = jnp.stack([row, both])
        beyond = move(outer, BEYOND_ROW)
        stages.append(dict(block=(own, row, col, both), outer=outer, beyond=beyond,
                           own_col=jnp.stack([own, row, beyond[0]]),
                           other_col=jnp.stack([col, both, beyond[1]])))

    allowed, present = geometry(tissue, row_at, col_at, tile_slot[0, 0])
    first_row = zh == 0
    allowed = jnp.stack([
        allowed[1],
        jnp.where(first_row, allowed[2], allowed[0]),
        jnp.where(first_row, allowed[0], allowed[2]),
    ])
    allowed = jnp.concatenate([
        allowed[:, 1],
        jnp.where(is_low, allowed[:, 2], allowed[:, 0]),
        jnp.where(is_low, allowed[:, 0], allowed[:, 2]),
    ])
    cot_block = cotangent[0, 0]
    dy = jnp.where(present > 0, cot_block, jnp.zeros_like(cot_block))
    dattn = dot(dy, proj_out, NT).astype(bf16)
    outs, dqs, backs, early = ([], [], [], [])
    for g in range(GROUPS):
        own_col, other_col = (stages[g]["own_col"], stages[g]["other_col"])
        side_col, third_col = (to_sibling(own_col), move(other_col, THIRD_COL))
        first = []
        if g + 1 < GROUPS:
            first += [stages[g + 1]["own_col"], stages[g + 1]["other_col"]]
        if g >= 2:
            first.append(backs[g - 2][3])
        own_col, side_col, third_col = lax.optimization_barrier((own_col, side_col, third_col, *first))[:3]
        out, dq, down, dside, dthird = attend(allowed, qkv, dattn, own_col, side_col, third_col, g)
        if g == 0:
            normed_side = to_sibling(after(normed, out))
            dy_mine, dy_side = swapped(
                jnp.concatenate([dy[:, :half], dy[:, inner:inner + half]], axis=1),
                after(jnp.concatenate([dy[:, half:inner], dy[:, inner + half:]], axis=1), out),
            )
            early += [normed_side, dy_side]
        side = to_sibling(dside)
        third = move(dthird, THIRD_COL, back=True)
        column = down.astype(f32) + side.astype(f32)
        outer = jnp.stack([column[2].astype(bf16), third[2]])
        if g == GROUPS - 1:
            outer, normed_side, dy_side = lax.optimization_barrier((outer, normed_side, dy_side))
        outs.append(out)
        dqs.append(dq)
        backs.append((column, third, down, outer))
    dkvs = []
    last = backs[-1][3]
    for g, (column, third, _, outer) in enumerate(backs):
        beyond = move(outer, BEYOND_ROW, back=True).astype(f32)
        row = (column[1] + beyond[0]).astype(bf16)
        both = (third[1].astype(f32) + beyond[1]).astype(bf16)
        col = third[0]
        if g == GROUPS - 2:
            row, both, col = lax.optimization_barrier((row, both, col, last))[:3]
        row = move(row, OTHER_ROW)
        both = move(both, OTHER_BOTH)
        col = move(col, OTHER_COL)
        total = column[0] + row.astype(f32) + both.astype(f32) + col.astype(f32)
        dkvs.append(total.astype(bf16))

    attn = jnp.concatenate(outs, axis=1)
    dq = jnp.concatenate(dqs, axis=1)
    branch = dot(attn, proj_out)
    branch = jnp.where(present > 0, branch, jnp.zeros_like(branch)).astype(bf16)
    early = early_grads(
        normed, normed_side, *swapped(dq[:, :half], dq[:, half:]), attn, to_sibling(attn), dy_mine, dy_side
    )
    *dkvs, early = lax.optimization_barrier((*dkvs, early))
    blocks = half // 128
    pairs = [part for total in dkvs for part in swapped(total[0], total[1])]
    late = late_grads(early, normed, normed_side, *pairs)
    dnormed = dot(dq, proj_in[:, :inner], NT)
    for g, total in enumerate(lax.optimization_barrier((*dkvs, late))[:GROUPS]):
        lo = inner + g * size
        dnormed = dnormed + (
            dot(total[0], proj_in[:, lo:lo + size], NT)
            + dot(total[1], proj_in[:, inner + lo:inner + lo + size], NT)
        )
    gain_gradient = jnp.sum(dnormed * xhat, axis=0)
    late = exchanged(late)


    centred = dnormed * layer_norm_gain
    input_gradient = inverse_deviation * (
        centred
        - jnp.mean(centred, axis=-1, keepdims=True)
        - xhat * jnp.mean(centred * xhat, axis=-1, keepdims=True)
    )
    branch_grad = input_gradient.astype(bf16)

    late, branch, branch_grad, gain_gradient = lax.optimization_barrier(
        (late, branch, branch_grad, gain_gradient)
    )
    share = jnp.sum(late.astype(f32), axis=0)
    share_q = unpacked(share[:blocks * SPAN])
    share_out = unpacked(share[blocks * SPAN:2 * blocks * SPAN])
    share_kv = unpacked(share[2 * blocks * SPAN:])

    def own_rows(value):
        rows = value.shape[0] // 2
        mine, other = swapped(value[:rows], value[rows:])
        return [jnp.where(is_low, mine, other), jnp.where(is_low, other, mine)]

    rows = share_out.shape[0] // 4
    low_z = lax.axis_index("zl") == 0
    parts = share_out.reshape(2, 2, rows, half)
    mine, other = swapped(parts[:, 0], parts[:, 1])
    parts = jnp.stack([jnp.where(is_low, mine, other), jnp.where(is_low, other, mine)], axis=1)
    mine, other = (jnp.where(low_z, parts[0], parts[1]), jnp.where(low_z, parts[1], parts[0]))
    other = lax.ppermute(other, "zl", [(0, 1), (1, 0)])
    moved = jnp.stack([jnp.where(low_z, mine, other), jnp.where(low_z, other, mine)])
    full_out = moved.transpose(2, 0, 1, 3).reshape(rows, 4 * half)
    full_q = own_rows(share_q)
    rows = width // 128
    summands = jnp.full((16 - rows, 128), square_sum(share), f32)
    summands = butterfly(jnp.concatenate([gain_gradient.reshape(rows, 128), summands], axis=0))
    gain = summands[:rows].reshape(-1)
    total_sq = summands[rows, 0] + square_sum(gain)
    count = width * 3 * inner + inner * width + width
    factor = 1.0 / jnp.maximum(jnp.sqrt(total_sq / count), 1.0)

    full_in = jnp.concatenate(full_q + own_rows(share_kv), axis=1)
    rows = SPAN // 2
    gain_own = lax.dynamic_slice(gain, ((chip_at * 2 + core) * rows,), (rows,))
    return (
        branch[None, None],
        branch_grad[None, None],
        factor * full_in,
        factor * full_out,
        factor * gain_own,
    )


def solution(mesh):
    fine = Mesh(mesh.devices.reshape(SIZES), AXES)
    row, col = (("x", "zh"), ("y", "zl", "core"))
    in_specs = (
        P(row, col, None, None),
        P(),
        P(),
        P(),
        P(),
        P(row, col),
        P(row, col, None, None),
    )
    out_specs = (
        P(row, col, None, None),
        P(row, col, None, None),
        P(AXES, None),
        P(AXES, None),
        P(AXES),
    )
    return jax.shard_map(local, mesh=fine, in_specs=in_specs, out_specs=out_specs, check_vma=False)
```

```python
import jax
import jax.numpy as jnp
from jax import lax
from jax.experimental import pallas as pl
from jax.experimental.pallas import tpu as pltpu
from jax.sharding import Mesh
from jax.sharding import PartitionSpec as P

HEAD_DIM = 64
REGION = 3
RADIUS = 3
EPSILON = 1e-05
NEG_BIG = -1e30
GROUPS = 3

AXES = ("x", "zh", "y", "zl", "core")
CHIPS = ("x", "zh", "y", "zl")
SIZES = (4, 2, 4, 2, 2)
ROWS, COLS = 8, 16
N_CHIP = 64
SPAN = 24

NN = (((1,), (0,)), ((), ()))
NT = (((1,), (1,)), ((), ()))
TN = (((0,), (0,)), ((), ()))
f32 = jnp.float32
bf16 = jnp.bfloat16


def dot(a, b, dims=NN):
    return lax.dot_general(a, b, dims, preferred_element_type=f32)


def routes(move):
    index = lambda p: (((p[0] * 2 + p[1]) * 4 + p[2]) * 2 + p[3]) * 2 + p[4]
    places = [(x, zh, y, zl, c) for x in range(4) for zh in range(2)
              for y in range(4) for zl in range(2) for c in range(2)]
    pairs = [(p, move(*p)) for p in places]
    return [(index(p), index(t)) for p, t in pairs if 0 <= t[0] < 4 and 0 <= t[2] < 4]


def third_column(x, zh, y, zl, c):
    if c == zl:
        return (x, zh, y, zl, 1 - c)
    return (x, zh, y + 1 - 2 * zl, zl, 1 - c)


OTHER_ROW = routes(lambda x, zh, y, zl, c: (x, 1 - zh, y, zl, c))
OTHER_COL = routes(lambda x, zh, y, zl, c: (x, zh, y, 1 - zl, c))
OTHER_BOTH = routes(lambda x, zh, y, zl, c: (x, 1 - zh, y, 1 - zl, c))
BEYOND_ROW = routes(lambda x, zh, y, zl, c: (x + 1 - 2 * zh, zh, y, zl, c))
THIRD_COL = routes(third_column)


def after(value, *others):
    return lax.optimization_barrier((value,) + others)[0]


def move(value, route, back=False):
    return lax.ppermute(value, AXES, [(t, f) for f, t in route] if back else route)


def to_sibling(value):
    return lax.ppermute(value, "core", [(0, 1), (1, 0)])


def apply_layer_norm(block):
    values = block.astype(f32)
    centred = values - jnp.mean(values, axis=-1, keepdims=True)
    inverse_deviation = lax.rsqrt(jnp.mean(centred * centred, axis=-1, keepdims=True) + EPSILON)
    return (centred * inverse_deviation, inverse_deviation)


def geometry(tissue, row_at, col_at, slot):
    padded = jnp.pad(tissue, REGION)
    window = lax.dynamic_slice(padded, (row_at * REGION, col_at * REGION), (3 * REGION, 3 * REGION))
    blocks = window.reshape(3, REGION, 3, REGION)
    occupied = jnp.sum(blocks, axis=(1, 3))
    inner = jnp.arange(REGION, dtype=jnp.int32)
    row_in = jnp.sum(blocks * inner[None, :, None, None], axis=(1, 3))
    col_in = jnp.sum(blocks * inner[None, None, None, :], axis=(1, 3))
    three = jnp.arange(3, dtype=jnp.int32)
    key_row = (row_at - 1 + three)[:, None] * REGION + row_in
    key_col = (col_at - 1 + three)[None, :] * REGION + col_in
    query_row = row_at * REGION + slot // REGION
    query_col = col_at * REGION + slot % REGION
    present = lax.dynamic_slice(tissue, (query_row, query_col), (1, 1))[0, 0]
    inside = (
        (jnp.abs(key_row - query_row) <= RADIUS)
        & (jnp.abs(key_col - query_col) <= RADIUS)
        & (occupied > 0)
    )
    centre = (three[:, None] == 1) & (three[None, :] == 1)
    return ((inside | centre).astype(jnp.int32), present)


def attend_kernel(allow_ref, q_ref, g_ref, own_ref, side_ref, third_ref,
                  out_ref, dq_ref, down_ref, dside_ref, dthird_ref, s_scr, dp_scr):
    tile_len = q_ref.shape[0]
    kv_refs = (own_ref, side_ref, third_ref)
    dkv_refs = (down_ref, dside_ref, dthird_ref)
    places = [(a, b) for b in range(3) for a in range(3)]
    first = lax.broadcasted_iota(jnp.int32, (tile_len, 2 * HEAD_DIM), 1) < HEAD_DIM

    def head_pair(v):
        zero = jnp.zeros_like(v)
        return jnp.concatenate([jnp.where(first, v, zero), jnp.where(first, zero, v)], axis=0)

    qq = head_pair(q_ref[...] * jnp.asarray(HEAD_DIM ** -0.5, bf16))
    gg = head_pair(g_ref[...])
    top = jnp.full((1, 2 * tile_len), NEG_BIG, f32)
    for i, (a, b) in enumerate(places):
        scores = dot(kv_refs[b][a, 0], qq, NT)
        scores = jnp.where(allow_ref[b * 3 + a] > 0, scores, NEG_BIG)
        s_scr[i] = scores
        top = jnp.maximum(top, jnp.max(scores, axis=0, keepdims=True))
    total = jnp.zeros((1, 2 * tile_len), f32)
    mix = jnp.zeros((1, 2 * tile_len), f32)
    for i, (a, b) in enumerate(places):
        weights = jnp.exp(s_scr[i] - top)
        dprobs = dot(kv_refs[b][a, 1], gg, NT)
        total = total + jnp.sum(weights, axis=0, keepdims=True)
        mix = mix + jnp.sum(dprobs * weights, axis=0, keepdims=True)
        s_scr[i] = weights
        dp_scr[i] = dprobs
    inverse = 1.0 / total
    mix = mix * inverse
    outs = [jnp.zeros((HEAD_DIM, tile_len), f32)] * 2
    dqs = [jnp.zeros((HEAD_DIM, tile_len), f32)] * 2
    for i, (a, b) in enumerate(places):
        probs = s_scr[i] * inverse
        probs_b = probs.astype(bf16)
        dscores = (probs * (dp_scr[i] - mix)).astype(bf16)
        dkv_refs[b][a, 1] = dot(probs_b, gg).astype(bf16)
        dkv_refs[b][a, 0] = dot(dscores, qq).astype(bf16)
        keys_t = kv_refs[b][a, 0].T
        vals_t = kv_refs[b][a, 1].T
        for h in range(2):
            part = slice(h * HEAD_DIM, (h + 1) * HEAD_DIM)
            lanes = slice(h * tile_len, (h + 1) * tile_len)
            outs[h] = outs[h] + dot(vals_t[part], probs_b[:, lanes])
            dqs[h] = dqs[h] + dot(keys_t[part], dscores[:, lanes])
    out_ref[...] = jnp.concatenate(outs, axis=0).T.astype(bf16)
    dq_ref[...] = (jnp.concatenate(dqs, axis=0).T * HEAD_DIM ** -0.5).astype(bf16)


def attend(allowed, qkv, dattn, own, side, third, group):
    tile_len, width = (own.shape[2], own.shape[3])
    block = 2 * HEAD_DIM
    steps = width // block
    place = lambda h: (0, h + group * steps)
    near = lambda h: (0, 0, 0, h)
    kv_spec = pl.BlockSpec((3, 2, tile_len, block), near)
    row_spec = pl.BlockSpec((tile_len, block), lambda h: (0, h))
    row_shape = jax.ShapeDtypeStruct((tile_len, width), bf16)
    kv_shape = jax.ShapeDtypeStruct(own.shape, bf16)
    scratch = pltpu.VMEM((9, tile_len, 2 * tile_len), f32)
    return pl.pallas_call(
        attend_kernel,
        grid=(steps,),
        in_specs=[
            pl.BlockSpec(memory_space=pltpu.SMEM),
            pl.BlockSpec((tile_len, block), place),
            pl.BlockSpec((tile_len, block), place),
            kv_spec, kv_spec, kv_spec,
        ],
        out_specs=[row_spec, row_spec, kv_spec, kv_spec, kv_spec],
        out_shape=[row_shape, row_shape, kv_shape, kv_shape, kv_shape],
        scratch_shapes=[scratch, scratch],
        compiler_params=pltpu.CompilerParams(vmem_limit_bytes=40 * 1024 * 1024),
        cost_estimate=pl.CostEstimate(
            flops=width * tile_len * tile_len * 9 * 12 * 4,
            bytes_accessed=width * tile_len * 2 * 40,
            transcendentals=width // HEAD_DIM * tile_len * tile_len * 9,
        ),
    )(allowed, qkv, dattn, own, side, third)


def grad_blocks(left_a, left_b, right_a, right_b, first, last):
    lanes = slice(first, last)
    grad = dot(left_a[:, lanes], right_a[...], TN) + dot(left_b[:, lanes], right_b[...], TN)
    return grad.astype(bf16)


def early_kernel(normed_a, normed_b, dq_a, dq_b, attn_a, attn_b, dy_a, dy_b, out_ref):
    step = 16 * SPAN
    blocks = dq_a.shape[1] // 128
    for r in range(normed_a.shape[1] // step):
        grad = grad_blocks(normed_a, normed_b, dq_a, dq_b, r * step, (r + 1) * step)
        for j in range(blocks):
            part = grad[:, j * 128:(j + 1) * 128].reshape(16, SPAN, 128)
            out_ref[r * 16:(r + 1) * 16, j] = part
    for r in range(attn_a.shape[1] // step):
        grad = grad_blocks(attn_a, attn_b, dy_a, dy_b, r * step, (r + 1) * step)
        for i in range(16):
            for q in range(2):
                for j in range(blocks):
                    col = (q * blocks + j) * 128
                    out_ref[2 * (r * 16 + i) + q, blocks + j] = grad[i * SPAN:(i + 1) * SPAN, col:col + 128]


def early_grads(*operands):
    blocks = operands[2].shape[1] // 128
    return pl.pallas_call(
        early_kernel,
        out_shape=jax.ShapeDtypeStruct((N_CHIP, 2 * blocks, SPAN, 128), bf16),
        compiler_params=pltpu.CompilerParams(vmem_limit_bytes=32 * 1024 * 1024),
    )(*operands)


def late_kernel(early_ref, normed_a, normed_b, *refs):
    step = 16 * SPAN
    out_ref = refs[-1]
    done = early_ref.shape[1]
    out_ref[:, :done] = early_ref[...]
    for g in range(len(refs) // 2):
        dkv_a, dkv_b = refs[2 * g:2 * g + 2]
        blocks = dkv_a.shape[1] // 128
        for r in range(normed_a.shape[1] // step):
            grad = grad_blocks(normed_a, normed_b, dkv_a, dkv_b, r * step, (r + 1) * step)
            for j in range(blocks):
                part = grad[:, j * 128:(j + 1) * 128].reshape(16, SPAN, 128)
                out_ref[r * 16:(r + 1) * 16, done + g * blocks + j] = part


def late_grads(*operands):
    blocks = operands[0].shape[1] + sum(d.shape[1] for d in operands[3::2]) // 128
    return pl.pallas_call(
        late_kernel,
        out_shape=jax.ShapeDtypeStruct((N_CHIP, blocks, SPAN, 128), bf16),
        compiler_params=pltpu.CompilerParams(vmem_limit_bytes=32 * 1024 * 1024),
    )(*operands)


def exchanged(value):
    return lax.all_to_all(value.reshape(N_CHIP, -1, 128), CHIPS, 0, 0, tiled=True)


def butterfly(value):
    for bit in range(7):
        value = value + lax.ppermute(value, AXES, [(i, i ^ (1 << bit)) for i in range(ROWS * COLS)])
    return value


def unpacked(share):
    count = share.shape[0] // SPAN
    return share.reshape(count, SPAN, 128).transpose(1, 0, 2).reshape(SPAN, count * 128)


def square_sum(value):
    return jnp.sum(value * value)


def local(tokens, layer_norm_gain, proj_in, proj_out, tissue, tile_slot, cotangent):
    chip_at = lax.axis_index(CHIPS)
    core = lax.axis_index("core")
    zh = lax.axis_index("zh")
    row_at = chip_at // (COLS // 2)
    col_at = (chip_at % (COLS // 2)) * 2 + core
    tile_len, width = tokens.shape[2:]
    inner = proj_out.shape[0]
    half = inner // 2
    is_low = core == 0

    def swapped(lower, upper):
        mine, other = (jnp.where(is_low, lower, upper), jnp.where(is_low, upper, lower))
        return (mine, to_sibling(other))

    xhat, inverse_deviation = apply_layer_norm(tokens[0, 0])
    normed = (xhat * layer_norm_gain).astype(bf16)
    size = inner // GROUPS
    qkv = dot(normed, proj_in).astype(bf16)

    def gather_block(g, *others):
        lo = inner + g * size
        own = jnp.stack([qkv[:, lo:lo + size], qkv[:, inner + lo:inner + lo + size]])
        if others:
            own = after(own, *others)
        return (own, move(own, OTHER_ROW), move(own, OTHER_COL), move(own, OTHER_BOTH))

    stages = []
    for g in range(GROUPS):
        others = []
        if g >= 1:
            others += stages[g - 1]["block"][1:]
        if g >= 2:
            others.append(stages[g - 2]["beyond"])
        own, row, col, both = gather_block(g, *others)
        outer = jnp.stack([row, both])
        beyond = move(outer, BEYOND_ROW)
        stages.append(dict(block=(own, row, col, both), outer=outer, beyond=beyond,
                           own_col=jnp.stack([own, row, beyond[0]]),
                           other_col=jnp.stack([col, both, beyond[1]])))

    allowed, present = geometry(tissue, row_at, col_at, tile_slot[0, 0])
    first_row = zh == 0
    allowed = jnp.stack([
        allowed[1],
        jnp.where(first_row, allowed[2], allowed[0]),
        jnp.where(first_row, allowed[0], allowed[2]),
    ])
    allowed = jnp.concatenate([
        allowed[:, 1],
        jnp.where(is_low, allowed[:, 2], allowed[:, 0]),
        jnp.where(is_low, allowed[:, 0], allowed[:, 2]),
    ])
    cot_block = cotangent[0, 0]
    dy = jnp.where(present > 0, cot_block, jnp.zeros_like(cot_block))
    dattn = dot(dy, proj_out, NT).astype(bf16)
    outs, dqs, backs, early = ([], [], [], [])
    for g in range(GROUPS):
        own_col, other_col = (stages[g]["own_col"], stages[g]["other_col"])
        side_col, third_col = (to_sibling(own_col), move(other_col, THIRD_COL))
        first = []
        if g + 1 < GROUPS:
            first += [stages[g + 1]["own_col"], stages[g + 1]["other_col"]]
        if g >= 2:
            first.append(backs[g - 2][3])
        own_col, side_col, third_col = lax.optimization_barrier((own_col, side_col, third_col, *first))[:3]
        out, dq, down, dside, dthird = attend(allowed, qkv, dattn, own_col, side_col, third_col, g)
        if g == 0:
            normed_side = to_sibling(after(normed, out))
            dy_mine, dy_side = swapped(
                jnp.concatenate([dy[:, :half], dy[:, inner:inner + half]], axis=1),
                after(jnp.concatenate([dy[:, half:inner], dy[:, inner + half:]], axis=1), out),
            )
            early += [normed_side, dy_side]
        side = to_sibling(dside)
        third = move(dthird, THIRD_COL, back=True)
        column = down.astype(f32) + side.astype(f32)
        outer = jnp.stack([column[2].astype(bf16), third[2]])
        if g == GROUPS - 1:
            outer, normed_side, dy_side = lax.optimization_barrier((outer, normed_side, dy_side))
        outs.append(out)
        dqs.append(dq)
        backs.append((column, third, down, outer))
    attn = jnp.concatenate(outs, axis=1)
    dq = jnp.concatenate(dqs, axis=1)
    dkvs = []
    last = backs[-1][3]
    beyonds = [move(back[3], BEYOND_ROW, back=True) for back in backs]
    early_attn, early_dq, _ = lax.optimization_barrier((attn, dq, last))
    early = early_grads(
        normed, normed_side, *swapped(early_dq[:, :half], early_dq[:, half:]),
        early_attn, to_sibling(early_attn), dy_mine, after(dy_side, beyonds[-1]),
    )
    for g, (column, third, _, outer) in enumerate(backs):
        beyond = beyonds[g].astype(f32)
        row = (column[1] + beyond[0]).astype(bf16)
        both = (third[1].astype(f32) + beyond[1]).astype(bf16)
        col = third[0]
        if g == GROUPS - 2:
            row, both, col = lax.optimization_barrier((row, both, col, last))[:3]
        row = move(row, OTHER_ROW)
        both = move(both, OTHER_BOTH)
        col = move(col, OTHER_COL)
        total = column[0] + row.astype(f32) + both.astype(f32) + col.astype(f32)
        dkvs.append(total.astype(bf16))

    branch = dot(attn, proj_out)
    branch = jnp.where(present > 0, branch, jnp.zeros_like(branch)).astype(bf16)
    *dkvs, early = lax.optimization_barrier((*dkvs, early))
    blocks = half // 128
    pairs = [part for total in dkvs for part in swapped(total[0], total[1])]
    late = late_grads(early, normed, normed_side, *pairs)
    dnormed = dot(dq, proj_in[:, :inner], NT)
    for g, total in enumerate(lax.optimization_barrier((*dkvs, late))[:GROUPS]):
        lo = inner + g * size
        dnormed = dnormed + (
            dot(total[0], proj_in[:, lo:lo + size], NT)
            + dot(total[1], proj_in[:, inner + lo:inner + lo + size], NT)
        )
    gain_gradient = jnp.sum(dnormed * xhat, axis=0)
    late = exchanged(late)


    centred = dnormed * layer_norm_gain
    input_gradient = inverse_deviation * (
        centred
        - jnp.mean(centred, axis=-1, keepdims=True)
        - xhat * jnp.mean(centred * xhat, axis=-1, keepdims=True)
    )
    branch_grad = input_gradient.astype(bf16)

    late, branch, branch_grad, gain_gradient = lax.optimization_barrier(
        (late, branch, branch_grad, gain_gradient)
    )
    share = jnp.sum(late.astype(f32), axis=0)
    share_q = unpacked(share[:blocks * SPAN])
    share_out = unpacked(share[blocks * SPAN:2 * blocks * SPAN])
    share_kv = unpacked(share[2 * blocks * SPAN:])

    def own_rows(value):
        rows = value.shape[0] // 2
        mine, other = swapped(value[:rows], value[rows:])
        return [jnp.where(is_low, mine, other), jnp.where(is_low, other, mine)]

    rows = share_out.shape[0] // 4
    low_z = lax.axis_index("zl") == 0
    parts = share_out.reshape(2, 2, rows, half)
    mine, other = swapped(parts[:, 0], parts[:, 1])
    parts = jnp.stack([jnp.where(is_low, mine, other), jnp.where(is_low, other, mine)], axis=1)
    mine, other = (jnp.where(low_z, parts[0], parts[1]), jnp.where(low_z, parts[1], parts[0]))
    other = lax.ppermute(other, "zl", [(0, 1), (1, 0)])
    moved = jnp.stack([jnp.where(low_z, mine, other), jnp.where(low_z, other, mine)])
    full_out = moved.transpose(2, 0, 1, 3).reshape(rows, 4 * half)
    full_q = own_rows(share_q)
    rows = width // 128
    summands = jnp.full((16 - rows, 128), square_sum(share), f32)
    summands = butterfly(jnp.concatenate([gain_gradient.reshape(rows, 128), summands], axis=0))
    gain = summands[:rows].reshape(-1)
    total_sq = summands[rows, 0] + square_sum(gain)
    count = width * 3 * inner + inner * width + width
    factor = 1.0 / jnp.maximum(jnp.sqrt(total_sq / count), 1.0)

    full_in = jnp.concatenate(full_q + own_rows(share_kv), axis=1)
    rows = SPAN // 2
    gain_own = lax.dynamic_slice(gain, ((chip_at * 2 + core) * rows,), (rows,))
    return (
        branch[None, None],
        branch_grad[None, None],
        factor * full_in,
        factor * full_out,
        factor * gain_own,
    )


def solution(mesh):
    fine = Mesh(mesh.devices.reshape(SIZES), AXES)
    row, col = (("x", "zh"), ("y", "zl", "core"))
    in_specs = (
        P(row, col, None, None),
        P(),
        P(),
        P(),
        P(),
        P(row, col),
        P(row, col, None, None),
    )
    out_specs = (
        P(row, col, None, None),
        P(row, col, None, None),
        P(AXES, None),
        P(AXES, None),
        P(AXES),
    )
    return jax.shard_map(local, mesh=fine, in_specs=in_specs, out_specs=out_specs, check_vma=False)
```

```python
import jax
import jax.numpy as jnp
from jax import lax
from jax.experimental import pallas as pl
from jax.experimental.pallas import tpu as pltpu
from jax.sharding import Mesh
from jax.sharding import PartitionSpec as P

HEAD_DIM = 64
REGION = 3
RADIUS = 3
EPSILON = 1e-05
NEG_BIG = -1e30
GROUPS = 3

AXES = ("x", "zh", "y", "zl", "core")
CHIPS = ("x", "zh", "y", "zl")
SIZES = (4, 2, 4, 2, 2)
ROWS, COLS = 8, 16
N_CHIP = 64
SPAN = 24

NN = (((1,), (0,)), ((), ()))
NT = (((1,), (1,)), ((), ()))
TN = (((0,), (0,)), ((), ()))
f32 = jnp.float32
bf16 = jnp.bfloat16


def dot(a, b, dims=NN):
    return lax.dot_general(a, b, dims, preferred_element_type=f32)


def routes(move):
    index = lambda p: (((p[0] * 2 + p[1]) * 4 + p[2]) * 2 + p[3]) * 2 + p[4]
    places = [(x, zh, y, zl, c) for x in range(4) for zh in range(2)
              for y in range(4) for zl in range(2) for c in range(2)]
    pairs = [(p, move(*p)) for p in places]
    return [(index(p), index(t)) for p, t in pairs if 0 <= t[0] < 4 and 0 <= t[2] < 4]


def third_column(x, zh, y, zl, c):
    if c == zl:
        return (x, zh, y, zl, 1 - c)
    return (x, zh, y + 1 - 2 * zl, zl, 1 - c)


OTHER_ROW = routes(lambda x, zh, y, zl, c: (x, 1 - zh, y, zl, c))
OTHER_COL = routes(lambda x, zh, y, zl, c: (x, zh, y, 1 - zl, c))
OTHER_BOTH = routes(lambda x, zh, y, zl, c: (x, 1 - zh, y, 1 - zl, c))
BEYOND_ROW = routes(lambda x, zh, y, zl, c: (x + 1 - 2 * zh, zh, y, zl, c))
THIRD_COL = routes(third_column)


def after(value, *others):
    return lax.optimization_barrier((value,) + others)[0]


def move(value, route, back=False):
    return lax.ppermute(value, AXES, [(t, f) for f, t in route] if back else route)


def to_sibling(value):
    return lax.ppermute(value, "core", [(0, 1), (1, 0)])


def apply_layer_norm(block):
    values = block.astype(f32)
    centred = values - jnp.mean(values, axis=-1, keepdims=True)
    inverse_deviation = lax.rsqrt(jnp.mean(centred * centred, axis=-1, keepdims=True) + EPSILON)
    return (centred * inverse_deviation, inverse_deviation)


def geometry(tissue, row_at, col_at, slot):
    padded = jnp.pad(tissue, REGION)
    window = lax.dynamic_slice(padded, (row_at * REGION, col_at * REGION), (3 * REGION, 3 * REGION))
    blocks = window.reshape(3, REGION, 3, REGION)
    occupied = jnp.sum(blocks, axis=(1, 3))
    inner = jnp.arange(REGION, dtype=jnp.int32)
    row_in = jnp.sum(blocks * inner[None, :, None, None], axis=(1, 3))
    col_in = jnp.sum(blocks * inner[None, None, None, :], axis=(1, 3))
    three = jnp.arange(3, dtype=jnp.int32)
    key_row = (row_at - 1 + three)[:, None] * REGION + row_in
    key_col = (col_at - 1 + three)[None, :] * REGION + col_in
    query_row = row_at * REGION + slot // REGION
    query_col = col_at * REGION + slot % REGION
    present = lax.dynamic_slice(tissue, (query_row, query_col), (1, 1))[0, 0]
    inside = (
        (jnp.abs(key_row - query_row) <= RADIUS)
        & (jnp.abs(key_col - query_col) <= RADIUS)
        & (occupied > 0)
    )
    centre = (three[:, None] == 1) & (three[None, :] == 1)
    return ((inside | centre).astype(jnp.int32), present)


def attend_kernel(allow_ref, q_ref, g_ref, own_ref, side_ref, third_ref,
                  out_ref, dq_ref, down_ref, dside_ref, dthird_ref, s_scr, dp_scr):
    tile_len = q_ref.shape[0]
    kv_refs = (own_ref, side_ref, third_ref)
    dkv_refs = (down_ref, dside_ref, dthird_ref)
    places = [(a, b) for b in range(3) for a in range(3)]
    first = lax.broadcasted_iota(jnp.int32, (tile_len, 2 * HEAD_DIM), 1) < HEAD_DIM

    def head_pair(v):
        zero = jnp.zeros_like(v)
        return jnp.concatenate([jnp.where(first, v, zero), jnp.where(first, zero, v)], axis=0)

    qq = head_pair(q_ref[...] * jnp.asarray(HEAD_DIM ** -0.5, bf16))
    gg = head_pair(g_ref[...])
    top = jnp.full((1, 2 * tile_len), NEG_BIG, f32)
    for i, (a, b) in enumerate(places):
        scores = dot(kv_refs[b][a, 0], qq, NT)
        scores = jnp.where(allow_ref[b * 3 + a] > 0, scores, NEG_BIG)
        s_scr[i] = scores
        top = jnp.maximum(top, jnp.max(scores, axis=0, keepdims=True))
    total = jnp.zeros((1, 2 * tile_len), f32)
    mix = jnp.zeros((1, 2 * tile_len), f32)
    for i, (a, b) in enumerate(places):
        weights = jnp.exp(s_scr[i] - top)
        dprobs = dot(kv_refs[b][a, 1], gg, NT)
        total = total + jnp.sum(weights, axis=0, keepdims=True)
        mix = mix + jnp.sum(dprobs * weights, axis=0, keepdims=True)
        s_scr[i] = weights
        dp_scr[i] = dprobs
    inverse = 1.0 / total
    mix = mix * inverse
    outs = [jnp.zeros((HEAD_DIM, tile_len), f32)] * 2
    dqs = [jnp.zeros((HEAD_DIM, tile_len), f32)] * 2
    for i, (a, b) in enumerate(places):
        probs = s_scr[i] * inverse
        probs_b = probs.astype(bf16)
        dscores = (probs * (dp_scr[i] - mix)).astype(bf16)
        dkv_refs[b][a, 1] = dot(probs_b, gg).astype(bf16)
        dkv_refs[b][a, 0] = dot(dscores, qq).astype(bf16)
        keys_t = kv_refs[b][a, 0].T
        vals_t = kv_refs[b][a, 1].T
        for h in range(2):
            part = slice(h * HEAD_DIM, (h + 1) * HEAD_DIM)
            lanes = slice(h * tile_len, (h + 1) * tile_len)
            outs[h] = outs[h] + dot(vals_t[part], probs_b[:, lanes])
            dqs[h] = dqs[h] + dot(keys_t[part], dscores[:, lanes])
    out_ref[...] = jnp.concatenate(outs, axis=0).T.astype(bf16)
    dq_ref[...] = (jnp.concatenate(dqs, axis=0).T * HEAD_DIM ** -0.5).astype(bf16)


def attend(allowed, qkv, dattn, own, side, third, group):
    tile_len, width = (own.shape[2], own.shape[3])
    block = 2 * HEAD_DIM
    steps = width // block
    place = lambda h: (0, h + group * steps)
    near = lambda h: (0, 0, 0, h)
    kv_spec = pl.BlockSpec((3, 2, tile_len, block), near)
    row_spec = pl.BlockSpec((tile_len, block), lambda h: (0, h))
    row_shape = jax.ShapeDtypeStruct((tile_len, width), bf16)
    kv_shape = jax.ShapeDtypeStruct(own.shape, bf16)
    scratch = pltpu.VMEM((9, tile_len, 2 * tile_len), f32)
    return pl.pallas_call(
        attend_kernel,
        grid=(steps,),
        in_specs=[
            pl.BlockSpec(memory_space=pltpu.SMEM),
            pl.BlockSpec((tile_len, block), place),
            pl.BlockSpec((tile_len, block), place),
            kv_spec, kv_spec, kv_spec,
        ],
        out_specs=[row_spec, row_spec, kv_spec, kv_spec, kv_spec],
        out_shape=[row_shape, row_shape, kv_shape, kv_shape, kv_shape],
        scratch_shapes=[scratch, scratch],
        compiler_params=pltpu.CompilerParams(vmem_limit_bytes=40 * 1024 * 1024),
        cost_estimate=pl.CostEstimate(
            flops=width * tile_len * tile_len * 9 * 12 * 4,
            bytes_accessed=width * tile_len * 2 * 40,
            transcendentals=width // HEAD_DIM * tile_len * tile_len * 9,
        ),
    )(allowed, qkv, dattn, own, side, third)


def grad_blocks(left_a, left_b, right_a, right_b, first, last):
    lanes = slice(first, last)
    grad = dot(left_a[:, lanes], right_a[...], TN) + dot(left_b[:, lanes], right_b[...], TN)
    return grad.astype(bf16)


def early_kernel(normed_a, normed_b, dq_a, dq_b, attn_a, attn_b, dy_a, dy_b, out_ref):
    step = 16 * SPAN
    blocks = dq_a.shape[1] // 128
    for r in range(normed_a.shape[1] // step):
        grad = grad_blocks(normed_a, normed_b, dq_a, dq_b, r * step, (r + 1) * step)
        for j in range(blocks):
            part = grad[:, j * 128:(j + 1) * 128].reshape(16, SPAN, 128)
            out_ref[r * 16:(r + 1) * 16, j] = part
    for r in range(attn_a.shape[1] // step):
        grad = grad_blocks(attn_a, attn_b, dy_a, dy_b, r * step, (r + 1) * step)
        for i in range(16):
            for q in range(2):
                for j in range(blocks):
                    col = (q * blocks + j) * 128
                    out_ref[2 * (r * 16 + i) + q, blocks + j] = grad[i * SPAN:(i + 1) * SPAN, col:col + 128]


def early_grads(*operands):
    blocks = operands[2].shape[1] // 128
    return pl.pallas_call(
        early_kernel,
        out_shape=jax.ShapeDtypeStruct((N_CHIP, 2 * blocks, SPAN, 128), bf16),
        compiler_params=pltpu.CompilerParams(vmem_limit_bytes=32 * 1024 * 1024),
    )(*operands)


def late_kernel(early_ref, normed_a, normed_b, *refs):
    step = 16 * SPAN
    out_ref = refs[-1]
    done = early_ref.shape[1]
    out_ref[:, :done] = early_ref[...]
    for g in range(len(refs) // 2):
        dkv_a, dkv_b = refs[2 * g:2 * g + 2]
        blocks = dkv_a.shape[1] // 128
        for r in range(normed_a.shape[1] // step):
            grad = grad_blocks(normed_a, normed_b, dkv_a, dkv_b, r * step, (r + 1) * step)
            for j in range(blocks):
                part = grad[:, j * 128:(j + 1) * 128].reshape(16, SPAN, 128)
                out_ref[r * 16:(r + 1) * 16, done + g * blocks + j] = part


def late_grads(*operands):
    blocks = operands[0].shape[1] + sum(d.shape[1] for d in operands[3::2]) // 128
    return pl.pallas_call(
        late_kernel,
        out_shape=jax.ShapeDtypeStruct((N_CHIP, blocks, SPAN, 128), bf16),
        compiler_params=pltpu.CompilerParams(vmem_limit_bytes=32 * 1024 * 1024),
    )(*operands)


def exchanged(value):
    return lax.all_to_all(value.reshape(N_CHIP, -1, 128), CHIPS, 0, 0, tiled=True)


def sum_kernel(parts_ref, gain_ref, share_ref, out_ref):
    rows = gain_ref.shape[0]
    step = pl.program_id(0)
    part = jnp.sum(parts_ref[...].astype(f32), axis=0)

    @pl.when(step == 0)
    def _():
        share_ref[...] = part

    @pl.when(step > 0)
    def _():
        share_ref[...] += part

    @pl.when(step == pl.num_programs(0) - 1)
    def _():
        share = share_ref[...]
        squares = jnp.sum(share * share, axis=0, keepdims=True)
        out_ref[:rows] = gain_ref[...]
        out_ref[rows:] = jnp.broadcast_to(squares, (out_ref.shape[0] - rows, 128))


def sum_parts(parts, gain):
    chips, rows, lanes = parts.shape
    return pl.pallas_call(
        sum_kernel,
        grid=(chips // 8,),
        in_specs=[
            pl.BlockSpec((8, rows, lanes), lambda i: (i, 0, 0)),
            pl.BlockSpec(gain.shape, lambda i: (0, 0)),
        ],
        out_specs=[
            pl.BlockSpec((rows, lanes), lambda i: (0, 0)),
            pl.BlockSpec((16, lanes), lambda i: (0, 0)),
        ],
        out_shape=[jax.ShapeDtypeStruct((rows, lanes), f32), jax.ShapeDtypeStruct((16, lanes), f32)],
        compiler_params=pltpu.CompilerParams(vmem_limit_bytes=32 * 1024 * 1024),
        cost_estimate=pl.CostEstimate(flops=1000000, bytes_accessed=1000000, transcendentals=0),
    )(parts, gain)


def butterfly(value):
    for bit in range(7):
        value = value + lax.ppermute(value, AXES, [(i, i ^ (1 << bit)) for i in range(ROWS * COLS)])
    return value


def unpacked(share):
    count = share.shape[0] // SPAN
    return share.reshape(count, SPAN, 128).transpose(1, 0, 2).reshape(SPAN, count * 128)


def square_sum(value):
    return jnp.sum(value * value)


def local(tokens, layer_norm_gain, proj_in, proj_out, tissue, tile_slot, cotangent):
    chip_at = lax.axis_index(CHIPS)
    core = lax.axis_index("core")
    zh = lax.axis_index("zh")
    row_at = chip_at // (COLS // 2)
    col_at = (chip_at % (COLS // 2)) * 2 + core
    tile_len, width = tokens.shape[2:]
    inner = proj_out.shape[0]
    half = inner // 2
    is_low = core == 0

    def swapped(lower, upper):
        mine, other = (jnp.where(is_low, lower, upper), jnp.where(is_low, upper, lower))
        return (mine, to_sibling(other))

    xhat, inverse_deviation = apply_layer_norm(tokens[0, 0])
    normed = (xhat * layer_norm_gain).astype(bf16)
    size = inner // GROUPS
    qkv = dot(normed, proj_in).astype(bf16)

    def gather_block(g, *others):
        lo = inner + g * size
        own = jnp.stack([qkv[:, lo:lo + size], qkv[:, inner + lo:inner + lo + size]])
        if others:
            own = after(own, *others)
        return (own, move(own, OTHER_ROW), move(own, OTHER_COL), move(own, OTHER_BOTH))

    stages = []
    for g in range(GROUPS):
        others = []
        if g >= 1:
            others += stages[g - 1]["block"][1:]
        if g >= 2:
            others.append(stages[g - 2]["beyond"])
        own, row, col, both = gather_block(g, *others)
        outer = jnp.stack([row, both])
        beyond = move(outer, BEYOND_ROW)
        stages.append(dict(block=(own, row, col, both), outer=outer, beyond=beyond,
                           own_col=jnp.stack([own, row, beyond[0]]),
                           other_col=jnp.stack([col, both, beyond[1]])))

    allowed, present = geometry(tissue, row_at, col_at, tile_slot[0, 0])
    first_row = zh == 0
    allowed = jnp.stack([
        allowed[1],
        jnp.where(first_row, allowed[2], allowed[0]),
        jnp.where(first_row, allowed[0], allowed[2]),
    ])
    allowed = jnp.concatenate([
        allowed[:, 1],
        jnp.where(is_low, allowed[:, 2], allowed[:, 0]),
        jnp.where(is_low, allowed[:, 0], allowed[:, 2]),
    ])
    cot_block = cotangent[0, 0]
    dy = jnp.where(present > 0, cot_block, jnp.zeros_like(cot_block))
    dattn = dot(dy, proj_out, NT).astype(bf16)
    outs, dqs, backs, early = ([], [], [], [])
    for g in range(GROUPS):
        own_col, other_col = (stages[g]["own_col"], stages[g]["other_col"])
        side_col, third_col = (to_sibling(own_col), move(other_col, THIRD_COL))
        first = []
        if g + 1 < GROUPS:
            first += [stages[g + 1]["own_col"], stages[g + 1]["other_col"]]
        if g >= 2:
            first.append(backs[g - 2][3])
        own_col, side_col, third_col = lax.optimization_barrier((own_col, side_col, third_col, *first))[:3]
        out, dq, down, dside, dthird = attend(allowed, qkv, dattn, own_col, side_col, third_col, g)
        if g == 0:
            normed_side = to_sibling(after(normed, out))
            dy_mine, dy_side = swapped(
                jnp.concatenate([dy[:, :half], dy[:, inner:inner + half]], axis=1),
                after(jnp.concatenate([dy[:, half:inner], dy[:, inner + half:]], axis=1), out),
            )
            early += [normed_side, dy_side]
        side = to_sibling(dside)
        third = move(dthird, THIRD_COL, back=True)
        column = down.astype(f32) + side.astype(f32)
        outer = jnp.stack([column[2].astype(bf16), third[2]])
        if g == GROUPS - 1:
            outer, normed_side, dy_side = lax.optimization_barrier((outer, normed_side, dy_side))
        outs.append(out)
        dqs.append(dq)
        backs.append((column, third, down, outer))
    dkvs = []
    last = backs[-1][3]
    for g, (column, third, _, outer) in enumerate(backs):
        beyond = move(outer, BEYOND_ROW, back=True).astype(f32)
        row = (column[1] + beyond[0]).astype(bf16)
        both = (third[1].astype(f32) + beyond[1]).astype(bf16)
        col = third[0]
        if g == GROUPS - 2:
            row, both, col = lax.optimization_barrier((row, both, col, last))[:3]
        row = move(row, OTHER_ROW)
        both = move(both, OTHER_BOTH)
        col = move(col, OTHER_COL)
        total = column[0] + row.astype(f32) + both.astype(f32) + col.astype(f32)
        dkvs.append(total.astype(bf16))

    attn = jnp.concatenate(outs, axis=1)
    dq = jnp.concatenate(dqs, axis=1)
    branch = dot(attn, proj_out)
    branch = jnp.where(present > 0, branch, jnp.zeros_like(branch)).astype(bf16)
    early = early_grads(
        normed, normed_side, *swapped(dq[:, :half], dq[:, half:]), attn, to_sibling(attn), dy_mine, dy_side
    )
    *dkvs, early = lax.optimization_barrier((*dkvs, early))
    blocks = half // 128
    pairs = [part for total in dkvs for part in swapped(total[0], total[1])]
    late = late_grads(early, normed, normed_side, *pairs)
    dnormed = dot(dq, proj_in[:, :inner], NT)
    for g, total in enumerate(lax.optimization_barrier((*dkvs, late))[:GROUPS]):
        lo = inner + g * size
        dnormed = dnormed + (
            dot(total[0], proj_in[:, lo:lo + size], NT)
            + dot(total[1], proj_in[:, inner + lo:inner + lo + size], NT)
        )
    gain_gradient = jnp.sum(dnormed * xhat, axis=0)
    late = exchanged(late)


    centred = dnormed * layer_norm_gain
    input_gradient = inverse_deviation * (
        centred
        - jnp.mean(centred, axis=-1, keepdims=True)
        - xhat * jnp.mean(centred * xhat, axis=-1, keepdims=True)
    )
    branch_grad = input_gradient.astype(bf16)

    late, branch, branch_grad, gain_gradient = lax.optimization_barrier(
        (late, branch, branch_grad, gain_gradient)
    )
    share, summands = sum_parts(late, gain_gradient.reshape(-1, 128))
    share_q = unpacked(share[:blocks * SPAN])
    share_out = unpacked(share[blocks * SPAN:2 * blocks * SPAN])
    share_kv = unpacked(share[2 * blocks * SPAN:])

    def own_rows(value):
        rows = value.shape[0] // 2
        mine, other = swapped(value[:rows], value[rows:])
        return [jnp.where(is_low, mine, other), jnp.where(is_low, other, mine)]

    rows = share_out.shape[0] // 4
    low_z = lax.axis_index("zl") == 0
    parts = share_out.reshape(2, 2, rows, half)
    mine, other = swapped(parts[:, 0], parts[:, 1])
    parts = jnp.stack([jnp.where(is_low, mine, other), jnp.where(is_low, other, mine)], axis=1)
    mine, other = (jnp.where(low_z, parts[0], parts[1]), jnp.where(low_z, parts[1], parts[0]))
    other = lax.ppermute(other, "zl", [(0, 1), (1, 0)])
    moved = jnp.stack([jnp.where(low_z, mine, other), jnp.where(low_z, other, mine)])
    full_out = moved.transpose(2, 0, 1, 3).reshape(rows, 4 * half)
    full_q = own_rows(share_q)
    rows = width // 128
    summands = butterfly(summands)
    gain = summands[:rows].reshape(-1)
    total_sq = jnp.sum(summands[rows]) + square_sum(gain)
    count = width * 3 * inner + inner * width + width
    factor = 1.0 / jnp.maximum(jnp.sqrt(total_sq / count), 1.0)

    full_in = jnp.concatenate(full_q + own_rows(share_kv), axis=1)
    rows = SPAN // 2
    gain_own = lax.dynamic_slice(gain, ((chip_at * 2 + core) * rows,), (rows,))
    return (
        branch[None, None],
        branch_grad[None, None],
        factor * full_in,
        factor * full_out,
        factor * gain_own,
    )


def solution(mesh):
    fine = Mesh(mesh.devices.reshape(SIZES), AXES)
    row, col = (("x", "zh"), ("y", "zl", "core"))
    in_specs = (
        P(row, col, None, None),
        P(),
        P(),
        P(),
        P(),
        P(row, col),
        P(row, col, None, None),
    )
    out_specs = (
        P(row, col, None, None),
        P(row, col, None, None),
        P(AXES, None),
        P(AXES, None),
        P(AXES),
    )
    return jax.shard_map(local, mesh=fine, in_specs=in_specs, out_specs=out_specs, check_vma=False)
```
